256 devices in a mesh: dp: 128 (over z, y, x_lo, core), mp: 2 (over x_hi).
Axes of the slice: x: 4 (x_hi: 2, x_lo: 2; x = x_hi * 2 + x_lo), y: 4, z: 8, core: 2. Of those that a mesh axis runs over, the one named last changes fastest.
Arguments:
- head_hidden: bfloat16 [16384, 2048], P('dp'), may hold values from -30 to 30
- proj_weight: bfloat16 [2048, 512], P(None, 'mp'), may hold values from -0.125 to 0.125
- pair_perm: int32 [8192], replicated, may hold values from 0 to 8191, as said below
Outputs:
- mean_contrast_cost: float32 [], replicated
- grad_emb: float32 [16384, 512], P('dp', 'mp')
- grad_proj: float32 [2048, 512], P(None, 'mp')
The draws below stay inside these ranges and needn't reach their ends.
Inputs may be any that keep to these rules, and one draw needn't show every extreme that they name: `pair_perm`: every number of 0 to 8191 appears once.
All inputs are finite; a program needn't handle non-finite values.
Results may differ from the reference program's by a relative error of at most 0.0079.
Values may be sent and summed in bfloat16 or wider, within the bound.
A program may use at most 64 MiB of HBM per device.

```python
import math
import jax
import jax.numpy as jnp
from jax import lax

E = 512
DH = 2048
ROWS = 16384
HALF = 8192


def pair_table(key):
    return jax.random.permutation(jax.random.fold_in(key, 11), HALF).astype(jnp.int32)


def draw_pair_perm(key, part):
    return pair_table(key)


def draw_head_hidden(key, part):
    table = pair_table(key)
    key = jax.random.fold_in(key, 5)
    class_key, centre_key, noise_key, jitter_key = jax.random.split(key, 4)
    classes = max(HALF // 64, 4)
    class_ids = jax.random.randint(class_key, (HALF,), 0, classes)
    centres = jnp.clip(jax.random.normal(centre_key, (classes, DH), jnp.float32), -4.0, 4.0)
    noise = jnp.clip(jax.random.normal(noise_key, (ROWS, DH), jnp.float32), -4.0, 4.0)
    lowest = 0.3
    highest = 3.0
    first_views = 2.0 * centres[class_ids] + noise[:HALF]
    ratio = jnp.arange(HALF, dtype=jnp.float32) / max(HALF - 1, 1)
    spread = lowest * (highest / lowest) ** ratio
    spread = spread * jax.random.uniform(jitter_key, (HALF,), jnp.float32, 0.7, 1.3)
    paired_rows = first_views + spread[:, None] * noise[HALF:]
    second_views = jnp.zeros((HALF, DH), jnp.float32).at[table].set(paired_rows)
    return jnp.concatenate([first_views, second_views], axis=0).astype(jnp.bfloat16)


def level_of(own_key, dims, pieces, least, high):
    factor_of, own = 1.0, jax.random.fold_in(own_key, 6)
    for position, parts in pieces:
        steps = jnp.exp(jax.random.uniform(jax.random.fold_in(own, position), (parts,), jnp.float32, least / len(pieces), high / len(pieces)))
        factor_of = factor_of * jnp.repeat(steps, dims[position] // parts).reshape([-1 if axis == position else 1 for axis in range(len(dims))])
    return factor_of


def gaussian(stream_key, extent, deviation, limit, pieces=(), kind=jnp.bfloat16):
    array = jax.random.normal(stream_key, extent, jnp.float32) * deviation
    if len(pieces) > 0:
        array = level_of(stream_key, extent, pieces, -0.22, 0.18) * array
    return jnp.clip(array, min=-limit, max=limit).astype(kind)


def setup_inputs(seed: int = 0) -> dict:
    arg_keys = jax.random.split(jax.random.key(seed), 4)
    return {
        "head_hidden": draw_head_hidden(jax.random.fold_in(arg_keys[3], 71), 0),
        "proj_weight": gaussian(arg_keys[1], (DH, E), DH ** -0.5, 0.125, ((1, 2),)),
        "pair_perm": draw_pair_perm(jax.random.fold_in(arg_keys[3], 71), 0),
    }


inverse_sharpness_factor = 10.0

def reference(head_hidden, proj_weight, pair_perm):
    embed = jnp.dot(head_hidden, proj_weight, preferred_element_type=jnp.float32).astype(jnp.bfloat16)
    embed_float = embed.astype(jnp.float32)
    inverse_norm = lax.rsqrt(lax.optimization_barrier(jnp.sum(embed_float * embed_float, axis=1)) + 1e-06)
    unitlength_vectors = (embed_float * inverse_norm[:, None]).astype(jnp.bfloat16)
    backward_pair = jnp.zeros((HALF,), jnp.int32).at[pair_perm].set(jnp.arange(HALF, dtype=jnp.int32))
    partner = jnp.concatenate([(HALF + pair_perm).astype(jnp.int32), backward_pair]).astype(jnp.int32)
    block_rows = math.gcd(ROWS, 512)
    count_blocks = ROWS // block_rows
    target_positions = jnp.arange(ROWS, dtype=jnp.int32)
    row_blocks = target_positions.reshape(count_blocks, block_rows)
    unit_blocks = unitlength_vectors.reshape(count_blocks, block_rows, E)
    pair_blocks = partner.reshape(count_blocks, block_rows)

    def first_pass(element):
        block, source_positions, pairs = element
        angle_agreement = jnp.dot(block, unitlength_vectors.T, preferred_element_type=jnp.float32)
        exponentiated_terms = jnp.where(target_positions[None, :] == source_positions[:, None], 0.0, jnp.exp(inverse_sharpness_factor * (angle_agreement - 1.0)))
        matched_pair_logit = jnp.take_along_axis(angle_agreement, pairs[:, None], axis=1)[:, 0]
        return (lax.optimization_barrier(jnp.sum(exponentiated_terms, axis=1)), matched_pair_logit)
    totals, matched_pair_logit = lax.map(first_pass, (unit_blocks, row_blocks, pair_blocks))
    log_partition_entries = jnp.log(totals.reshape(ROWS))
    matched_pair_logit = matched_pair_logit.reshape(ROWS)
    mean_contrast_cost = jnp.mean(log_partition_entries - inverse_sharpness_factor * (matched_pair_logit - 1.0))
    log_blocks = log_partition_entries.reshape(count_blocks, block_rows)

    def second_pass(element):
        block, source_positions, pairs, logs = element
        angle_agreement = jnp.dot(block, unitlength_vectors.T, preferred_element_type=jnp.float32)
        stabilized_logits = inverse_sharpness_factor * (angle_agreement - 1.0)
        projection_matrix_piece = jnp.exp(stabilized_logits - logs[:, None]) + jnp.exp(stabilized_logits - log_partition_entries[None, :])
        projection_matrix_piece = jnp.where(target_positions[None, :] == source_positions[:, None], 0.0, projection_matrix_piece)
        projection_matrix_piece = projection_matrix_piece - jnp.where(target_positions[None, :] == pairs[:, None], 2.0, 0.0)
        return inverse_sharpness_factor * jnp.dot(projection_matrix_piece.astype(jnp.bfloat16), unitlength_vectors, preferred_element_type=jnp.float32)
    unitvec_derivative = lax.map(second_pass, (unit_blocks, row_blocks, pair_blocks, log_blocks)).reshape(ROWS, E)
    inner_dots = lax.optimization_barrier(jnp.sum(embed_float * unitvec_derivative, axis=1))
    grad_emb = inverse_norm[:, None] * unitvec_derivative - embed_float * (inverse_norm ** 3 * inner_dots)[:, None]
    grad_proj = jnp.dot(head_hidden.T, grad_emb.astype(jnp.bfloat16), preferred_element_type=jnp.float32)
    return (mean_contrast_cost, grad_emb, grad_proj)
```

```python
import jax
import jax.numpy as jnp
from jax import lax
from jax.experimental import pallas as pl
from jax.experimental.pallas import tpu as pltpu
from jax.sharding import PartitionSpec as P

MESH = pl.DeviceIdType.MESH
F32 = jnp.float32
BF16 = jnp.bfloat16
SHARPNESS = 10.0
R = 128
NZ, NY, NX, NC = 8, 4, 2, 2
ROWS = R * NZ * NY * NX * NC

PLANE = [(ky, kx, kh) for ky in range(NY) for kx in range(2) for kh in range(2)]
COLUMN = [(kz, kc) for kz in range(NZ) for kc in range(2)]
GROUP = [(kx, kc) for kx in range(2) for kc in range(2)]


def nt(a, b):
    return lax.dot_general(a, b, (((1,), (1,)), ((), ())), preferred_element_type=F32)


def to_rows(x):
    return jnp.sum(x.T, axis=0, keepdims=True)


def to_columns(row):
    return jnp.broadcast_to(row, (R, R)).T


def kernel(
    h_ref, w_ref, perm_ref,
    loss_ref, gemb_ref, gproj_ref,
    ui, uj, raw, sim, mark, rowmsg, colmsg, losses, tsum,
    gs, gr, gpart, g4, hq, gp, gpb, ry, rz, rzb,
    s_mp, r_mp, s_i, r_i, s_j, r_j, s_f, r_f, s_row, r_row, s_col, r_col,
    s_loss, r_loss, s_rs, r_rs, s_h, r_h, s_g, r_g, s_y, r_y, s_z, r_z,
    s_az, r_az, s_ay, r_ay, s_ax, r_ax, s_ac, r_ac,
):
    dp = lax.axis_index("dp")
    xh = lax.axis_index("mp")
    c = lax.rem(dp, 2)
    xl = lax.rem(dp // 2, 2)
    y = lax.rem(dp // 4, 4)
    z = dp // 16
    p_me = y * 2 + xl
    q_me = xl * 2 + c

    def dev(z_, y_, xl_, c_, xh_):
        return (((z_ * 4 + y_) * 2 + xl_) * 2 + c_, xh_)

    def step(v, k, n):
        return v if k == 0 else lax.rem(v + k, n)

    def plane_dev(k):
        return dev(z, step(y, k[0], 4), step(xl, k[1], 2), c, step(xh, k[2], 2))

    def column_dev(k):
        return dev(step(z, k[0], 8), y, xl, step(c, k[1], 2), xh)

    def group_dev(k):
        return dev(z, y, step(xl, k[0], 2), step(c, k[1], 2), xh)

    me = (dp, xh)

    def send(src, dst, ssem, rsem, to):
        copy = pltpu.make_async_remote_copy(
            src_ref=src, dst_ref=dst, send_sem=ssem, recv_sem=rsem, device_id=to, device_id_type=MESH
        )
        copy.start()
        return copy

    def arrived(dst, ssem, rsem, frm):
        pltpu.make_async_remote_copy(
            src_ref=dst, dst_ref=dst, send_sem=ssem, recv_sem=rsem, device_id=frm, device_id_type=MESH
        ).wait_recv()

    sent = []

    barrier = pltpu.get_barrier_semaphore()
    peers = [plane_dev(k) for k in PLANE[1:]] + [column_dev(k) for k in COLUMN[1:]] + [group_dev((1, 1))]
    for peer in peers:
        pl.semaphore_signal(barrier, inc=1, device_id=peer, device_id_type=MESH)

    embed = jnp.dot(h_ref[...], w_ref[...], preferred_element_type=F32).astype(BF16)
    raw[0] = embed
    pl.semaphore_wait(barrier, len(peers))
    partner_dev = plane_dev((0, 0, 1))
    sent.append(send(raw.at[0], raw.at[1], s_mp, r_mp, partner_dev))

    first = z < 4
    lanes = lax.broadcasted_iota(jnp.int32, (1, R), 1)
    b_row = []
    for zz in range(8):
        jglob = (((zz * 4 + y) * 2 + xl) * 2 + xh) * R + lanes
        if zz < 4:
            other = perm_ref[pl.ds(zz * 16 + y * 4 + xl * 2 + xh, 1), :] + ROWS // 2
        else:
            other = jnp.full((1, R), -1, jnp.int32)
        b_row.append(jnp.where(first, jglob, other).astype(F32))
    b_row = jnp.concatenate(b_row, axis=1)
    for p in range(8):
        mine = (z * 16 + p * 2 + c) * R + lanes
        pair = perm_ref[pl.ds(lax.rem(z, 4) * 16 + p * 2 + c, 1), :] + ROWS // 2
        a_row = jnp.where(first, pair, mine).astype(F32)
        a_col = to_columns(a_row)
        mark[p * R:(p + 1) * R, :] = jnp.where(
            jnp.concatenate([a_col] * 8, axis=1) == b_row, -2.0, 0.0
        )

    arrived(raw.at[1], s_mp, r_mp, partner_dev)
    e0 = raw[0].astype(F32)
    e1 = raw[1].astype(F32)
    inv = lax.rsqrt(jnp.sum(e0 * e0 + e1 * e1, axis=1, keepdims=True) + 1e-06)
    own_i = pl.ds(pl.multiple_of(p_me * R, R), R)
    own_j = pl.ds(pl.multiple_of(z * R, R), R)
    ui[0, own_i, :] = (e0 * inv).astype(BF16)
    ui[1, own_i, :] = (e1 * inv).astype(BF16)

    mine = ui.at[:, own_i, :]
    i_peers = [(ky, kx, 0) for ky in range(4) for kx in range(2)][1:]
    for n, k in enumerate(i_peers):
        sent.append(send(mine, mine, s_i.at[n], r_i.at[n], plane_dev(k)))

    @pl.when(c == xh)
    def _():
        uj[0, own_j, :] = ui[0, own_i, :]
        uj[1, own_j, :] = ui[1, own_i, :]
        here = uj.at[:, own_j, :]
        out = []
        for kz in range(1, 8):
            out.append(send(here, here, s_j.at[kz], r_j.at[kz], column_dev((kz, 0))))
        out.append(send(here, here, s_f.at[0], r_f.at[0], column_dev((0, 1))))
        for kz in range(1, 8):
            frm = lax.rem(z + (8 - kz), 8)
            part = uj.at[:, pl.ds(pl.multiple_of(frm * R, R), R), :]
            arrived(part, s_j.at[kz], r_j.at[kz], column_dev((8 - kz, 0)))
            out.append(send(part, part, s_f.at[kz], r_f.at[kz], column_dev((0, 1))))
        for copy in out:
            copy.wait_send()

    @pl.when(c != xh)
    def _():
        for kz in range(8):
            frm = lax.rem(z + (8 - kz), 8)
            part = uj.at[:, pl.ds(pl.multiple_of(frm * R, R), R), :]
            arrived(part, s_f.at[kz], r_f.at[kz], column_dev((0, 1)))

    for n, (ky, kx, _) in enumerate(i_peers):
        frm = lax.rem(y + (4 - ky), 4) * 2 + lax.rem(xl + (2 - kx), 2)
        part = ui.at[:, pl.ds(pl.multiple_of(frm * R, R), R), :]
        arrived(part, s_i.at[n], r_i.at[n], plane_dev(((4 - ky) % 4, (2 - kx) % 2, 0)))

    for n, k in enumerate(GROUP):
        q = step(xl, k[0], 2) * 2 + step(c, k[1], 2)
        cols = pl.ds(pl.multiple_of(q * 512, 512), 512)
        if n == 0:
            hq[0:R, :] = h_ref[:, cols]
        else:
            sent.append(
                send(h_ref.at[:, cols], hq.at[n * R:(n + 1) * R, :], s_h.at[n], r_h.at[n], group_dev(k))
            )

    for b in range(4):
        rows = slice(b * 256, (b + 1) * 256)
        sim[rows, :] = nt(ui[0, rows, :], uj[0]) + nt(ui[1, rows, :], uj[1])
    eye = lax.broadcasted_iota(jnp.int32, (R, R), 0) == lax.broadcasted_iota(jnp.int32, (R, R), 1)
    block = sim[own_i, own_j]
    sim[own_i, own_j] = jnp.where(jnp.logical_and(eye, c == xh), -1e9, block)

    own_row = p_me * 2 + xh
    own_col = z * 2 + c
    tsum[...] = jnp.zeros_like(tsum)
    rowmsg[own_row] = jnp.zeros((16, R), F32)

    @pl.loop(0, 8)
    def _(p):
        rows = pl.ds(pl.multiple_of(p * R, R), R)
        s = sim[rows, :]
        hit = s * mark[rows, :]
        e = jnp.exp(SHARPNESS * (s - 1.0))
        sim[rows, :] = e
        part = e[:, 0:R]
        hits = hit[:, 0:R]
        for t in range(1, 8):
            part = part + e[:, t * R:(t + 1) * R]
            hits = hits + hit[:, t * R:(t + 1) * R]
        rowmsg[own_row, pl.ds(p, 1), :] = to_rows(part)
        rowmsg[own_row, 8:9, :] = rowmsg[own_row, 8:9, :] - 0.5 * jnp.sum(hits, axis=0, keepdims=True)
        tsum[...] = tsum[...] + jnp.sum(e, axis=0, keepdims=True)

    total = tsum[...]
    for zz in range(8):
        colmsg[own_col, zz:zz + 1, :] = total[:, zz * R:(zz + 1) * R]

    for n, k in enumerate(PLANE):
        if n:
            there = rowmsg.at[own_row]
            sent.append(send(there, there, s_row.at[n], r_row.at[n], plane_dev(k)))
    for n, k in enumerate(COLUMN):
        if n:
            there = colmsg.at[own_col]
            sent.append(send(there, there, s_col.at[n], r_col.at[n], column_dev(k)))
    for n, k in enumerate(PLANE):
        if n:
            back = ((4 - k[0]) % 4, k[1], k[2])
            frm = (step(y, back[0], 4) * 2 + step(xl, back[1], 2)) * 2 + step(xh, back[2], 2)
            arrived(rowmsg.at[frm], s_row.at[n], r_row.at[n], plane_dev(back))
    for n, k in enumerate(COLUMN):
        if n:
            back = ((8 - k[0]) % 8, k[1])
            frm = step(z, back[0], 8) * 2 + step(c, back[1], 2)
            arrived(colmsg.at[frm], s_col.at[n], r_col.at[n], column_dev(back))

    all_rows = rowmsg[0]
    all_cols = colmsg[0]
    for n in range(1, 16):
        all_rows = all_rows + rowmsg[n]
        all_cols = all_cols + colmsg[n]
    row_total = all_rows[0:8]
    hit_total = all_rows[8:9]

    cost = jnp.sum(jnp.log(row_total), axis=0, keepdims=True) - SHARPNESS * (hit_total - 8.0)
    losses[own_col] = jnp.broadcast_to(cost, (8, R))
    for n, k in enumerate(COLUMN):
        if n:
            there = losses.at[own_col]
            sent.append(send(there, there, s_loss.at[n], r_loss.at[n], column_dev(k)))

    inv_rows = 1.0 / row_total
    inv_cols = 1.0 / all_cols
    tsum[...] = jnp.concatenate([inv_cols[t:t + 1] for t in range(8)], axis=1)
    losses_t = gpart
    for p in range(8):
        losses_t[p] = to_columns(inv_rows[p:p + 1])
    for ky in range(4):
        y_to = step(y, ky, 4)
        rows = pl.ds(pl.multiple_of(y_to * 256, 256), 256)
        col = losses_t[pl.ds(y_to * 2, 2)].reshape(256, R)
        wide = jnp.concatenate([col] * 8, axis=1)
        weights = (sim[rows, :] * (wide + tsum[...]) + mark[rows, :]).astype(BF16)
        acc = None
        for f in range(2):
            g = jnp.dot(weights, uj[f], preferred_element_type=F32)
            gs[ky, 0, f, 0:R, :] = g[0:R].astype(BF16)
            gs[ky, 1, f, 0:R, :] = g[R:].astype(BF16)
            t = g * ui[f, rows, :].astype(F32)
            t = t[:, 0:R] + t[:, R:]
            acc = t if acc is None else acc + t
        for half in range(2):
            v = to_rows(acc[half * R:(half + 1) * R])
            hi = v.astype(BF16)
            lo = (v - hi.astype(F32)).astype(BF16)
            line = jnp.broadcast_to(jnp.concatenate([hi, lo], axis=1).astype(F32), (16, 256)).astype(BF16)
            gs[ky, half, 0, R:, :] = line
            gs[ky, half, 1, R:, :] = line
        for kx in range(2):
            for kh in range(2):
                n = (ky * 2 + kx) * 2 + kh
                if n:
                    sent.append(
                        send(
                            gs.at[ky, step(xl, kx, 2), kh], gr.at[n], s_rs.at[n], r_rs.at[n],
                            plane_dev((ky, kx, kh)),
                        )
                    )
    g = gs[0, xl, 0].astype(F32)
    for n, k in enumerate(PLANE):
        if n:
            arrived(gr.at[n], s_rs.at[n], r_rs.at[n], plane_dev(((4 - k[0]) % 4, k[1], k[2])))
            g = g + gr[n].astype(F32)
    inner = to_columns(g[R:R + 1, 0:R] + g[R:R + 1, R:])
    unit = raw[0].astype(F32) * inv
    grad = (SHARPNESS * inv) * (g[0:R] - unit * jnp.concatenate([inner, inner], axis=1))
    gemb_ref[...] = grad
    g4[0:R, :] = grad.astype(BF16)

    for n, k in enumerate(GROUP):
        if n:
            sent.append(
                send(g4.at[0:R, :], g4.at[n * R:(n + 1) * R, :], s_g.at[n], r_g.at[n], group_dev(k))
            )
    for n, k in enumerate(GROUP):
        if n:
            arrived(hq.at[n * R:(n + 1) * R, :], s_h.at[n], r_h.at[n], group_dev(k))
            arrived(g4.at[n * R:(n + 1) * R, :], s_g.at[n], r_g.at[n], group_dev(k))
    full = lax.dot_general(hq[...], g4[...], (((0,), (0,)), ((), ())), preferred_element_type=F32)
    gp[...] = full
    gpb[...] = full.astype(BF16)
    for ky in range(1, 4):
        y_to = step(y, ky, 4)
        part = gpb.at[pl.ds(pl.multiple_of(y_to * R, R), R), :]
        sent.append(send(part, ry.at[ky], s_y.at[ky], r_y.at[ky], plane_dev((ky, 0, 0))))
    part = gp[pl.ds(pl.multiple_of(y * R, R), R), :]
    for ky in range(1, 4):
        arrived(ry.at[ky], s_y.at[ky], r_y.at[ky], plane_dev((4 - ky, 0, 0)))
        part = part + ry[ky].astype(F32)
    gp[0:R, :] = part
    rzb[...] = part.astype(BF16)
    for kz in range(1, 8):
        z_to = step(z, kz, 8)
        piece = rzb.at[pl.ds(pl.multiple_of(z_to * 16, 16), 16), :]
        sent.append(send(piece, rz.at[kz], s_z.at[kz], r_z.at[kz], column_dev((kz, 0))))
    piece = gp[pl.ds(pl.multiple_of(z * 16, 16), 16), :]
    for kz in range(1, 8):
        arrived(rz.at[kz], s_z.at[kz], r_z.at[kz], column_dev((8 - kz, 0)))
        piece = piece + rz[kz].astype(F32)

    def span(q_, y_, z_):
        return pl.ds(pl.multiple_of(q_ * 512 + y_ * R + z_ * 16, 16), 16)

    gproj_ref[span(q_me, y, z), :] = piece.astype(BF16)
    there = gproj_ref.at[span(q_me, y, z), :]
    for kz in range(1, 8):
        sent.append(send(there, there, s_az.at[kz], r_az.at[kz], column_dev((kz, 0))))
    for kz in range(1, 8):
        frm = gproj_ref.at[span(q_me, y, step(z, 8 - kz, 8)), :]
        arrived(frm, s_az.at[kz], r_az.at[kz], column_dev((8 - kz, 0)))
    there = gproj_ref.at[pl.ds(pl.multiple_of(q_me * 512 + y * R, R), R), :]
    for ky in range(1, 4):
        sent.append(send(there, there, s_ay.at[ky], r_ay.at[ky], plane_dev((ky, 0, 0))))
    for ky in range(1, 4):
        y_from = step(y, 4 - ky, 4)
        frm = gproj_ref.at[pl.ds(pl.multiple_of(q_me * 512 + y_from * R, R), R), :]
        arrived(frm, s_ay.at[ky], r_ay.at[ky], plane_dev((4 - ky, 0, 0)))

    def quarter(q):
        return gproj_ref.at[pl.ds(pl.multiple_of(q * 512, 512), 512), :]

    there = quarter(q_me)
    sent.append(send(there, there, s_ax, r_ax, group_dev((1, 0))))
    sent.append(send(there, there, s_ac.at[0], r_ac.at[0], group_dev((0, 1))))
    there = quarter((1 - xl) * 2 + c)
    arrived(there, s_ax, r_ax, group_dev((1, 0)))
    sent.append(send(there, there, s_ac.at[1], r_ac.at[1], group_dev((0, 1))))

    for n, k in enumerate(COLUMN):
        if n:
            back = ((8 - k[0]) % 8, k[1])
            frm = step(z, back[0], 8) * 2 + step(c, back[1], 2)
            arrived(losses.at[frm], s_loss.at[n], r_loss.at[n], column_dev(back))
    cost = losses[0]
    for n in range(1, 16):
        cost = cost + losses[n]
    loss_ref[...] = jnp.broadcast_to(jnp.sum(cost, axis=1, keepdims=True) * (1.0 / ROWS), (8, R))

    arrived(quarter(xl * 2 + (1 - c)), s_ac.at[0], r_ac.at[0], group_dev((0, 1)))
    arrived(quarter((1 - xl) * 2 + (1 - c)), s_ac.at[1], r_ac.at[1], group_dev((0, 1)))
    for copy in sent:
        copy.wait_send()


def per_device(head_hidden, proj_weight, pair_perm):
    dma = pltpu.SemaphoreType.DMA
    vmem = pltpu.VMEM
    space = pl.BlockSpec(memory_space=pltpu.VMEM)
    pairs = []
    for shape in [(), (7,), (8,), (8,), (16,), (16,), (16,), (16,), (4,), (4,), (4,), (8,), (8,), (4,), (), (2,)]:
        pairs += [dma(shape), dma(shape)]
    loss, grad_emb, grad_proj = pl.pallas_call(
        kernel,
        out_shape=(
            jax.ShapeDtypeStruct((8, R), F32),
            jax.ShapeDtypeStruct((R, 256), F32),
            jax.ShapeDtypeStruct((2048, 256), BF16),
        ),
        in_specs=[space] * 3,
        out_specs=[space] * 3,
        scratch_shapes=[
            vmem((2, 1024, 256), BF16),
            vmem((2, 1024, 256), BF16),
            vmem((2, R, 256), BF16),
            vmem((1024, 1024), F32),
            vmem((1024, 1024), F32),
            vmem((16, 16, R), F32),
            vmem((16, 8, R), F32),
            vmem((16, 8, R), F32),
            vmem((1, 1024), F32),
            vmem((4, 2, 2, R + 16, 256), BF16),
            vmem((16, R + 16, 256), BF16),
            vmem((8, R, R), F32),
            vmem((512, 256), BF16),
            vmem((512, 512), BF16),
            vmem((512, 256), F32),
            vmem((512, 256), BF16),
            vmem((4, R, 256), BF16),
            vmem((8, 16, 256), BF16),
            vmem((R, 256), BF16),
        ] + pairs,
        compiler_params=pltpu.CompilerParams(
            collective_id=0, has_side_effects=True, vmem_limit_bytes=48 * 1024 * 1024
        ),
    )(head_hidden, proj_weight, pair_perm.reshape(64, R))
    return loss[0, 0], grad_emb, grad_proj.astype(F32)


def solution(mesh):
    placed = (P("dp", None), P(None, "mp"), P())
    return jax.shard_map(
        per_device,
        mesh=mesh,
        in_specs=placed,
        out_specs=(P(), P("dp", "mp"), P(None, "mp")),
        check_vma=False,
    )
```

```python
import jax
import jax.numpy as jnp
from jax import lax
from jax.experimental import pallas as pl
from jax.experimental.pallas import tpu as pltpu
from jax.sharding import PartitionSpec as P

MESH = pl.DeviceIdType.MESH
F32 = jnp.float32
BF16 = jnp.bfloat16
SHARPNESS = 10.0
R = 128
H = 64
ROWS = 16384
COPIES = 192


def far(k, n):
    return min(k, n - k)


PLANE = sorted([(ky, kx) for ky in range(4) for kx in range(4)][1:], key=lambda k: -far(k[0], 4) - far(k[1], 4))
COLUMN = sorted([(kz, kc) for kz in range(8) for kc in range(2)][1:], key=lambda k: -far(k[0], 8))
GROUP = [(kx, kc) for kx in range(2) for kc in range(2)]


def nt(a, b):
    return lax.dot_general(a, b, (((1,), (1,)), ((), ())), preferred_element_type=F32)


def to_rows(x):
    return jnp.sum(x.T, axis=0, keepdims=True)


def to_columns(row):
    return jnp.broadcast_to(row, (R, R)).T


def inverse_norm(e0, e1):
    return lax.rsqrt(jnp.sum(e0 * e0 + e1 * e1, axis=1, keepdims=True) + 1e-06)


def kernel(
    h_hbm, w_hbm, perm_hbm,
    loss_ref, gemb_ref, gproj_ref,
    h_ref, w_ref, perm_ref, ei, ej, ui, uj, sim, mark, rowmsg, colmsg, losses, tsum, factor,
    sa, sb, ra, rb, sa2, sb2, ra2, rb2, ia, ib, iar, ibr, ia2, ib2, iar2, ibr2, isum,
    g4, hq, gp, gpb, ry, rz, rzb, s_in, s_out, s_back,
):
    dp = lax.axis_index("dp")
    xh = lax.axis_index("mp")
    c = lax.rem(dp, 2)
    xl = lax.rem(dp // 2, 2)
    y = lax.rem(dp // 4, 4)
    z = dp // 16
    x = xh * 2 + xl
    p_me = y * 2 + xl
    q_me = xl * 2 + c
    fetches = c == xh

    def dev(dz=0, dy=0, dx=0, dc=0):
        x_ = step(x, dx, 4)
        return (((step(z, dz, 8) * 4 + step(y, dy, 4)) * 2 + lax.rem(x_, 2)) * 2 + step(c, dc, 2), x_ // 2)

    def step(v, k, n):
        k = k % n
        return v if k == 0 else lax.rem(v + k, n)

    def group_dev(kx, kc):
        return (((z * 4 + y) * 2 + step(xl, kx, 2)) * 2 + step(c, kc, 2), xh)

    slots = {}

    def copy(key, src, dst, to):
        n = slots.setdefault(key, len(slots))
        return pltpu.make_async_remote_copy(
            src_ref=src, dst_ref=dst, send_sem=s_out.at[n], recv_sem=s_back.at[n],
            device_id=to, device_id_type=MESH,
        )

    sent = []

    def send(key, src, dst, to):
        one = copy(key, src, dst, to)
        one.start()
        sent.append(one)

    def arrived(key, dst):
        copy(key, dst, dst, dev(dc=1)).wait_recv()

    loads = [
        pltpu.make_async_copy(h_hbm, h_ref, s_in.at[0]),
        pltpu.make_async_copy(w_hbm, w_ref, s_in.at[1]),
        pltpu.make_async_copy(perm_hbm, perm_ref, s_in.at[2]),
    ]
    for load in loads:
        load.start()

    barrier = pltpu.get_barrier_semaphore()
    peers = [dev(dz=kz, dc=kc) for kz, kc in COLUMN] + [dev(dy=ky, dx=kx) for ky, kx in PLANE] + [group_dev(1, 1)]
    for peer in peers:
        pl.semaphore_signal(barrier, inc=1, device_id=peer, device_id_type=MESH)
    for load in loads:
        load.wait()

    embed = jnp.dot(h_ref[...], w_ref[...], preferred_element_type=F32).astype(BF16)
    ei[y, x] = embed

    @pl.when(fetches)
    def _():
        ej[xh, z] = ei[y, x]

    pl.semaphore_wait(barrier, len(peers))

    own = ei.at[y, x]
    for k in (2, 1, 3):
        send(("x", k), own, own, dev(dx=k))
    for k in (1, 3, 2):
        send(("y", k), own, own, dev(dy=k))

    def along_z(half, f):
        piece = ej.at[f, z]
        for k in (2, 6, 1, 7):
            copy(("z", half, k), piece, piece, dev(dz=k)).start()
        copy(("c", half, 0), piece, piece, dev(dc=1)).start()

    @pl.when(fetches)
    def _():
        along_z(0, xh)

    first = z < 4
    lanes = lax.broadcasted_iota(jnp.int32, (1, R), 1)
    b_row = []
    for zz in range(8):
        jglob = (((zz * 4 + y) * 2 + xl) * 2 + xh) * R + lanes
        if zz < 4:
            other = perm_ref[pl.ds(zz * 16 + y * 4 + xl * 2 + xh, 1), :] + ROWS // 2
        else:
            other = jnp.full((1, R), -1, jnp.int32)
        b_row.append(jnp.where(first, jglob, other).astype(F32))
    b_row = jnp.concatenate(b_row, axis=1)
    for p in range(8):
        mine = (z * 16 + p * 2 + c) * R + lanes
        pair = perm_ref[pl.ds(lax.rem(z, 4) * 16 + p * 2 + c, 1), :] + ROWS // 2
        a_col = to_columns(jnp.where(first, pair, mine).astype(F32))
        mark[p * R:(p + 1) * R, :] = jnp.where(jnp.concatenate([a_col] * 8, axis=1) == b_row, -2.0, 0.0)

    def on_from_x(k):
        piece = ei.at[y, step(x, -k, 4)]
        arrived(("x", k), piece)
        part = ei.at[y, step(x, -k, 4), 0:H]
        for ky in (2, 1, 3):
            send(("xy", k, ky), part, part, dev(dy=ky))

    def on_from_y(k):
        piece = ei.at[step(y, -k, 4), x]
        arrived(("y", k), piece)
        part = ei.at[step(y, -k, 4), x, H:R]
        for kx in (2, 1, 3):
            send(("yx", k, kx), part, part, dev(dx=kx))

    on_from_x(1)
    on_from_x(3)
    on_from_y(1)
    on_from_y(3)
    on_from_x(2)

    @pl.when(fetches)
    def _():
        ej[1 - xh, z] = ei[y, step(x, 2, 4)]
        along_z(1, 1 - xh)

    on_from_y(2)

    def hand(half, f, k):
        piece = ej.at[f, step(z, -k, 8)]
        copy(("c", half, k), piece, piece, dev(dc=1)).start()

    def from_z(half, f, k):
        piece = ej.at[f, step(z, -k, 8)]
        if k == 4:
            for s in range(2):
                arrived(("z", half, 4, s), ej.at[f, step(z, 4, 8), s * H:(s + 1) * H])
        else:
            arrived(("z", half, k), piece)
        if k == 2:
            copy(("z", half, 3), piece, piece, dev(dz=1)).start()
            part = ej.at[f, step(z, -2, 8), 0:H]
            copy(("z", half, 4, 0), part, part, dev(dz=2)).start()
        if k == 6:
            copy(("z", half, 5), piece, piece, dev(dz=-1)).start()
            part = ej.at[f, step(z, 2, 8), H:R]
            copy(("z", half, 4, 1), part, part, dev(dz=-2)).start()
        hand(half, f, k)

    @pl.when(fetches)
    def _():
        for k in (2, 6, 1, 7):
            from_z(0, xh, k)
        for k in (2, 6, 1, 7):
            from_z(1, 1 - xh, k)

    for k in (1, 3, 2):
        for j in (1, 3, 2):
            arrived(("xy", k, j), ei.at[step(y, -j, 4), step(x, -k, 4), 0:H])
            arrived(("yx", k, j), ei.at[step(y, -k, 4), step(x, -j, 4), H:R])

    def unit(dst, rows, e0, e1):
        e0 = e0.astype(F32)
        e1 = e1.astype(F32)
        inv = inverse_norm(e0, e1)
        dst[0, rows, :] = (e0 * inv).astype(BF16)
        dst[1, rows, :] = (e1 * inv).astype(BF16)

    for p in range(8):
        unit(ui, slice(p * R, (p + 1) * R), ei[p // 2, p % 2], ei[p // 2, 2 + p % 2])

    @pl.when(fetches)
    def _():
        for half, f in ((0, xh), (1, 1 - xh)):
            for k in (3, 5, 4):
                from_z(half, f, k)

    @pl.when(jnp.logical_not(fetches))
    def _():
        for half, f in ((0, xh), (1, 1 - xh)):
            for k in range(8):
                arrived(("c", half, k), ej.at[f, step(z, -k, 8)])

    for zz in range(8):
        unit(uj, slice(zz * R, (zz + 1) * R), ej[0, zz], ej[1, zz])

    for n, (kx, kc) in enumerate(GROUP):
        q = step(xl, kx, 2) * 2 + step(c, kc, 2)
        quarter_columns = pl.ds(pl.multiple_of(q * 512, 512), 512)
        if n == 0:
            hq[0:R, :] = h_ref[:, quarter_columns]
        else:
            send(("h", n), h_ref.at[:, quarter_columns], hq.at[n * R:(n + 1) * R, :], group_dev(kx, kc))

    for b in range(4):
        rows = slice(b * 256, (b + 1) * 256)
        sim[rows, :] = nt(ui[0, rows, :], uj[0]) + nt(ui[1, rows, :], uj[1])
    own_i = pl.ds(pl.multiple_of(p_me * R, R), R)
    own_j = pl.ds(pl.multiple_of(z * R, R), R)
    eye = lax.broadcasted_iota(jnp.int32, (R, R), 0) == lax.broadcasted_iota(jnp.int32, (R, R), 1)
    block = sim[own_i, own_j]
    sim[own_i, own_j] = jnp.where(jnp.logical_and(eye, fetches), -1e9, block)

    own_row = y * 4 + x
    own_col = z * 2 + c
    tsum[...] = jnp.zeros_like(tsum)
    rowmsg[own_row] = jnp.zeros((16, R), F32)

    @pl.loop(0, 8)
    def _(p):
        rows = pl.ds(pl.multiple_of(p * R, R), R)
        s = sim[rows, :]
        hit = s * mark[rows, :]
        e = jnp.exp(SHARPNESS * (s - 1.0))
        sim[rows, :] = e
        part = e[:, 0:R]
        hits = hit[:, 0:R]
        for t in range(1, 8):
            part = part + e[:, t * R:(t + 1) * R]
            hits = hits + hit[:, t * R:(t + 1) * R]
        rowmsg[own_row, pl.ds(p, 1), :] = to_rows(part)
        rowmsg[own_row, 8:9, :] = rowmsg[own_row, 8:9, :] - 0.5 * jnp.sum(hits, axis=0, keepdims=True)
        tsum[...] = tsum[...] + jnp.sum(e, axis=0, keepdims=True)

    total = tsum[...]
    for zz in range(8):
        colmsg[own_col, zz:zz + 1, :] = total[:, zz * R:(zz + 1) * R]

    for kz, kc in COLUMN:
        send(("col", kz, kc), colmsg.at[own_col], colmsg.at[own_col], dev(dz=kz, dc=kc))
    for ky, kx in PLANE:
        send(("row", ky, kx), rowmsg.at[own_row], rowmsg.at[own_row], dev(dy=ky, dx=kx))
    for ky, kx in PLANE:
        arrived(("row", ky, kx), rowmsg.at[step(y, -ky, 4) * 4 + step(x, -kx, 4)])
    for kz, kc in COLUMN:
        arrived(("col", kz, kc), colmsg.at[step(z, -kz, 8) * 2 + step(c, kc, 2)])

    all_rows = rowmsg[0]
    all_cols = colmsg[0]
    for n in range(1, 16):
        all_rows = all_rows + rowmsg[n]
        all_cols = all_cols + colmsg[n]
    row_total = all_rows[0:8]
    hit_total = all_rows[8:9]
    cost = jnp.sum(jnp.log(row_total), axis=0, keepdims=True) - SHARPNESS * (hit_total - 8.0)
    losses[own_col] = jnp.broadcast_to(cost, (8, R))

    inv_rows = 1.0 / row_total
    inv_cols = 1.0 / all_cols
    tsum[...] = jnp.concatenate([inv_cols[t:t + 1] for t in range(8)], axis=1)
    for p in range(8):
        factor[p] = to_columns(inv_rows[p:p + 1])
    for ky in (2, 1, 3, 0):
        y_to = step(y, ky, 4)
        rows = pl.ds(pl.multiple_of(y_to * 256, 256), 256)
        wide = jnp.concatenate([factor[pl.ds(y_to * 2, 2)].reshape(256, R)] * 8, axis=1)
        weights = (sim[rows, :] * (wide + tsum[...]) + mark[rows, :]).astype(BF16)
        acc = None
        for f in range(2):
            g = jnp.dot(weights, uj[f], preferred_element_type=F32)
            for half in range(2):
                sa[2 * f + half, y_to] = g[half * R:half * R + H].astype(BF16)
                sb[y_to, 2 * f + half] = g[half * R + H:(half + 1) * R].astype(BF16)
            t = g * ui[f, rows, :].astype(F32)
            t = t[:, 0:R] + t[:, R:]
            acc = t if acc is None else acc + t
        for kx in (2, 1, 3):
            send(("ra", kx, ky), sa.at[step(x, kx, 4), y_to], ra.at[kx, y_to], dev(dx=kx))
        if ky:
            send(("rb", ky), sb.at[y_to], rb.at[ky], dev(dy=ky))
        for half in range(2):
            v = to_rows(acc[half * R:(half + 1) * R])
            ia[half, pl.ds(y_to, 1), :] = v
            ib[y_to, half:half + 1, :] = v
        if ky:
            send(("ib", ky), ib.at[y_to], ibr.at[ky], dev(dy=ky))
    for kx in (2, 1, 3):
        send(("ia", kx), ia.at[step(xl, kx, 2)], iar.at[kx], dev(dx=kx))
    for kz, kc in COLUMN:
        send(("loss", kz, kc), losses.at[own_col], losses.at[own_col], dev(dz=kz, dc=kc))

    for ky in (2, 1, 3):
        arrived(("rb", ky), rb.at[ky])
        arrived(("ib", ky), ibr.at[ky])
    line = ib[y] + ibr[1] + ibr[2] + ibr[3]
    isum[1] = line
    for half in range(2):
        ib2[half] = jnp.broadcast_to(line[half:half + 1], (8, R))
    for kx in (2, 1, 3):
        x_to = step(x, kx, 4)
        g = sb[y, x_to].astype(F32) + rb[1, x_to].astype(F32) + rb[2, x_to].astype(F32) + rb[3, x_to].astype(F32)
        sb2[kx] = g.astype(BF16)
        send(("rb2", kx), sb2.at[kx], rb2.at[kx], dev(dx=kx))
        send(("ib2", kx), ib2.at[step(xl, kx, 2)], ibr2.at[kx], dev(dx=kx))
    g_b = sb[y, x].astype(F32) + rb[1, x].astype(F32) + rb[2, x].astype(F32) + rb[3, x].astype(F32)
    for kx in (2, 1, 3):
        arrived(("ia", kx), iar.at[kx])
        for ky in range(4):
            arrived(("ra", kx, ky), ra.at[kx, step(y, ky, 4)])
    line = ia[xl] + iar[1] + iar[2] + iar[3]
    isum[0] = line
    for yy in range(4):
        ia2[yy] = jnp.broadcast_to(line[yy:yy + 1], (8, R))
    for ky in (2, 1, 3):
        y_to = step(y, ky, 4)
        g = sa[x, y_to].astype(F32) + ra[1, y_to].astype(F32) + ra[2, y_to].astype(F32) + ra[3, y_to].astype(F32)
        sa2[ky] = g.astype(BF16)
        send(("ra2", ky), sa2.at[ky], ra2.at[ky], dev(dy=ky))
        send(("ia2", ky), ia2.at[y_to], iar2.at[ky], dev(dy=ky))
    g_a = sa[x, y].astype(F32) + ra[1, y].astype(F32) + ra[2, y].astype(F32) + ra[3, y].astype(F32)
    inner_a = isum[0, pl.ds(y, 1), :]
    inner_b = isum[1, pl.ds(xl, 1), :]
    for k in (1, 3, 2):
        arrived(("rb2", k), rb2.at[k])
        arrived(("ib2", k), ibr2.at[k])
        arrived(("ra2", k), ra2.at[k])
        arrived(("ia2", k), iar2.at[k])
        g_a = g_a + ra2[k].astype(F32)
        g_b = g_b + rb2[k].astype(F32)
        inner_a = inner_a + iar2[k, 0:1]
        inner_b = inner_b + ibr2[k, 0:1]
    inner = to_columns(jnp.where(lanes < H, inner_a, inner_b))
    inv = inverse_norm(ei[y, xl].astype(F32), ei[y, 2 + xl].astype(F32))
    own_unit = ei[y, x].astype(F32) * inv
    g = jnp.concatenate([g_a, g_b], axis=0)
    grad = (SHARPNESS * inv) * (g - own_unit * jnp.concatenate([inner, inner], axis=1))
    gemb_ref[...] = grad
    g4[0:R, :] = grad.astype(BF16)

    for n, (kx, kc) in enumerate(GROUP):
        if n:
            send(("g", n), g4.at[0:R, :], g4.at[n * R:(n + 1) * R, :], group_dev(kx, kc))
    for n in range(1, 4):
        arrived(("h", n), hq.at[n * R:(n + 1) * R, :])
        arrived(("g", n), g4.at[n * R:(n + 1) * R, :])
    full = lax.dot_general(hq[...], g4[...], (((0,), (0,)), ((), ())), preferred_element_type=F32)
    gp[...] = full
    gpb[...] = full.astype(BF16)
    for ky in (2, 1, 3):
        part = gpb.at[pl.ds(pl.multiple_of(step(y, ky, 4) * R, R), R), :]
        send(("gy", ky), part, ry.at[ky], dev(dy=ky))
    part = gp[pl.ds(pl.multiple_of(y * R, R), R), :]
    for ky in (1, 3, 2):
        arrived(("gy", ky), ry.at[ky])
        part = part + ry[ky].astype(F32)
    gp[0:R, :] = part
    rzb[...] = part.astype(BF16)
    for kz in (4, 3, 5, 2, 6, 1, 7):
        piece = rzb.at[pl.ds(pl.multiple_of(step(z, kz, 8) * 16, 16), 16), :]
        send(("gz", kz), piece, rz.at[kz], dev(dz=kz))
    piece = gp[pl.ds(pl.multiple_of(z * 16, 16), 16), :]
    for kz in (1, 7, 2, 6, 3, 5, 4):
        arrived(("gz", kz), rz.at[kz])
        piece = piece + rz[kz].astype(F32)

    def rows_of(q_, y_, z_=None):
        if z_ is None:
            return gproj_ref.at[pl.ds(pl.multiple_of(q_ * 512 + y_ * R, R), R), :]
        return gproj_ref.at[pl.ds(pl.multiple_of(q_ * 512 + y_ * R + z_ * 16, 16), 16), :]

    gproj_ref[pl.ds(pl.multiple_of(q_me * 512 + y * R + z * 16, 16), 16), :] = piece.astype(BF16)
    mine = rows_of(q_me, y, z)
    for kz in (4, 3, 5, 2, 6, 1, 7):
        send(("az", kz), mine, mine, dev(dz=kz))
    for kz in (1, 7, 2, 6, 3, 5, 4):
        arrived(("az", kz), rows_of(q_me, y, step(z, -kz, 8)))

    def to_group(ky):
        there = rows_of(q_me, step(y, -ky, 4))
        send(("ax", ky), there, there, group_dev(1, 0))
        send(("ac", 0, ky), there, there, group_dev(0, 1))

    mine = rows_of(q_me, y)
    for ky in (2, 1, 3):
        send(("ay", ky), mine, mine, dev(dy=ky))
    to_group(0)
    for ky in (1, 3, 2):
        arrived(("ay", ky), rows_of(q_me, step(y, -ky, 4)))
        to_group(ky)
    for ky in (0, 1, 3, 2):
        there = rows_of((1 - xl) * 2 + c, step(y, -ky, 4))
        arrived(("ax", ky), there)
        send(("ac", 1, ky), there, there, group_dev(0, 1))

    for kz, kc in COLUMN:
        arrived(("loss", kz, kc), losses.at[step(z, -kz, 8) * 2 + step(c, kc, 2)])
    cost = losses[0]
    for n in range(1, 16):
        cost = cost + losses[n]
    loss_ref[...] = jnp.broadcast_to(jnp.sum(cost, axis=1, keepdims=True) * (1.0 / ROWS), (8, R))

    for ky in (0, 1, 3, 2):
        arrived(("ac", 0, ky), rows_of(xl * 2 + (1 - c), step(y, -ky, 4)))
        arrived(("ac", 1, ky), rows_of((1 - xl) * 2 + (1 - c), step(y, -ky, 4)))
    for one in sent:
        one.wait_send()

    @pl.when(fetches)
    def _():
        whole = ej.at[0, 0]
        half_piece = ej.at[0, 0, 0:H]
        for half in range(2):
            for k in (2, 6, 1, 7, 3, 5):
                copy(("z", half, k), whole, whole, dev(dc=1)).wait_send()
            for s in range(2):
                copy(("z", half, 4, s), half_piece, half_piece, dev(dc=1)).wait_send()
            for k in range(8):
                copy(("c", half, k), whole, whole, dev(dc=1)).wait_send()


def per_device(head_hidden, proj_weight, pair_perm):
    vmem = pltpu.VMEM
    hbm = pl.BlockSpec(memory_space=pltpu.HBM)
    space = pl.BlockSpec(memory_space=pltpu.VMEM)
    loss, grad_emb, grad_proj = pl.pallas_call(
        kernel,
        out_shape=(
            jax.ShapeDtypeStruct((8, R), F32),
            jax.ShapeDtypeStruct((R, 256), F32),
            jax.ShapeDtypeStruct((2048, 256), BF16),
        ),
        in_specs=[hbm] * 3,
        out_specs=[space] * 3,
        scratch_shapes=[
            vmem((R, 2048), BF16),
            vmem((2048, 256), BF16),
            vmem((64, R), jnp.int32),
            vmem((4, 4, R, 256), BF16),
            vmem((2, 8, R, 256), BF16),
            vmem((2, 1024, 256), BF16),
            vmem((2, 1024, 256), BF16),
            vmem((1024, 1024), F32),
            vmem((1024, 1024), F32),
            vmem((16, 16, R), F32),
            vmem((16, 8, R), F32),
            vmem((16, 8, R), F32),
            vmem((1, 1024), F32),
            vmem((8, R, R), F32),
            vmem((4, 4, H, 256), BF16),
            vmem((4, 4, H, 256), BF16),
            vmem((4, 4, H, 256), BF16),
            vmem((4, 4, H, 256), BF16),
            vmem((4, H, 256), BF16),
            vmem((4, H, 256), BF16),
            vmem((4, H, 256), BF16),
            vmem((4, H, 256), BF16),
            vmem((2, 8, R), F32),
            vmem((4, 8, R), F32),
            vmem((4, 8, R), F32),
            vmem((4, 8, R), F32),
            vmem((4, 8, R), F32),
            vmem((2, 8, R), F32),
            vmem((4, 8, R), F32),
            vmem((4, 8, R), F32),
            vmem((2, 8, R), F32),
            vmem((512, 256), BF16),
            vmem((512, 512), BF16),
            vmem((512, 256), F32),
            vmem((512, 256), BF16),
            vmem((4, R, 256), BF16),
            vmem((8, 16, 256), BF16),
            vmem((R, 256), BF16),
            pltpu.SemaphoreType.DMA((3,)),
            pltpu.SemaphoreType.DMA((COPIES,)),
            pltpu.SemaphoreType.DMA((COPIES,)),
        ],
        compiler_params=pltpu.CompilerParams(
            collective_id=0, has_side_effects=True, vmem_limit_bytes=56 * 1024 * 1024
        ),
    )(head_hidden, proj_weight, pair_perm.reshape(64, R))
    return loss[0, 0], grad_emb, grad_proj.astype(F32)


def solution(mesh):
    placed = (P("dp", None), P(None, "mp"), P())
    return jax.shard_map(
        per_device,
        mesh=mesh,
        in_specs=placed,
        out_specs=(P(), P("dp", "mp"), P(None, "mp")),
        check_vma=False,
    )
```

```python
import jax
import jax.numpy as jnp
from jax import lax
from jax.experimental import pallas as pl
from jax.experimental.pallas import tpu as pltpu
from jax.sharding import PartitionSpec as P

MESH = pl.DeviceIdType.MESH
F32 = jnp.float32
BF16 = jnp.bfloat16
SHARPNESS = 10.0
EXP2_SCALE = SHARPNESS * 1.4426950408889634
ORDER = (0, 1, 7, 2, 6, 3, 5, 4)
R = 128
H = 64
ROWS = 16384
COPIES = 224


def far(k, n):
    return min(k, n - k)


PLANE = sorted([(ky, kx) for ky in range(4) for kx in range(4)][1:], key=lambda k: -far(k[0], 4) - far(k[1], 4))
COLUMN = sorted([(kz, kc) for kz in range(8) for kc in range(2)][1:], key=lambda k: -far(k[0], 8))
GROUP = [(kx, kc) for kx in range(2) for kc in range(2)]


def nt(a, b):
    return lax.dot_general(a, b, (((1,), (1,)), ((), ())), preferred_element_type=F32)


def to_rows(x):
    return jnp.sum(x.T, axis=0, keepdims=True)


def to_columns(row):
    return jnp.broadcast_to(row, (R, R)).T


def inverse_norm(e0, e1):
    return lax.rsqrt(jnp.sum(e0 * e0 + e1 * e1, axis=1, keepdims=True) + 1e-06)


def kernel(
    h_hbm, w_hbm, perm_hbm,
    loss_ref, gemb_ref, gproj_ref,
    h_ref, w_ref, perm_ref, ei, ej, ui, uj, sim, mark, rowmsg, colmsg, losses, tsum, isum_cols, rowacc, factor,
    sa, sb, ra, rb, sa2, sb2, ra2, rb2, ia, ib, iar, ibr, ia2, ib2, iar2, ibr2, isum,
    g4, hq, gp, gpb, ry, rz, rzb, s_in, s_out, s_back,
):
    dp = lax.axis_index("dp")
    xh = lax.axis_index("mp")
    c = lax.rem(dp, 2)
    xl = lax.rem(dp // 2, 2)
    y = lax.rem(dp // 4, 4)
    z = dp // 16
    x = xh * 2 + xl
    p_me = y * 2 + xl
    q_me = xl * 2 + c
    fetches = c == xh

    def dev(dz=0, dy=0, dx=0, dc=0):
        x_ = step(x, dx, 4)
        return (((step(z, dz, 8) * 4 + step(y, dy, 4)) * 2 + lax.rem(x_, 2)) * 2 + step(c, dc, 2), x_ // 2)

    def step(v, k, n):
        k = k % n
        return v if k == 0 else lax.rem(v + k, n)

    def group_dev(kx, kc):
        return (((z * 4 + y) * 2 + step(xl, kx, 2)) * 2 + step(c, kc, 2), xh)

    slots = {}

    def copy(key, src, dst, to):
        n = slots.setdefault(key, len(slots))
        return pltpu.make_async_remote_copy(
            src_ref=src, dst_ref=dst, send_sem=s_out.at[n], recv_sem=s_back.at[n],
            device_id=to, device_id_type=MESH,
        )

    sent = []

    def send(key, src, dst, to):
        one = copy(key, src, dst, to)
        one.start()
        sent.append(one)

    def arrived(key, dst):
        copy(key, dst, dst, dev(dc=1)).wait_recv()

    loads = [
        pltpu.make_async_copy(h_hbm, h_ref, s_in.at[0]),
        pltpu.make_async_copy(w_hbm, w_ref, s_in.at[1]),
        pltpu.make_async_copy(perm_hbm, perm_ref, s_in.at[2]),
    ]
    for load in loads:
        load.start()

    barrier = pltpu.get_barrier_semaphore()
    peers = [dev(dz=kz, dc=kc) for kz, kc in COLUMN] + [dev(dy=ky, dx=kx) for ky, kx in PLANE] + [group_dev(1, 1)]
    for peer in peers:
        pl.semaphore_signal(barrier, inc=1, device_id=peer, device_id_type=MESH)
    for load in loads:
        load.wait()

    embed = jnp.dot(h_ref[...], w_ref[...], preferred_element_type=F32).astype(BF16)
    ei[y, x] = embed

    @pl.when(fetches)
    def _():
        ej[xh, z] = ei[y, x]

    pl.semaphore_wait(barrier, len(peers))

    own = ei.at[y, x]
    for k in (2, 1, 3):
        send(("x", k), own, own, dev(dx=k))
    for k in (1, 3, 2):
        send(("y", k), own, own, dev(dy=k))

    def along_z(half, f):
        piece = ej.at[f, z]
        for k in (2, 6, 1, 7):
            copy(("z", half, k), piece, piece, dev(dz=k)).start()
        copy(("c", half, 0), piece, piece, dev(dc=1)).start()

    @pl.when(fetches)
    def _():
        along_z(0, xh)

    first = z < 4
    lanes = lax.broadcasted_iota(jnp.int32, (1, R), 1)
    b_row = []
    for k in ORDER:
        zz = step(z, -k, 8)
        jglob = (((zz * 4 + y) * 2 + xl) * 2 + xh) * R + lanes
        pair = perm_ref[pl.ds(lax.rem(zz, 4) * 16 + y * 4 + xl * 2 + xh, 1), :] + ROWS // 2
        b_row.append(jnp.where(first, jglob, jnp.where(zz < 4, pair, -1)).astype(F32))
    b_row = jnp.concatenate(b_row, axis=1)
    for p in range(8):
        mine = (z * 16 + p * 2 + c) * R + lanes
        pair = perm_ref[pl.ds(lax.rem(z, 4) * 16 + p * 2 + c, 1), :] + ROWS // 2
        a_col = to_columns(jnp.where(first, pair, mine).astype(F32))
        mark[p * R:(p + 1) * R, :] = jnp.where(jnp.concatenate([a_col] * 8, axis=1) == b_row, -2.0, 0.0)

    def on_from_x(k):
        piece = ei.at[y, step(x, -k, 4)]
        arrived(("x", k), piece)
        part = ei.at[y, step(x, -k, 4), 0:H]
        for ky in (2, 1, 3):
            send(("xy", k, ky), part, part, dev(dy=ky))

    def on_from_y(k):
        piece = ei.at[step(y, -k, 4), x]
        arrived(("y", k), piece)
        part = ei.at[step(y, -k, 4), x, H:R]
        for kx in (2, 1, 3):
            send(("yx", k, kx), part, part, dev(dx=kx))

    on_from_x(1)
    on_from_x(3)
    on_from_y(1)
    on_from_y(3)
    on_from_x(2)

    @pl.when(fetches)
    def _():
        ej[1 - xh, z] = ei[y, step(x, 2, 4)]
        along_z(1, 1 - xh)

    on_from_y(2)

    def hand(half, f, k):
        piece = ej.at[f, step(z, -k, 8)]
        copy(("c", half, k), piece, piece, dev(dc=1)).start()

    def from_z(half, f, k):
        piece = ej.at[f, step(z, -k, 8)]
        if k == 4:
            for s in range(2):
                arrived(("z", half, 4, s), ej.at[f, step(z, 4, 8), s * H:(s + 1) * H])
        else:
            arrived(("z", half, k), piece)
        if k == 2:
            copy(("z", half, 3), piece, piece, dev(dz=1)).start()
            part = ej.at[f, step(z, -2, 8), 0:H]
            copy(("z", half, 4, 0), part, part, dev(dz=2)).start()
        if k == 6:
            copy(("z", half, 5), piece, piece, dev(dz=-1)).start()
            part = ej.at[f, step(z, 2, 8), H:R]
            copy(("z", half, 4, 1), part, part, dev(dz=-2)).start()
        hand(half, f, k)

    @pl.when(fetches)
    def _():
        for k in (2, 6, 1, 7):
            from_z(0, xh, k)
        for k in (2, 6, 1, 7):
            from_z(1, 1 - xh, k)

    for k in (1, 3, 2):
        for j in (1, 3, 2):
            arrived(("xy", k, j), ei.at[step(y, -j, 4), step(x, -k, 4), 0:H])
            arrived(("yx", k, j), ei.at[step(y, -k, 4), step(x, -j, 4), H:R])

    def unit(dst, rows, e0, e1):
        e0 = e0.astype(F32)
        e1 = e1.astype(F32)
        inv = inverse_norm(e0, e1)
        dst[0, rows, :] = (e0 * inv).astype(BF16)
        dst[1, rows, :] = (e1 * inv).astype(BF16)

    for p in range(8):
        unit(ui, slice(p * R, (p + 1) * R), ei[p // 2, p % 2], ei[p // 2, 2 + p % 2])

    def send_hidden(n):
        kx, kc = GROUP[n]
        q = step(xl, kx, 2) * 2 + step(c, kc, 2)
        quarter_columns = pl.ds(pl.multiple_of(q * 512, 512), 512)
        if n == 0:
            hq[0:R, :] = h_ref[:, quarter_columns]
        else:
            send(("h", n), h_ref.at[:, quarter_columns], hq.at[n * R:(n + 1) * R, :], group_dev(kx, kc))

    for n in range(3):
        send_hidden(n)

    own_row = y * 4 + x
    own_col = z * 2 + c
    rowacc[...] = jnp.zeros_like(rowacc)
    rowmsg[own_row] = jnp.zeros((16, R), F32)

    def columns(first_slot, last_slot):
        for slot in range(first_slot, last_slot):
            zz = step(z, -ORDER[slot], 8)
            unit(uj, slice(slot * R, (slot + 1) * R), ej[0, zz], ej[1, zz])
        cols = slice(first_slot * R, last_slot * R)
        sums = None
        hits = None
        for b in range(4):
            rows = slice(b * 256, (b + 1) * 256)
            s = nt(ui[0, rows, :], uj[0, cols, :]) + nt(ui[1, rows, :], uj[1, cols, :])
            hit = jnp.sum(s * mark[rows, cols], axis=0, keepdims=True)
            e = jnp.exp2(EXP2_SCALE * s - EXP2_SCALE)
            if first_slot == 0:
                at = lax.broadcasted_iota(jnp.int32, (256, R), 0) - lax.broadcasted_iota(jnp.int32, (256, R), 1)
                diagonal = at == jnp.where(fetches, p_me * R - b * 256, -ROWS)
                e = jnp.concatenate([jnp.where(diagonal, 0.0, e[:, 0:R]), e[:, R:]], axis=1)
            sim[rows, cols] = e
            part = e[:, 0:R]
            for t in range(1, last_slot - first_slot):
                part = part + e[:, t * R:(t + 1) * R]
            rowacc[rows, :] = rowacc[rows, :] + part
            total = jnp.sum(e, axis=0, keepdims=True)
            sums = total if sums is None else sums + total
            hits = hit if hits is None else hits + hit
        line = hits[:, 0:R]
        for slot in range(first_slot, last_slot):
            t = slot - first_slot
            colmsg[own_col, pl.ds(step(z, -ORDER[slot], 8), 1), :] = sums[:, t * R:(t + 1) * R]
            if t:
                line = line + hits[:, t * R:(t + 1) * R]
        rowmsg[own_row, 8:9, :] = rowmsg[own_row, 8:9, :] - 0.5 * line

    def handed(slots_):
        for slot in slots_:
            for half, f in ((0, xh), (1, 1 - xh)):
                arrived(("c", half, ORDER[slot]), ej.at[f, step(z, -ORDER[slot], 8)])

    @pl.when(jnp.logical_not(fetches))
    def _():
        handed(range(5))

    columns(0, 5)
    @pl.when(fetches)
    def _():
        for half, f in ((0, xh), (1, 1 - xh)):
            for k in (3, 5, 4):
                from_z(half, f, k)

    @pl.when(jnp.logical_not(fetches))
    def _():
        handed(range(5, 8))

    columns(5, 8)
    for p in range(8):
        rowmsg[own_row, p:p + 1, :] = to_rows(rowacc[p * R:(p + 1) * R, :])

    for kz, kc in COLUMN:
        send(("col", kz, kc), colmsg.at[own_col], colmsg.at[own_col], dev(dz=kz, dc=kc))
    for ky, kx in PLANE:
        send(("row", ky, kx), rowmsg.at[own_row], rowmsg.at[own_row], dev(dy=ky, dx=kx))
    send_hidden(3)
    for ky, kx in PLANE:
        arrived(("row", ky, kx), rowmsg.at[step(y, -ky, 4) * 4 + step(x, -kx, 4)])
    for kz, kc in COLUMN:
        arrived(("col", kz, kc), colmsg.at[step(z, -kz, 8) * 2 + step(c, kc, 2)])

    all_rows = rowmsg[0]
    all_cols = colmsg[0]
    for n in range(1, 16):
        all_rows = all_rows + rowmsg[n]
        all_cols = all_cols + colmsg[n]
    row_total = all_rows[0:8]
    hit_total = all_rows[8:9]
    cost = jnp.sum(jnp.log(row_total), axis=0, keepdims=True) - SHARPNESS * (hit_total - 8.0)
    losses[own_col] = jnp.broadcast_to(cost, (8, R))

    inv_rows = 1.0 / row_total
    inv_cols = 1.0 / all_cols
    isum_cols[...] = inv_cols
    tsum[...] = jnp.concatenate([isum_cols[pl.ds(step(z, -k, 8), 1), :] for k in ORDER], axis=1)
    for p in range(8):
        factor[p] = to_columns(inv_rows[p:p + 1])
    for ky in (2, 1, 3, 0):
        y_to = step(y, ky, 4)
        rows = pl.ds(pl.multiple_of(y_to * 256, 256), 256)
        wide = jnp.concatenate([factor[pl.ds(y_to * 2, 2)].reshape(256, R)] * 8, axis=1)
        weights = (sim[rows, :] * (wide + tsum[...]) + mark[rows, :]).astype(BF16)
        acc = None
        for f in range(2):
            g = jnp.dot(weights, uj[f], preferred_element_type=F32)
            for half in range(2):
                sa[2 * f + half, y_to] = g[half * R:half * R + H].astype(BF16)
                sb[y_to, 2 * f + half] = g[half * R + H:(half + 1) * R].astype(BF16)
            t = g * ui[f, rows, :].astype(F32)
            t = t[:, 0:R] + t[:, R:]
            acc = t if acc is None else acc + t
        for kx in (2, 1, 3):
            send(("ra", kx, ky), sa.at[step(x, kx, 4), y_to], ra.at[kx, y_to], dev(dx=kx))
        if ky:
            send(("rb", ky), sb.at[y_to], rb.at[ky], dev(dy=ky))
        for half in range(2):
            v = to_rows(acc[half * R:(half + 1) * R])
            ia[half, pl.ds(y_to, 1), :] = v
            ib[y_to, half:half + 1, :] = v
        if ky:
            send(("ib", ky), ib.at[y_to], ibr.at[ky], dev(dy=ky))
    for kx in (2, 1, 3):
        send(("ia", kx), ia.at[step(xl, kx, 2)], iar.at[kx], dev(dx=kx))
    for kz, kc in COLUMN:
        send(("loss", kz, kc), losses.at[own_col], losses.at[own_col], dev(dz=kz, dc=kc))

    for ky in (2, 1, 3):
        arrived(("rb", ky), rb.at[ky])
        arrived(("ib", ky), ibr.at[ky])
    line = ib[y] + ibr[1] + ibr[2] + ibr[3]
    isum[1] = line
    for half in range(2):
        ib2[half] = jnp.broadcast_to(line[half:half + 1], (8, R))
    for kx in (2, 1, 3):
        x_to = step(x, kx, 4)
        g = sb[y, x_to].astype(F32) + rb[1, x_to].astype(F32) + rb[2, x_to].astype(F32) + rb[3, x_to].astype(F32)
        sb2[kx] = g.astype(BF16)
        send(("rb2", kx), sb2.at[kx], rb2.at[kx], dev(dx=kx))
        send(("ib2", kx), ib2.at[step(xl, kx, 2)], ibr2.at[kx], dev(dx=kx))
    g_b = sb[y, x].astype(F32) + rb[1, x].astype(F32) + rb[2, x].astype(F32) + rb[3, x].astype(F32)
    for kx in (2, 1, 3):
        arrived(("ia", kx), iar.at[kx])
        for ky in range(4):
            arrived(("ra", kx, ky), ra.at[kx, step(y, ky, 4)])
    line = ia[xl] + iar[1] + iar[2] + iar[3]
    isum[0] = line
    for yy in range(4):
        ia2[yy] = jnp.broadcast_to(line[yy:yy + 1], (8, R))
    for ky in (2, 1, 3):
        y_to = step(y, ky, 4)
        g = sa[x, y_to].astype(F32) + ra[1, y_to].astype(F32) + ra[2, y_to].astype(F32) + ra[3, y_to].astype(F32)
        sa2[ky] = g.astype(BF16)
        send(("ra2", ky), sa2.at[ky], ra2.at[ky], dev(dy=ky))
        send(("ia2", ky), ia2.at[y_to], iar2.at[ky], dev(dy=ky))
    g_a = sa[x, y].astype(F32) + ra[1, y].astype(F32) + ra[2, y].astype(F32) + ra[3, y].astype(F32)
    inner_a = isum[0, pl.ds(y, 1), :]
    inner_b = isum[1, pl.ds(xl, 1), :]
    for k in (1, 3, 2):
        arrived(("rb2", k), rb2.at[k])
        arrived(("ib2", k), ibr2.at[k])
        arrived(("ra2", k), ra2.at[k])
        arrived(("ia2", k), iar2.at[k])
        g_a = g_a + ra2[k].astype(F32)
        g_b = g_b + rb2[k].astype(F32)
        inner_a = inner_a + iar2[k, 0:1]
        inner_b = inner_b + ibr2[k, 0:1]
    inner = to_columns(jnp.where(lanes < H, inner_a, inner_b))
    inv = inverse_norm(ei[y, xl].astype(F32), ei[y, 2 + xl].astype(F32))
    own_unit = ei[y, x].astype(F32) * inv
    g = jnp.concatenate([g_a, g_b], axis=0)
    grad = (SHARPNESS * inv) * (g - own_unit * jnp.concatenate([inner, inner], axis=1))
    gemb_ref[...] = grad
    g4[0:R, :] = grad.astype(BF16)

    def block_of(n):
        return g4.at[n * R:(n + 1) * R, :]

    def tn(a, b):
        return lax.dot_general(a, b, (((0,), (0,)), ((), ())), preferred_element_type=F32)

    send(("g", 2), block_of(0), block_of(2), group_dev(1, 0))
    send(("g", 1), block_of(0), block_of(1), group_dev(0, 1))
    for n in range(1, 4):
        arrived(("h", n), hq.at[n * R:(n + 1) * R, :])
    arrived(("g", 1), block_of(1))
    near = tn(hq[0:2 * R, :], g4[0:2 * R, :])
    arrived(("g", 2), block_of(2))
    send(("g", 3), block_of(2), block_of(3), group_dev(0, 1))
    arrived(("g", 3), block_of(3))
    full = near + tn(hq[2 * R:, :], g4[2 * R:, :])
    gp[...] = full
    gpb[...] = full.astype(BF16)
    for ky in (2, 1, 3):
        part = gpb.at[pl.ds(pl.multiple_of(step(y, ky, 4) * R, R), R), :]
        send(("gy", ky), part, ry.at[ky], dev(dy=ky))
    part = gp[pl.ds(pl.multiple_of(y * R, R), R), :]
    for ky in (1, 3, 2):
        arrived(("gy", ky), ry.at[ky])
        part = part + ry[ky].astype(F32)
    gp[0:R, :] = part
    rzb[...] = part.astype(BF16)
    for kz in (4, 3, 5, 2, 6, 1, 7):
        piece = rzb.at[pl.ds(pl.multiple_of(step(z, kz, 8) * 16, 16), 16), :]
        send(("gz", kz), piece, rz.at[kz], dev(dz=kz))
    piece = gp[pl.ds(pl.multiple_of(z * 16, 16), 16), :]
    for kz in (1, 7, 2, 6, 3, 5, 4):
        arrived(("gz", kz), rz.at[kz])
        piece = piece + rz[kz].astype(F32)

    def rows_of(q_, y_, z_=None):
        if z_ is None:
            return gproj_ref.at[pl.ds(pl.multiple_of(q_ * 512 + y_ * R, R), R), :]
        return gproj_ref.at[pl.ds(pl.multiple_of(q_ * 512 + y_ * R + z_ * 16, 16), 16), :]

    gproj_ref[pl.ds(pl.multiple_of(q_me * 512 + y * R + z * 16, 16), 16), :] = piece.astype(BF16)
    mine = rows_of(q_me, y, z)
    for kz in (4, 3, 5, 2, 6, 1, 7):
        send(("az", kz), mine, mine, dev(dz=kz))

    def spread(kz):
        there = rows_of(q_me, y, step(z, -kz, 8))
        if kz:
            arrived(("az", kz), there)
        for ky in (2, 1, 3):
            send(("ay", ky, kz), there, there, dev(dy=ky))
        send(("ax", 0, kz), there, there, group_dev(1, 0))

    by_distance = (0, 1, 7, 2, 6, 3, 5, 4)
    for kz in by_distance:
        spread(kz)

    mine = rows_of(q_me, y)
    send(("ac", 0, 0), mine, mine, group_dev(0, 1))
    for ky in (1, 3, 2):
        y_from = step(y, -ky, 4)
        for kz in by_distance:
            arrived(("ay", ky, kz), rows_of(q_me, y_from, step(z, -kz, 8)))
        there = rows_of(q_me, y_from)
        send(("ax", ky), there, there, group_dev(1, 0))
        send(("ac", 0, ky), there, there, group_dev(0, 1))
    for kz in by_distance:
        arrived(("ax", 0, kz), rows_of((1 - xl) * 2 + c, y, step(z, -kz, 8)))
    for ky in (0, 1, 3, 2):
        there = rows_of((1 - xl) * 2 + c, step(y, -ky, 4))
        if ky:
            arrived(("ax", ky), there)
        send(("ac", 1, ky), there, there, group_dev(0, 1))

    for kz, kc in COLUMN:
        arrived(("loss", kz, kc), losses.at[step(z, -kz, 8) * 2 + step(c, kc, 2)])
    cost = losses[0]
    for n in range(1, 16):
        cost = cost + losses[n]
    loss_ref[...] = jnp.broadcast_to(jnp.sum(cost, axis=1, keepdims=True) * (1.0 / ROWS), (8, R))

    for ky in (0, 1, 3, 2):
        arrived(("ac", 0, ky), rows_of(xl * 2 + (1 - c), step(y, -ky, 4)))
        arrived(("ac", 1, ky), rows_of((1 - xl) * 2 + (1 - c), step(y, -ky, 4)))
    for one in sent:
        one.wait_send()

    @pl.when(fetches)
    def _():
        whole = ej.at[0, 0]
        half_piece = ej.at[0, 0, 0:H]
        for half in range(2):
            for k in (2, 6, 1, 7, 3, 5):
                copy(("z", half, k), whole, whole, dev(dc=1)).wait_send()
            for s in range(2):
                copy(("z", half, 4, s), half_piece, half_piece, dev(dc=1)).wait_send()
            for k in range(8):
                copy(("c", half, k), whole, whole, dev(dc=1)).wait_send()


def per_device(head_hidden, proj_weight, pair_perm):
    vmem = pltpu.VMEM
    hbm = pl.BlockSpec(memory_space=pltpu.HBM)
    space = pl.BlockSpec(memory_space=pltpu.VMEM)
    loss, grad_emb, grad_proj = pl.pallas_call(
        kernel,
        out_shape=(
            jax.ShapeDtypeStruct((8, R), F32),
            jax.ShapeDtypeStruct((R, 256), F32),
            jax.ShapeDtypeStruct((2048, 256), BF16),
        ),
        in_specs=[hbm] * 3,
        out_specs=[space] * 3,
        scratch_shapes=[
            vmem((R, 2048), BF16),
            vmem((2048, 256), BF16),
            vmem((64, R), jnp.int32),
            vmem((4, 4, R, 256), BF16),
            vmem((2, 8, R, 256), BF16),
            vmem((2, 1024, 256), BF16),
            vmem((2, 1024, 256), BF16),
            vmem((1024, 1024), F32),
            vmem((1024, 1024), F32),
            vmem((16, 16, R), F32),
            vmem((16, 8, R), F32),
            vmem((16, 8, R), F32),
            vmem((1, 1024), F32),
            vmem((8, R), F32),
            vmem((1024, R), F32),
            vmem((8, R, R), F32),
            vmem((4, 4, H, 256), BF16),
            vmem((4, 4, H, 256), BF16),
            vmem((4, 4, H, 256), BF16),
            vmem((4, 4, H, 256), BF16),
            vmem((4, H, 256), BF16),
            vmem((4, H, 256), BF16),
            vmem((4, H, 256), BF16),
            vmem((4, H, 256), BF16),
            vmem((2, 8, R), F32),
            vmem((4, 8, R), F32),
            vmem((4, 8, R), F32),
            vmem((4, 8, R), F32),
            vmem((4, 8, R), F32),
            vmem((2, 8, R), F32),
            vmem((4, 8, R), F32),
            vmem((4, 8, R), F32),
            vmem((2, 8, R), F32),
            vmem((512, 256), BF16),
            vmem((512, 512), BF16),
            vmem((512, 256), F32),
            vmem((512, 256), BF16),
            vmem((4, R, 256), BF16),
            vmem((8, 16, 256), BF16),
            vmem((R, 256), BF16),
            pltpu.SemaphoreType.DMA((3,)),
            pltpu.SemaphoreType.DMA((COPIES,)),
            pltpu.SemaphoreType.DMA((COPIES,)),
        ],
        compiler_params=pltpu.CompilerParams(
            collective_id=0, has_side_effects=True, vmem_limit_bytes=40 * 1024 * 1024
        ),
    )(*[pltpu.with_memory_space_constraint(v, pltpu.HBM) for v in (head_hidden, proj_weight, pair_perm.reshape(64, R))])
    return loss[0, 0], grad_emb, grad_proj.astype(F32)


def solution(mesh):
    placed = (P("dp", None), P(None, "mp"), P())
    return jax.shard_map(
        per_device,
        mesh=mesh,
        in_specs=placed,
        out_specs=(P(), P("dp", "mp"), P(None, "mp")),
        check_vma=False,
    )
```

```python
import jax
import jax.numpy as jnp
from jax import lax
from jax.experimental import pallas as pl
from jax.experimental.pallas import tpu as pltpu
from jax.sharding import PartitionSpec as P

MESH = pl.DeviceIdType.MESH
F32 = jnp.float32
BF16 = jnp.bfloat16
SHARPNESS = 10.0
EXP2_SCALE = SHARPNESS * 1.4426950408889634
ORDER = (0, 1, 7, 2, 6, 3, 5, 4)
R = 128
H = 64
ROWS = 16384
COPIES = 288


def far(k, n):
    return min(k, n - k)


PLANE = sorted([(ky, kx) for ky in range(4) for kx in range(4)][1:], key=lambda k: -far(k[0], 4) - far(k[1], 4))
COLUMN = sorted([(kz, kc) for kz in range(8) for kc in range(2)][1:], key=lambda k: -far(k[0], 8))
GROUP = [(kx, kc) for kx in range(2) for kc in range(2)]


def nt(a, b):
    return lax.dot_general(a, b, (((1,), (1,)), ((), ())), preferred_element_type=F32)


def to_rows(x):
    return jnp.sum(x.T, axis=0, keepdims=True)


def to_columns(row):
    return jnp.broadcast_to(row, (R, R)).T


def inverse_norm(e0, e1):
    return lax.rsqrt(jnp.sum(e0 * e0 + e1 * e1, axis=1, keepdims=True) + 1e-06)


def kernel(
    h_hbm, w_hbm, perm_hbm,
    loss_ref, gemb_ref, gproj_ref,
    h_ref, w_ref, perm_ref, ei, ej, ui, uj, sim, mark, rowmsg, colmsg, losses, tsum, isum_cols, rowacc, factor,
    sa, sb, ra, rb, sa2, sb2, ra2, rb2, inner_out, inner_in,
    g4, hq, gp, gpb, ry, rz, rzb, s_in, s_out, s_back,
):
    dp = lax.axis_index("dp")
    xh = lax.axis_index("mp")
    c = lax.rem(dp, 2)
    xl = lax.rem(dp // 2, 2)
    y = lax.rem(dp // 4, 4)
    z = dp // 16
    x = xh * 2 + xl
    p_me = y * 2 + xl
    q_me = xl * 2 + c
    fetches = c == xh

    def dev(dz=0, dy=0, dx=0, dc=0):
        x_ = step(x, dx, 4)
        return (((step(z, dz, 8) * 4 + step(y, dy, 4)) * 2 + lax.rem(x_, 2)) * 2 + step(c, dc, 2), x_ // 2)

    def step(v, k, n):
        k = k % n
        return v if k == 0 else lax.rem(v + k, n)

    def group_dev(kx, kc):
        return (((z * 4 + y) * 2 + step(xl, kx, 2)) * 2 + step(c, kc, 2), xh)

    slots = {}

    def copy(key, src, dst, to):
        n = slots.setdefault(key, len(slots))
        return pltpu.make_async_remote_copy(
            src_ref=src, dst_ref=dst, send_sem=s_out.at[n], recv_sem=s_back.at[n],
            device_id=to, device_id_type=MESH,
        )

    sent = []

    def send(key, src, dst, to):
        one = copy(key, src, dst, to)
        one.start()
        sent.append(one)

    def arrived(key, dst):
        copy(key, dst, dst, dev(dc=1)).wait_recv()

    loads = [
        pltpu.make_async_copy(h_hbm, h_ref, s_in.at[0]),
        pltpu.make_async_copy(w_hbm, w_ref, s_in.at[1]),
        pltpu.make_async_copy(perm_hbm, perm_ref, s_in.at[2]),
    ]
    for load in loads:
        load.start()

    barrier = pltpu.get_barrier_semaphore()
    peers = [dev(dz=kz, dc=kc) for kz, kc in COLUMN] + [dev(dy=ky, dx=kx) for ky, kx in PLANE] + [group_dev(1, 1)]
    for peer in peers:
        pl.semaphore_signal(barrier, inc=1, device_id=peer, device_id_type=MESH)
    for load in loads:
        load.wait()

    embed = jnp.dot(h_ref[...], w_ref[...], preferred_element_type=F32).astype(BF16)
    ei[y, x] = embed

    @pl.when(fetches)
    def _():
        ej[xh, z] = ei[y, x]

    pl.semaphore_wait(barrier, len(peers))

    def half_rows(ref, *at):
        return [ref.at[(*at, slice(0, H))], ref.at[(*at, slice(H, R))]]

    own = half_rows(ei, y, x)
    for k, i in ((2, 0), (2, 1), (1, 0), (3, 0), (1, 1), (3, 1)):
        send(("x", k, i), own[i], own[i], dev(dx=k))
    for k, i in ((1, 1), (3, 1), (2, 1), (1, 0), (3, 0), (2, 0)):
        send(("y", k, i), own[i], own[i], dev(dy=k))

    def along_z(half, f, i):
        piece = half_rows(ej, f, z)[i]
        for k in (2, 6, 1, 7):
            copy(("z", half, k, i), piece, piece, dev(dz=k)).start()

    def hand(half, f, k):
        piece = ej.at[f, step(z, -k, 8)]
        copy(("c", half, k), piece, piece, dev(dc=1)).start()

    @pl.when(fetches)
    def _():
        along_z(0, xh, 0)
        along_z(0, xh, 1)
        hand(0, xh, 0)

    first = z < 4
    lanes = lax.broadcasted_iota(jnp.int32, (1, R), 1)
    b_row = []
    for k in ORDER:
        zz = step(z, -k, 8)
        jglob = (((zz * 4 + y) * 2 + xl) * 2 + xh) * R + lanes
        pair = perm_ref[pl.ds(lax.rem(zz, 4) * 16 + y * 4 + xl * 2 + xh, 1), :] + ROWS // 2
        b_row.append(jnp.where(first, jglob, jnp.where(zz < 4, pair, -1)).astype(F32))
    b_row = jnp.concatenate(b_row, axis=1)
    for p in range(8):
        mine = (z * 16 + p * 2 + c) * R + lanes
        pair = perm_ref[pl.ds(lax.rem(z, 4) * 16 + p * 2 + c, 1), :] + ROWS // 2
        a_col = to_columns(jnp.where(first, pair, mine).astype(F32))
        mark[p * R:(p + 1) * R, :] = jnp.where(jnp.concatenate([a_col] * 8, axis=1) == b_row, -2.0, 0.0)

    def on_from_x(k):
        part = half_rows(ei, y, step(x, -k, 4))[0]
        arrived(("x", k, 0), part)
        for ky in (2, 1, 3):
            send(("xy", k, ky), part, part, dev(dy=ky))

    def on_from_y(k):
        part = half_rows(ei, step(y, -k, 4), x)[1]
        arrived(("y", k, 1), part)
        for kx in (2, 1, 3):
            send(("yx", k, kx), part, part, dev(dx=kx))

    across = step(x, 2, 4)
    on_from_x(2)

    @pl.when(fetches)
    def _():
        ej[1 - xh, z, 0:H] = ei[y, across, 0:H]
        along_z(1, 1 - xh, 0)

    arrived(("x", 2, 1), half_rows(ei, y, across)[1])

    @pl.when(fetches)
    def _():
        ej[1 - xh, z, H:R] = ei[y, across, H:R]
        along_z(1, 1 - xh, 1)
        hand(1, 1 - xh, 0)

    on_from_x(1)
    on_from_x(3)
    on_from_y(1)
    on_from_y(3)
    on_from_y(2)

    def from_z(half, f, k, i):
        part = half_rows(ej, f, step(z, -k, 8))[i]
        arrived(("z", half, k, i), part)
        if k == 2:
            if i == 0:
                copy(("z", half, 4, 0), part, part, dev(dz=2)).start()
            copy(("z", half, 3, i), part, part, dev(dz=1)).start()
        if k == 6:
            if i == 1:
                copy(("z", half, 4, 1), part, part, dev(dz=-2)).start()
            copy(("z", half, 5, i), part, part, dev(dz=-1)).start()

    @pl.when(fetches)
    def _():
        for half, f in ((0, xh), (1, 1 - xh)):
            for k, i in ((2, 0), (6, 1), (2, 1), (6, 0)):
                from_z(half, f, k, i)
            hand(half, f, 2)
            hand(half, f, 6)
            for k in (1, 7):
                from_z(half, f, k, 0)
                from_z(half, f, k, 1)
                hand(half, f, k)

    for k in (1, 3, 2):
        if k != 2:
            arrived(("x", k, 1), half_rows(ei, y, step(x, -k, 4))[1])
        arrived(("y", k, 0), half_rows(ei, step(y, -k, 4), x)[0])
    for k in (1, 3, 2):
        for j in (1, 3, 2):
            arrived(("xy", k, j), half_rows(ei, step(y, -j, 4), step(x, -k, 4))[0])
            arrived(("yx", k, j), half_rows(ei, step(y, -k, 4), step(x, -j, 4))[1])

    def unit(dst, rows, e0, e1):
        e0 = e0.astype(F32)
        e1 = e1.astype(F32)
        inv = inverse_norm(e0, e1)
        dst[0, rows, :] = (e0 * inv).astype(BF16)
        dst[1, rows, :] = (e1 * inv).astype(BF16)

    for p in range(8):
        unit(ui, slice(p * R, (p + 1) * R), ei[p // 2, p % 2], ei[p // 2, 2 + p % 2])

    def send_hidden(n):
        kx, kc = GROUP[n]
        q = step(xl, kx, 2) * 2 + step(c, kc, 2)
        quarter_columns = pl.ds(pl.multiple_of(q * 512, 512), 512)
        if n == 0:
            hq[0:R, :] = h_ref[:, quarter_columns]
        else:
            send(("h", n), h_ref.at[:, quarter_columns], hq.at[n * R:(n + 1) * R, :], group_dev(kx, kc))

    for n in range(3):
        send_hidden(n)

    own_row = y * 4 + x
    own_col = z * 2 + c
    rowacc[...] = jnp.zeros_like(rowacc)
    rowmsg[own_row] = jnp.zeros((16, R), F32)

    def columns(first_slot, last_slot):
        for slot in range(first_slot, last_slot):
            zz = step(z, -ORDER[slot], 8)
            unit(uj, slice(slot * R, (slot + 1) * R), ej[0, zz], ej[1, zz])
        cols = slice(first_slot * R, last_slot * R)
        sums = None
        hits = None
        for b in range(4):
            rows = slice(b * 256, (b + 1) * 256)
            s = nt(ui[0, rows, :], uj[0, cols, :]) + nt(ui[1, rows, :], uj[1, cols, :])
            hit = jnp.sum(s * mark[rows, cols], axis=0, keepdims=True)
            e = jnp.exp2(EXP2_SCALE * s - EXP2_SCALE)
            if first_slot == 0:
                at = lax.broadcasted_iota(jnp.int32, (256, R), 0) - lax.broadcasted_iota(jnp.int32, (256, R), 1)
                diagonal = at == jnp.where(fetches, p_me * R - b * 256, -ROWS)
                e = jnp.concatenate([jnp.where(diagonal, 0.0, e[:, 0:R]), e[:, R:]], axis=1)
            sim[rows, cols] = e
            part = e[:, 0:R]
            for t in range(1, last_slot - first_slot):
                part = part + e[:, t * R:(t + 1) * R]
            rowacc[rows, :] = rowacc[rows, :] + part
            total = jnp.sum(e, axis=0, keepdims=True)
            sums = total if sums is None else sums + total
            hits = hit if hits is None else hits + hit
        line = hits[:, 0:R]
        for slot in range(first_slot, last_slot):
            t = slot - first_slot
            colmsg[own_col, pl.ds(step(z, -ORDER[slot], 8), 1), :] = sums[:, t * R:(t + 1) * R]
            if t:
                line = line + hits[:, t * R:(t + 1) * R]
        rowmsg[own_row, 8:9, :] = rowmsg[own_row, 8:9, :] - 0.5 * line

    def handed(slots_):
        for slot in slots_:
            for half, f in ((0, xh), (1, 1 - xh)):
                arrived(("c", half, ORDER[slot]), ej.at[f, step(z, -ORDER[slot], 8)])

    @pl.when(jnp.logical_not(fetches))
    def _():
        handed(range(5))

    columns(0, 5)
    @pl.when(fetches)
    def _():
        for half, f in ((0, xh), (1, 1 - xh)):
            for k in (3, 5, 4):
                from_z(half, f, k, 0)
                from_z(half, f, k, 1)
                hand(half, f, k)

    @pl.when(jnp.logical_not(fetches))
    def _():
        handed(range(5, 8))

    columns(5, 8)
    for p in range(8):
        rowmsg[own_row, p:p + 1, :] = to_rows(rowacc[p * R:(p + 1) * R, :])

    for kz, kc in COLUMN:
        send(("col", kz, kc), colmsg.at[own_col], colmsg.at[own_col], dev(dz=kz, dc=kc))
    for ky, kx in PLANE:
        send(("row", ky, kx), rowmsg.at[own_row], rowmsg.at[own_row], dev(dy=ky, dx=kx))
    send_hidden(3)
    for ky, kx in PLANE:
        arrived(("row", ky, kx), rowmsg.at[step(y, -ky, 4) * 4 + step(x, -kx, 4)])
    for kz, kc in COLUMN:
        arrived(("col", kz, kc), colmsg.at[step(z, -kz, 8) * 2 + step(c, kc, 2)])

    all_rows = rowmsg[0]
    all_cols = colmsg[0]
    for n in range(1, 16):
        all_rows = all_rows + rowmsg[n]
        all_cols = all_cols + colmsg[n]
    row_total = all_rows[0:8]
    hit_total = all_rows[8:9]
    cost = jnp.sum(jnp.log(row_total), axis=0, keepdims=True) - SHARPNESS * (hit_total - 8.0)
    losses[own_col] = jnp.broadcast_to(cost, (8, R))

    inv_rows = 1.0 / row_total
    inv_cols = 1.0 / all_cols
    isum_cols[...] = inv_cols
    tsum[...] = jnp.concatenate([isum_cols[pl.ds(step(z, -k, 8), 1), :] for k in ORDER], axis=1)
    for p in range(8):
        factor[p] = to_columns(inv_rows[p:p + 1])
    def send_b(ky, kx):
        y_to, x_to = step(y, ky, 4), step(x, kx, 4)
        send(("rb", ky, kx), sb.at[y_to, x_to], rb.at[ky, x_to], dev(dy=ky))

    for ky in (2, 1, 3, 0):
        y_to = step(y, ky, 4)
        rows = pl.ds(pl.multiple_of(y_to * 256, 256), 256)
        wide = jnp.concatenate([factor[pl.ds(y_to * 2, 2)].reshape(256, R)] * 8, axis=1)
        weights = (sim[rows, :] * (wide + tsum[...]) + mark[rows, :]).astype(BF16)
        acc = None
        for f in range(2):
            g = jnp.dot(weights, uj[f], preferred_element_type=F32)
            for half in range(2):
                sa[2 * f + half, y_to] = g[half * R:half * R + H].astype(BF16)
                sb[y_to, 2 * f + half] = g[half * R + H:(half + 1) * R].astype(BF16)
            t = g * ui[f, rows, :].astype(F32)
            t = t[:, 0:R] + t[:, R:]
            acc = t if acc is None else acc + t
        for kx in (2, 1, 3):
            send(("ra", kx, ky), sa.at[step(x, kx, 4), y_to], ra.at[kx, y_to], dev(dx=kx))
        if ky:
            send_b(ky, 2)
        for half in range(2):
            v = to_rows(acc[half * R:(half + 1) * R])
            inner_out[y_to, half] = jnp.broadcast_to(v, (8, R))
        for kx in (2, 1, 3, 0):
            if ky or kx:
                send(
                    ("in", ky, kx), inner_out.at[y_to, step(xl, kx, 2)], inner_in.at[ky * 4 + kx],
                    dev(dy=ky, dx=kx),
                )
    for kx in (1, 3, 0):
        for ky in (2, 1, 3):
            send_b(ky, kx)
    for kz, kc in COLUMN:
        send(("loss", kz, kc), losses.at[own_col], losses.at[own_col], dev(dz=kz, dc=kc))

    def total_a(ky):
        y_to = step(y, ky, 4)
        g = sa[x, y_to].astype(F32)
        for kx in (1, 2, 3):
            arrived(("ra", kx, ky), ra.at[kx, y_to])
            g = g + ra[kx, y_to].astype(F32)
        return g

    def total_b(kx):
        x_to = step(x, kx, 4)
        g = sb[y, x_to].astype(F32)
        for ky in (1, 2, 3):
            arrived(("rb", ky, kx), rb.at[ky, x_to])
            g = g + rb[ky, x_to].astype(F32)
        return g

    for k in (2, 1, 3):
        sa2[k] = total_a(k).astype(BF16)
        send(("ra2", k), sa2.at[k], ra2.at[k], dev(dy=k))
        sb2[k] = total_b(k).astype(BF16)
        send(("rb2", k), sb2.at[k], rb2.at[k], dev(dx=k))
    g_a = total_a(0)
    g_b = total_b(0)
    inner = inner_out[y, xl, 0:1]
    for ky, kx in PLANE:
        arrived(("in", ky, kx), inner_in.at[ky * 4 + kx])
        inner = inner + inner_in[ky * 4 + kx, 0:1]
    for k in (2, 1, 3):
        arrived(("ra2", k), ra2.at[k])
        arrived(("rb2", k), rb2.at[k])
        g_a = g_a + ra2[k].astype(F32)
        g_b = g_b + rb2[k].astype(F32)
    inner = to_columns(inner)
    inv = inverse_norm(ei[y, xl].astype(F32), ei[y, 2 + xl].astype(F32))
    own_unit = ei[y, x].astype(F32) * inv
    g = jnp.concatenate([g_a, g_b], axis=0)
    grad = (SHARPNESS * inv) * (g - own_unit * jnp.concatenate([inner, inner], axis=1))
    gemb_ref[...] = grad
    g4[0:R, :] = grad.astype(BF16)

    def block_of(n):
        return g4.at[n * R:(n + 1) * R, :]

    def tn(a, b):
        return lax.dot_general(a, b, (((0,), (0,)), ((), ())), preferred_element_type=F32)

    send(("g", 2), block_of(0), block_of(2), group_dev(1, 0))
    send(("g", 1), block_of(0), block_of(1), group_dev(0, 1))
    for n in range(1, 4):
        arrived(("h", n), hq.at[n * R:(n + 1) * R, :])
    arrived(("g", 1), block_of(1))
    near = tn(hq[0:2 * R, :], g4[0:2 * R, :])
    arrived(("g", 2), block_of(2))
    send(("g", 3), block_of(2), block_of(3), group_dev(0, 1))
    arrived(("g", 3), block_of(3))
    full = near + tn(hq[2 * R:, :], g4[2 * R:, :])
    gp[...] = full
    gpb[...] = full.astype(BF16)
    def piece_at(kz, ky):
        return pl.ds(pl.multiple_of(step(y, ky, 4) * R + step(z, kz, 8) * 16, 16), 16)

    for kz in (4, 3, 5, 2, 6, 1, 7, 0):
        for ky in (2, 1, 3):
            send(("gy", ky, kz), gpb.at[piece_at(kz, ky), :], ry.at[ky, kz], dev(dy=ky))
    for kz in (4, 3, 5, 2, 6, 1, 7, 0):
        piece = gp[piece_at(kz, 0), :]
        for ky in (1, 3, 2):
            arrived(("gy", ky, kz), ry.at[ky, kz])
            piece = piece + ry[ky, kz].astype(F32)
        if kz:
            rzb[kz] = piece.astype(BF16)
            send(("gz", kz), rzb.at[kz], rz.at[kz], dev(dz=kz))
    for kz in (1, 7, 2, 6, 3, 5, 4):
        arrived(("gz", kz), rz.at[kz])
        piece = piece + rz[kz].astype(F32)

    def rows_of(q_, y_, z_=None):
        if z_ is None:
            return gproj_ref.at[pl.ds(pl.multiple_of(q_ * 512 + y_ * R, R), R), :]
        return gproj_ref.at[pl.ds(pl.multiple_of(q_ * 512 + y_ * R + z_ * 16, 16), 16), :]

    gproj_ref[pl.ds(pl.multiple_of(q_me * 512 + y * R + z * 16, 16), 16), :] = piece.astype(BF16)
    mine = rows_of(q_me, y, z)
    for kz in (4, 3, 5, 2, 6, 1, 7):
        send(("az", kz), mine, mine, dev(dz=kz))

    def spread(kz):
        there = rows_of(q_me, y, step(z, -kz, 8))
        if kz:
            arrived(("az", kz), there)
        for ky in (2, 1, 3):
            send(("ay", ky, kz), there, there, dev(dy=ky))
        send(("ax", 0, kz), there, there, group_dev(1, 0))

    by_distance = (0, 1, 7, 2, 6, 3, 5, 4)
    for kz in by_distance:
        spread(kz)

    mine = rows_of(q_me, y)
    send(("ac", 0, 0), mine, mine, group_dev(0, 1))
    for ky in (1, 3, 2):
        y_from = step(y, -ky, 4)
        for kz in by_distance:
            arrived(("ay", ky, kz), rows_of(q_me, y_from, step(z, -kz, 8)))
        there = rows_of(q_me, y_from)
        send(("ax", ky), there, there, group_dev(1, 0))
        send(("ac", 0, ky), there, there, group_dev(0, 1))
    for kz in by_distance:
        arrived(("ax", 0, kz), rows_of((1 - xl) * 2 + c, y, step(z, -kz, 8)))
    for ky in (0, 1, 3, 2):
        there = rows_of((1 - xl) * 2 + c, step(y, -ky, 4))
        if ky:
            arrived(("ax", ky), there)
        send(("ac", 1, ky), there, there, group_dev(0, 1))

    for kz, kc in COLUMN:
        arrived(("loss", kz, kc), losses.at[step(z, -kz, 8) * 2 + step(c, kc, 2)])
    cost = losses[0]
    for n in range(1, 16):
        cost = cost + losses[n]
    loss_ref[...] = jnp.broadcast_to(jnp.sum(cost, axis=1, keepdims=True) * (1.0 / ROWS), (8, R))

    for ky in (0, 1, 3, 2):
        arrived(("ac", 0, ky), rows_of(xl * 2 + (1 - c), step(y, -ky, 4)))
        arrived(("ac", 1, ky), rows_of((1 - xl) * 2 + (1 - c), step(y, -ky, 4)))
    for one in sent:
        one.wait_send()

    @pl.when(fetches)
    def _():
        whole = ej.at[0, 0]
        part = ej.at[0, 0, 0:H]
        for half in range(2):
            for k in range(1, 8):
                for i in range(2):
                    copy(("z", half, k, i), part, part, dev(dc=1)).wait_send()
            for k in range(8):
                copy(("c", half, k), whole, whole, dev(dc=1)).wait_send()


def per_device(head_hidden, proj_weight, pair_perm):
    vmem = pltpu.VMEM
    hbm = pl.BlockSpec(memory_space=pltpu.HBM)
    space = pl.BlockSpec(memory_space=pltpu.VMEM)
    loss, grad_emb, grad_proj = pl.pallas_call(
        kernel,
        out_shape=(
            jax.ShapeDtypeStruct((8, R), F32),
            jax.ShapeDtypeStruct((R, 256), F32),
            jax.ShapeDtypeStruct((2048, 256), BF16),
        ),
        in_specs=[hbm] * 3,
        out_specs=[space] * 3,
        scratch_shapes=[
            vmem((R, 2048), BF16),
            vmem((2048, 256), BF16),
            vmem((64, R), jnp.int32),
            vmem((4, 4, R, 256), BF16),
            vmem((2, 8, R, 256), BF16),
            vmem((2, 1024, 256), BF16),
            vmem((2, 1024, 256), BF16),
            vmem((1024, 1024), F32),
            vmem((1024, 1024), F32),
            vmem((16, 16, R), F32),
            vmem((16, 8, R), F32),
            vmem((16, 8, R), F32),
            vmem((1, 1024), F32),
            vmem((8, R), F32),
            vmem((1024, R), F32),
            vmem((8, R, R), F32),
            vmem((4, 4, H, 256), BF16),
            vmem((4, 4, H, 256), BF16),
            vmem((4, 4, H, 256), BF16),
            vmem((4, 4, H, 256), BF16),
            vmem((4, H, 256), BF16),
            vmem((4, H, 256), BF16),
            vmem((4, H, 256), BF16),
            vmem((4, H, 256), BF16),
            vmem((4, 2, 8, R), F32),
            vmem((16, 8, R), F32),
            vmem((512, 256), BF16),
            vmem((512, 512), BF16),
            vmem((512, 256), F32),
            vmem((512, 256), BF16),
            vmem((4, 8, 16, 256), BF16),
            vmem((8, 16, 256), BF16),
            vmem((8, 16, 256), BF16),
            pltpu.SemaphoreType.DMA((3,)),
            pltpu.SemaphoreType.DMA((COPIES,)),
            pltpu.SemaphoreType.DMA((COPIES,)),
        ],
        compiler_params=pltpu.CompilerParams(
            collective_id=0, has_side_effects=True, vmem_limit_bytes=40 * 1024 * 1024
        ),
    )(*[pltpu.with_memory_space_constraint(v, pltpu.HBM) for v in (head_hidden, proj_weight, pair_perm.reshape(64, R))])
    return loss[0, 0], grad_emb, grad_proj.astype(F32)


def solution(mesh):
    placed = (P("dp", None), P(None, "mp"), P())
    return jax.shard_map(
        per_device,
        mesh=mesh,
        in_specs=placed,
        out_specs=(P(), P("dp", "mp"), P(None, "mp")),
        check_vma=False,
    )
```

```python
import jax
import jax.numpy as jnp
from jax import lax
from jax.experimental import pallas as pl
from jax.experimental.pallas import tpu as pltpu
from jax.sharding import PartitionSpec as P

MESH = pl.DeviceIdType.MESH
F32 = jnp.float32
BF16 = jnp.bfloat16
SHARPNESS = 10.0
EXP2_SCALE = SHARPNESS * 1.4426950408889634
ORDER = (0, 1, 7, 2, 6, 3, 5, 4)
R = 128
H = 64
ROWS = 16384
COPIES = 320


def far(k, n):
    return min(k, n - k)


PLANE = sorted([(ky, kx) for ky in range(4) for kx in range(4)][1:], key=lambda k: -far(k[0], 4) - far(k[1], 4))
COLUMN = sorted([(kz, kc) for kz in range(8) for kc in range(2)][1:], key=lambda k: -far(k[0], 8))


def nt(a, b):
    return lax.dot_general(a, b, (((1,), (1,)), ((), ())), preferred_element_type=F32)


def to_rows(x):
    return jnp.sum(x.T, axis=0, keepdims=True)


def to_columns(row):
    return jnp.broadcast_to(row, (R, R)).T


def inverse_norm(e0, e1):
    return lax.rsqrt(jnp.sum(e0 * e0 + e1 * e1, axis=1, keepdims=True) + 1e-06)


def kernel(
    h_hbm, w_hbm, perm_hbm,
    loss_ref, gemb_ref, gproj_ref,
    h_ref, w_ref, perm_ref, ei, ej, ui, uj, sim, mark, rowmsg, colmsg, losses, tsum, isum_cols, rowacc, factor,
    sa, sb, ra, rb, sa2, sb2, ra2, rb2, inner_out, inner_in,
    gout, g4, hq, gp, gpb, ry, rz, rzb, s_in, s_out, s_back,
):
    dp = lax.axis_index("dp")
    xh = lax.axis_index("mp")
    c = lax.rem(dp, 2)
    xl = lax.rem(dp // 2, 2)
    y = lax.rem(dp // 4, 4)
    z = dp // 16
    x = xh * 2 + xl
    p_me = y * 2 + xl
    fetches = c == xh

    def dev(dz=0, dy=0, dx=0, dc=0):
        x_ = step(x, dx, 4)
        return (((step(z, dz, 8) * 4 + step(y, dy, 4)) * 2 + lax.rem(x_, 2)) * 2 + step(c, dc, 2), x_ // 2)

    def step(v, k, n):
        k = k % n
        return v if k == 0 else lax.rem(v + k, n)

    neighbour = (((z * 4 + y) * 2 + (1 - xl)) * 2 + c, xh)

    slots = {}

    def copy(key, src, dst, to):
        n = slots.setdefault(key, len(slots))
        return pltpu.make_async_remote_copy(
            src_ref=src, dst_ref=dst, send_sem=s_out.at[n], recv_sem=s_back.at[n],
            device_id=to, device_id_type=MESH,
        )

    sent = []

    def send(key, src, dst, to):
        one = copy(key, src, dst, to)
        one.start()
        sent.append(one)

    def arrived(key, dst):
        copy(key, dst, dst, dev(dc=1)).wait_recv()

    depth = 512
    parts = [slice(k * depth, (k + 1) * depth) for k in range(2048 // depth)]
    loads = []
    for n, part in enumerate(parts):
        loads.append(pltpu.make_async_copy(h_hbm.at[:, part], h_ref.at[:, part], s_in.at[2 * n]))
        loads.append(pltpu.make_async_copy(w_hbm.at[part, :], w_ref.at[part, :], s_in.at[2 * n + 1]))
    loads.append(pltpu.make_async_copy(perm_hbm, perm_ref, s_in.at[2 * len(parts)]))
    for load in loads:
        load.start()

    barrier = pltpu.get_barrier_semaphore()
    peers = [dev(dz=kz, dc=kc) for kz, kc in COLUMN] + [dev(dy=ky, dx=kx) for ky, kx in PLANE]
    peers += [dev(dx=1, dc=1), dev(dx=3, dc=1)]
    for peer in peers:
        pl.semaphore_signal(barrier, inc=1, device_id=peer, device_id_type=MESH)

    total = None
    for n, part in enumerate(parts):
        loads[2 * n].wait()
        loads[2 * n + 1].wait()
        product = jnp.dot(h_ref[:, part], w_ref[part, :], preferred_element_type=F32)
        total = product if total is None else total + product
    ei[y, x] = total.astype(BF16)
    loads[-1].wait()

    @pl.when(fetches)
    def _():
        ej[xh, z] = ei[y, x]

    pl.semaphore_wait(barrier, len(peers))

    def half_rows(ref, *at):
        return [ref.at[(*at, slice(0, H))], ref.at[(*at, slice(H, R))]]

    own = half_rows(ei, y, x)
    for k, i in ((2, 0), (2, 1), (1, 0), (3, 0), (1, 1), (3, 1)):
        send(("x", k, i), own[i], own[i], dev(dx=k))
    for k, i in ((1, 1), (3, 1), (2, 1), (1, 0), (3, 0), (2, 0)):
        send(("y", k, i), own[i], own[i], dev(dy=k))

    def along_z(half, f, i):
        piece = half_rows(ej, f, z)[i]
        for k in (2, 6, 1, 7):
            copy(("z", half, k, i), piece, piece, dev(dz=k)).start()

    def hand(half, f, k):
        piece = ej.at[f, step(z, -k, 8)]
        copy(("c", half, k), piece, piece, dev(dc=1)).start()

    @pl.when(fetches)
    def _():
        along_z(0, xh, 0)
        along_z(0, xh, 1)
        hand(0, xh, 0)

    first = z < 4
    lanes = lax.broadcasted_iota(jnp.int32, (1, R), 1)
    b_row = []
    for k in ORDER:
        zz = step(z, -k, 8)
        jglob = (((zz * 4 + y) * 2 + xl) * 2 + xh) * R + lanes
        pair = perm_ref[pl.ds(lax.rem(zz, 4) * 16 + y * 4 + xl * 2 + xh, 1), :] + ROWS // 2
        b_row.append(jnp.where(first, jglob, jnp.where(zz < 4, pair, -1)).astype(F32))
    b_row = jnp.concatenate(b_row, axis=1)
    for p in range(8):
        mine = (z * 16 + p * 2 + c) * R + lanes
        pair = perm_ref[pl.ds(lax.rem(z, 4) * 16 + p * 2 + c, 1), :] + ROWS // 2
        a_col = to_columns(jnp.where(first, pair, mine).astype(F32))
        mark[p * R:(p + 1) * R, :] = jnp.where(jnp.concatenate([a_col] * 8, axis=1) == b_row, -2.0, 0.0)

    def on_from_x(k):
        part = half_rows(ei, y, step(x, -k, 4))[0]
        arrived(("x", k, 0), part)
        for ky in (2, 1, 3):
            send(("xy", k, ky), part, part, dev(dy=ky))

    def on_from_y(k):
        part = half_rows(ei, step(y, -k, 4), x)[1]
        arrived(("y", k, 1), part)
        for kx in (2, 1, 3):
            send(("yx", k, kx), part, part, dev(dx=kx))

    across = step(x, 2, 4)
    on_from_x(2)

    @pl.when(fetches)
    def _():
        ej[1 - xh, z, 0:H] = ei[y, across, 0:H]
        along_z(1, 1 - xh, 0)

    arrived(("x", 2, 1), half_rows(ei, y, across)[1])

    @pl.when(fetches)
    def _():
        ej[1 - xh, z, H:R] = ei[y, across, H:R]
        along_z(1, 1 - xh, 1)
        hand(1, 1 - xh, 0)

    on_from_x(1)
    on_from_x(3)
    on_from_y(1)
    on_from_y(3)
    on_from_y(2)

    def from_z(half, f, k, i):
        part = half_rows(ej, f, step(z, -k, 8))[i]
        arrived(("z", half, k, i), part)
        if k == 2:
            if i == 0:
                copy(("z", half, 4, 0), part, part, dev(dz=2)).start()
            copy(("z", half, 3, i), part, part, dev(dz=1)).start()
        if k == 6:
            if i == 1:
                copy(("z", half, 4, 1), part, part, dev(dz=-2)).start()
            copy(("z", half, 5, i), part, part, dev(dz=-1)).start()

    @pl.when(fetches)
    def _():
        for half, f in ((0, xh), (1, 1 - xh)):
            for k, i in ((2, 0), (6, 1), (2, 1), (6, 0)):
                from_z(half, f, k, i)
            hand(half, f, 2)
            hand(half, f, 6)
            for k in (1, 7):
                from_z(half, f, k, 0)
                from_z(half, f, k, 1)
                hand(half, f, k)

    def unit(dst, rows, e0, e1):
        e0 = e0.astype(F32)
        e1 = e1.astype(F32)
        inv = inverse_norm(e0, e1)
        dst[0, rows, :] = (e0 * inv).astype(BF16)
        dst[1, rows, :] = (e1 * inv).astype(BF16)

    def unit_columns(slots_):
        for slot in slots_:
            zz = step(z, -ORDER[slot], 8)
            unit(uj, slice(slot * R, (slot + 1) * R), ej[0, zz], ej[1, zz])

    def handed(slots_):
        for slot in slots_:
            for half, f in ((0, xh), (1, 1 - xh)):
                arrived(("c", half, ORDER[slot]), ej.at[f, step(z, -ORDER[slot], 8)])

    own_row = y * 4 + x
    own_col = z * 2 + c
    rowmsg[own_row] = jnp.zeros((16, R), F32)

    def scores(first_slot, last_slot, ky, so_far):
        y_from = step(y, -ky, 4)
        rows = pl.ds(pl.multiple_of(y_from * 256, 256), 256)
        cols = slice(first_slot * R, last_slot * R)
        s = nt(ui[0, rows, :], uj[0, cols, :]) + nt(ui[1, rows, :], uj[1, cols, :])
        hit = jnp.sum(s * mark[rows, cols], axis=0, keepdims=True)
        e = jnp.exp2(EXP2_SCALE * s - EXP2_SCALE)
        if first_slot == 0 and ky == 0:
            at = lax.broadcasted_iota(jnp.int32, (256, R), 0) - lax.broadcasted_iota(jnp.int32, (256, R), 1)
            diagonal = at == jnp.where(fetches, xl * R, -ROWS)
            e = jnp.concatenate([jnp.where(diagonal, 0.0, e[:, 0:R]), e[:, R:]], axis=1)
        sim[rows, cols] = e
        part = e[:, 0:R]
        for t in range(1, last_slot - first_slot):
            part = part + e[:, t * R:(t + 1) * R]
        rowacc[rows, :] = part if first_slot == 0 else rowacc[rows, :] + part
        total = jnp.sum(e, axis=0, keepdims=True)
        return (total, hit) if so_far is None else (so_far[0] + total, so_far[1] + hit)

    def hand_in(first_slot, last_slot, so_far):
        sums, hits = so_far
        line = hits[:, 0:R]
        for slot in range(first_slot, last_slot):
            t = slot - first_slot
            colmsg[own_col, pl.ds(step(z, -ORDER[slot], 8), 1), :] = sums[:, t * R:(t + 1) * R]
            if t:
                line = line + hits[:, t * R:(t + 1) * R]
        rowmsg[own_row, 8:9, :] = rowmsg[own_row, 8:9, :] - 0.5 * line

    @pl.when(jnp.logical_not(fetches))
    def _():
        handed(range(5))

    unit_columns(range(5))
    so_far = None
    for ky in (0, 1, 3, 2):
        y_from = step(y, -ky, 4)
        if ky == 0:
            for k in (1, 3):
                arrived(("x", k, 1), half_rows(ei, y, step(x, -k, 4))[1])
        else:
            arrived(("y", ky, 0), half_rows(ei, y_from, x)[0])
            for k in (1, 3, 2):
                arrived(("xy", k, ky), half_rows(ei, y_from, step(x, -k, 4))[0])
                arrived(("yx", ky, k), half_rows(ei, y_from, step(x, -k, 4))[1])
        for half in range(2):
            rows = pl.ds(pl.multiple_of(y_from * 256 + half * R, R), R)
            unit(ui, rows, ei[y_from, half], ei[y_from, 2 + half])
        so_far = scores(0, 5, ky, so_far)
    hand_in(0, 5, so_far)

    def hidden_rows(kc, x_):
        return pl.ds(pl.multiple_of((kc * 2 + x_) * R, R), R)

    def half_of(core):
        return pl.ds(pl.multiple_of(core * 1024, 1024), 1024)

    def send_hidden(kc):
        for n, dx in ((0, 1), (1, 3)):
            cols = pl.ds(pl.multiple_of(step(c, kc, 2) * 1024 + n * 512, 512), 512)
            there = hq.at[hidden_rows(kc, xl), n * 512:(n + 1) * 512]
            send(("hx", n, kc), h_ref.at[:, cols], there, dev(dx=dx, dc=kc))

    hq[hidden_rows(0, xl), :] = h_ref[:, half_of(c)]
    send(("h",), h_ref.at[:, half_of(1 - c)], hq.at[hidden_rows(1, xl), :], dev(dc=1))
    send_hidden(0)

    @pl.when(fetches)
    def _():
        for half, f in ((0, xh), (1, 1 - xh)):
            for k in (3, 5, 4):
                from_z(half, f, k, 0)
                from_z(half, f, k, 1)
                hand(half, f, k)

    @pl.when(jnp.logical_not(fetches))
    def _():
        handed(range(5, 8))

    unit_columns(range(5, 8))
    so_far = None
    for ky in (0, 1, 3, 2):
        so_far = scores(5, 8, ky, so_far)
    hand_in(5, 8, so_far)
    for p in range(8):
        rowmsg[own_row, p:p + 1, :] = to_rows(rowacc[p * R:(p + 1) * R, :])

    for kz, kc in COLUMN:
        send(("col", kz, kc), colmsg.at[own_col], colmsg.at[own_col], dev(dz=kz, dc=kc))
    for ky, kx in PLANE:
        send(("row", ky, kx), rowmsg.at[own_row], rowmsg.at[own_row], dev(dy=ky, dx=kx))
    send_hidden(1)
    for ky, kx in PLANE:
        arrived(("row", ky, kx), rowmsg.at[step(y, -ky, 4) * 4 + step(x, -kx, 4)])
    for kz, kc in COLUMN:
        arrived(("col", kz, kc), colmsg.at[step(z, -kz, 8) * 2 + step(c, kc, 2)])

    all_rows = rowmsg[0]
    all_cols = colmsg[0]
    for n in range(1, 16):
        all_rows = all_rows + rowmsg[n]
        all_cols = all_cols + colmsg[n]
    row_total = all_rows[0:8]
    hit_total = all_rows[8:9]
    cost = jnp.sum(jnp.log(row_total), axis=0, keepdims=True) - SHARPNESS * (hit_total - 8.0)
    losses[own_col] = jnp.broadcast_to(cost, (8, R))

    inv_rows = 1.0 / row_total
    inv_cols = 1.0 / all_cols
    isum_cols[...] = inv_cols
    tsum[...] = jnp.concatenate([isum_cols[pl.ds(step(z, -k, 8), 1), :] for k in ORDER], axis=1)
    for p in range(8):
        factor[p] = to_columns(inv_rows[p:p + 1])
    def send_b(ky, kx):
        y_to, x_to = step(y, ky, 4), step(x, kx, 4)
        send(("rb", ky, kx), sb.at[y_to, x_to], rb.at[ky, x_to], dev(dy=ky))

    for ky in (2, 1, 3, 0):
        y_to = step(y, ky, 4)
        rows = pl.ds(pl.multiple_of(y_to * 256, 256), 256)
        wide = jnp.concatenate([factor[pl.ds(y_to * 2, 2)].reshape(256, R)] * 8, axis=1)
        weights = (sim[rows, :] * (wide + tsum[...]) + mark[rows, :]).astype(BF16)
        acc = None
        for f in range(2):
            g = jnp.dot(weights, uj[f], preferred_element_type=F32)
            for q in range(2):
                sa[2 * f + q, y_to] = g[0:R, q * R:(q + 1) * R].astype(BF16)
                sb[y_to, 2 * f + q] = g[R:2 * R, q * R:(q + 1) * R].astype(BF16)
            t = g * ui[f, rows, :].astype(F32)
            t = t[:, 0:R] + t[:, R:]
            acc = t if acc is None else acc + t
        for kx in (2, 1, 3):
            send(("ra", kx, ky), sa.at[step(x, kx, 4), y_to], ra.at[kx, y_to], dev(dx=kx))
        if ky:
            send_b(ky, 2)
        for half in range(2):
            v = to_rows(acc[half * R:(half + 1) * R])
            inner_out[y_to, half:half + 1, :] = v
        for kx in (2, 1, 3, 0):
            if ky or kx:
                send(
                    ("in", ky, kx), inner_out.at[y_to], inner_in.at[ky * 4 + kx],
                    dev(dy=ky, dx=kx),
                )
    for kx in (1, 3, 0):
        for ky in (2, 1, 3):
            send_b(ky, kx)
    for kz, kc in COLUMN:
        send(("loss", kz, kc), losses.at[own_col], losses.at[own_col], dev(dz=kz, dc=kc))

    def total_a(ky):
        y_to = step(y, ky, 4)
        g = sa[x, y_to].astype(F32)
        for kx in (1, 2, 3):
            arrived(("ra", kx, ky), ra.at[kx, y_to])
            g = g + ra[kx, y_to].astype(F32)
        return g

    def total_b(kx):
        x_to = step(x, kx, 4)
        g = sb[y, x_to].astype(F32)
        for ky in (1, 2, 3):
            arrived(("rb", ky, kx), rb.at[ky, x_to])
            g = g + rb[ky, x_to].astype(F32)
        return g

    for k in (2, 1, 3):
        sa2[k] = total_a(k).astype(BF16)
        send(("ra2", k), sa2.at[k], ra2.at[k], dev(dy=k))
        sb2[k] = total_b(k).astype(BF16)
        send(("rb2", k), sb2.at[k], rb2.at[k], dev(dx=k))
    g_a = total_a(0)
    g_b = total_b(0)
    inner = inner_out[y]
    for ky, kx in PLANE:
        arrived(("in", ky, kx), inner_in.at[ky * 4 + kx])
        inner = inner + inner_in[ky * 4 + kx]
    for k in (2, 1, 3):
        arrived(("ra2", k), ra2.at[k])
        arrived(("rb2", k), rb2.at[k])
        g_a = g_a + ra2[k].astype(F32)
        g_b = g_b + rb2[k].astype(F32)
    quarter = pl.ds(pl.multiple_of(xl * R, R), R)
    for half, g in ((0, g_a), (1, g_b)):
        inv = inverse_norm(ei[y, half].astype(F32), ei[y, 2 + half].astype(F32))
        some_unit = ei[y, 2 * xh + half, :, quarter].astype(F32) * inv
        grad = (SHARPNESS * inv) * (g - some_unit * to_columns(inner[half:half + 1]))
        g4[half * R:(half + 1) * R, :] = grad.astype(BF16)
        gout[half] = grad

    def tn(a, b):
        return lax.dot_general(a, b, (((0,), (0,)), ((), ())), preferred_element_type=F32)

    send(("g",), g4.at[0:2 * R, :], g4.at[2 * R:4 * R, :], dev(dc=1))
    send(("ge",), gout.at[1 - xl], gemb_ref.at[:, quarter], neighbour)
    gemb_ref[:, quarter] = gout[xl]
    arrived(("h",), hq.at[hidden_rows(1, xl), :])
    for kc in range(2):
        for n in range(2):
            arrived(("hx", n, kc), hq.at[hidden_rows(kc, 1 - xl), n * 512:(n + 1) * 512])
    near = tn(hq[0:2 * R, :], g4[0:2 * R, :])
    arrived(("g",), g4.at[2 * R:4 * R, :])
    full = near + tn(hq[2 * R:, :], g4[2 * R:, :])
    gp[...] = full
    gpb[...] = full.astype(BF16)
    def piece_at(kz, ky):
        return pl.ds(pl.multiple_of(step(y, ky, 4) * 256 + step(z, kz, 8) * 32, 32), 32)

    for kz in (4, 3, 5, 2, 6, 1, 7, 0):
        for ky in (2, 1, 3):
            send(("gy", ky, kz), gpb.at[piece_at(kz, ky), :], ry.at[ky, kz], dev(dy=ky))
    for kz in (4, 3, 5, 2, 6, 1, 7, 0):
        piece = gp[piece_at(kz, 0), :]
        for ky in (1, 3, 2):
            arrived(("gy", ky, kz), ry.at[ky, kz])
            piece = piece + ry[ky, kz].astype(F32)
        if kz:
            rzb[kz] = piece.astype(BF16)
            send(("gz", kz), rzb.at[kz], rz.at[kz], dev(dz=kz))
    for kz in (1, 7, 2, 6, 3, 5, 4):
        arrived(("gz", kz), rz.at[kz])
        piece = piece + rz[kz].astype(F32)

    def place(x_, c_, y_, z_=None):
        rows = slice(None) if z_ is None else pl.ds(pl.multiple_of(z_ * 32, 32), 32)
        return gproj_ref.at[c_, y_, rows, pl.ds(pl.multiple_of(x_ * R, R), R)]

    gproj_ref[c, y, pl.ds(pl.multiple_of(z * 32, 32), 32), quarter] = piece.astype(BF16)
    mine = place(xl, c, y, z)
    for kz in (4, 3, 5, 2, 6, 1, 7):
        send(("az", kz), mine, mine, dev(dz=kz))
    for kz in ORDER:
        there = place(xl, c, y, step(z, -kz, 8))
        if kz:
            arrived(("az", kz), there)
        for ky in (2, 1, 3):
            send(("ay", ky, kz), there, there, dev(dy=ky))
        send(("ax", 0, kz), there, there, neighbour)

    mine = place(xl, c, y)
    send(("ac", 0, 0), mine, mine, dev(dc=1))
    for ky in (1, 3, 2):
        y_from = step(y, -ky, 4)
        for kz in ORDER:
            arrived(("ay", ky, kz), place(xl, c, y_from, step(z, -kz, 8)))
        there = place(xl, c, y_from)
        send(("ax", ky), there, there, neighbour)
        send(("ac", 0, ky), there, there, dev(dc=1))
    for kz in ORDER:
        arrived(("ax", 0, kz), place(1 - xl, c, y, step(z, -kz, 8)))
    for ky in (0, 1, 3, 2):
        there = place(1 - xl, c, step(y, -ky, 4))
        if ky:
            arrived(("ax", ky), there)
        send(("ac", 1, ky), there, there, dev(dc=1))

    for kz, kc in COLUMN:
        arrived(("loss", kz, kc), losses.at[step(z, -kz, 8) * 2 + step(c, kc, 2)])
    cost = losses[0]
    for n in range(1, 16):
        cost = cost + losses[n]
    loss_ref[...] = jnp.broadcast_to(jnp.sum(cost, axis=1, keepdims=True) * (1.0 / ROWS), (8, R))

    for ky in (0, 1, 3, 2):
        y_from = step(y, -ky, 4)
        arrived(("ac", 0, ky), place(xl, 1 - c, y_from))
        arrived(("ac", 1, ky), place(1 - xl, 1 - c, y_from))
    arrived(("ge",), gemb_ref.at[:, pl.ds(pl.multiple_of((1 - xl) * R, R), R)])
    for one in sent:
        one.wait_send()

    @pl.when(fetches)
    def _():
        whole = ej.at[0, 0]
        part = ej.at[0, 0, 0:H]
        for half in range(2):
            for k in range(1, 8):
                for i in range(2):
                    copy(("z", half, k, i), part, part, dev(dc=1)).wait_send()
            for k in range(8):
                copy(("c", half, k), whole, whole, dev(dc=1)).wait_send()


def finish(loss_in, gemb_in, gproj_in, loss_out, gemb_out, gproj_out, wide, sems):
    copies = [pltpu.make_async_copy(gemb_in, gemb_out, sems.at[8])]
    copies[0].start()
    for n in range(8):
        rows = slice(n * 256, (n + 1) * 256)
        wide[rows, :] = gproj_in[rows, :].astype(F32)
        copies.append(pltpu.make_async_copy(wide.at[rows, :], gproj_out.at[rows, :], sems.at[n]))
        copies[-1].start()
    loss_out[...] = loss_in[0:1, 0:1]
    for one in copies:
        one.wait()


def per_device(head_hidden, proj_weight, pair_perm):
    vmem = pltpu.VMEM
    hbm = pl.BlockSpec(memory_space=pltpu.HBM)
    space = pl.BlockSpec(memory_space=pltpu.VMEM)
    loss, grad_emb, grad_proj = pl.pallas_call(
        kernel,
        out_shape=(
            jax.ShapeDtypeStruct((8, R), F32),
            jax.ShapeDtypeStruct((R, 256), F32),
            jax.ShapeDtypeStruct((2, 4, 256, 256), BF16),
        ),
        in_specs=[hbm] * 3,
        out_specs=[space] * 3,
        scratch_shapes=[
            vmem((R, 2048), BF16),
            vmem((2048, 256), BF16),
            vmem((64, R), jnp.int32),
            vmem((4, 4, R, 256), BF16),
            vmem((2, 8, R, 256), BF16),
            vmem((2, 1024, 256), BF16),
            vmem((2, 1024, 256), BF16),
            vmem((1024, 1024), F32),
            vmem((1024, 1024), F32),
            vmem((16, 16, R), F32),
            vmem((16, 8, R), F32),
            vmem((16, 8, R), F32),
            vmem((1, 1024), F32),
            vmem((8, R), F32),
            vmem((1024, R), F32),
            vmem((8, R, R), F32),
            vmem((4, 4, R, R), BF16),
            vmem((4, 4, R, R), BF16),
            vmem((4, 4, R, R), BF16),
            vmem((4, 4, R, R), BF16),
            vmem((4, R, R), BF16),
            vmem((4, R, R), BF16),
            vmem((4, R, R), BF16),
            vmem((4, R, R), BF16),
            vmem((4, 8, R), F32),
            vmem((16, 8, R), F32),
            vmem((2, R, R), F32),
            vmem((512, R), BF16),
            vmem((512, 1024), BF16),
            vmem((1024, R), F32),
            vmem((1024, R), BF16),
            vmem((4, 8, 32, R), BF16),
            vmem((8, 32, R), BF16),
            vmem((8, 32, R), BF16),
            pltpu.SemaphoreType.DMA((9,)),
            pltpu.SemaphoreType.DMA((COPIES,)),
            pltpu.SemaphoreType.DMA((COPIES,)),
        ],
        compiler_params=pltpu.CompilerParams(
            collective_id=0, has_side_effects=True, vmem_limit_bytes=40 * 1024 * 1024
        ),
    )(*[pltpu.with_memory_space_constraint(v, pltpu.HBM) for v in (head_hidden, proj_weight, pair_perm.reshape(64, R))])
    hbm = pl.BlockSpec(memory_space=pl.ANY)
    loss, grad_emb, grad_proj = pl.pallas_call(
        finish,
        out_shape=(
            jax.ShapeDtypeStruct((1, 1), F32),
            jax.ShapeDtypeStruct((R, 256), F32),
            jax.ShapeDtypeStruct((2048, 256), F32),
        ),
        in_specs=[space] * 3,
        out_specs=[space, hbm, hbm],
        scratch_shapes=[vmem((2048, 256), F32), pltpu.SemaphoreType.DMA((9,))],
        compiler_params=pltpu.CompilerParams(vmem_limit_bytes=16 * 1024 * 1024),
    )(loss, grad_emb, grad_proj.reshape(2048, 256))
    return loss[0, 0], grad_emb, grad_proj


def solution(mesh):
    placed = (P("dp", None), P(None, "mp"), P())
    return jax.shard_map(
        per_device,
        mesh=mesh,
        in_specs=placed,
        out_specs=(P(), P("dp", "mp"), P(None, "mp")),
        check_vma=False,
    )
```

```python
import jax
import jax.numpy as jnp
from jax import lax
from jax.experimental import pallas as pl
from jax.experimental.pallas import tpu as pltpu
from jax.sharding import PartitionSpec as P

MESH = pl.DeviceIdType.MESH
F32 = jnp.float32
BF16 = jnp.bfloat16
SHARPNESS = 10.0
EXP2_SCALE = SHARPNESS * 1.4426950408889634
ORDER = (0, 1, 7, 2, 6, 3, 5, 4)
R = 128
H = 64
ROWS = 16384
COPIES = 320


def far(k, n):
    return min(k, n - k)


PLANE = sorted([(ky, kx) for ky in range(4) for kx in range(4)][1:], key=lambda k: -far(k[0], 4) - far(k[1], 4))
COLUMN = sorted([(kz, kc) for kz in range(8) for kc in range(2)][1:], key=lambda k: -far(k[0], 8))


def nt(a, b):
    return lax.dot_general(a, b, (((1,), (1,)), ((), ())), preferred_element_type=F32)


def to_rows(x):
    return jnp.sum(x.T, axis=0, keepdims=True)


def to_columns(row):
    return jnp.broadcast_to(row, (R, R)).T


def inverse_norm(e0, e1):
    return lax.rsqrt(jnp.sum(e0 * e0 + e1 * e1, axis=1, keepdims=True) + 1e-06)


def kernel(
    h_hbm, w_hbm, perm_hbm,
    loss_ref, gemb_ref, gproj_ref,
    h_ref, w_ref, perm_ref, ei, ej, ui, uj, sim, mark, rowmsg, colmsg, losses, tsum, isum_cols, rowacc, factor,
    sa, sb, ra, rb, sa2, sb2, ra2, rb2, inner_out, inner_in,
    gout, g4, hq, gp, gpb, ry, rz, rzb, s_in, s_out, s_back,
):
    dp = lax.axis_index("dp")
    xh = lax.axis_index("mp")
    c = lax.rem(dp, 2)
    xl = lax.rem(dp // 2, 2)
    y = lax.rem(dp // 4, 4)
    z = dp // 16
    x = xh * 2 + xl
    p_me = y * 2 + xl
    fetches = c == xh

    def dev(dz=0, dy=0, dx=0, dc=0):
        x_ = step(x, dx, 4)
        return (((step(z, dz, 8) * 4 + step(y, dy, 4)) * 2 + lax.rem(x_, 2)) * 2 + step(c, dc, 2), x_ // 2)

    def step(v, k, n):
        k = k % n
        return v if k == 0 else lax.rem(v + k, n)

    def pair_dev(kz):
        return (((step(z, kz, 8) * 4 + y) * 2 + (1 - xl)) * 2 + c, xh)

    neighbour = pair_dev(0)

    slots = {}

    def copy(key, src, dst, to):
        n = slots.setdefault(key, len(slots))
        return pltpu.make_async_remote_copy(
            src_ref=src, dst_ref=dst, send_sem=s_out.at[n], recv_sem=s_back.at[n],
            device_id=to, device_id_type=MESH,
        )

    sent = []

    def send(key, src, dst, to):
        one = copy(key, src, dst, to)
        one.start()
        sent.append(one)

    def flush(start, stop):
        for one in sent[start:stop]:
            one.wait_send()
        del sent[start:stop]

    def arrived(key, dst):
        copy(key, dst, dst, dev(dc=1)).wait_recv()

    depth = 512
    parts = [slice(k * depth, (k + 1) * depth) for k in range(2048 // depth)]
    loads = []
    for n, part in enumerate(parts):
        loads.append(pltpu.make_async_copy(h_hbm.at[:, part], h_ref.at[:, part], s_in.at[2 * n]))
        loads.append(pltpu.make_async_copy(w_hbm.at[part, :], w_ref.at[part, :], s_in.at[2 * n + 1]))
    loads.append(pltpu.make_async_copy(perm_hbm, perm_ref, s_in.at[2 * len(parts)]))
    for load in loads:
        load.start()

    barrier = pltpu.get_barrier_semaphore()
    peers = [dev(dx=k) for k in (2, 1, 3)] + [dev(dy=k) for k in (2, 1, 3)] + [dev(dz=k) for k in (2, 6, 1, 7)] + [dev(dc=1)]
    for peer in peers:
        pl.semaphore_signal(barrier, inc=1, device_id=peer, device_id_type=MESH)

    total = None
    for n, part in enumerate(parts):
        loads[2 * n].wait()
        loads[2 * n + 1].wait()
        product = jnp.dot(h_ref[:, part], w_ref[part, :], preferred_element_type=F32)
        total = product if total is None else total + product
    ei[y, x] = total.astype(BF16)
    loads[-1].wait()

    @pl.when(fetches)
    def _():
        ej[xh, z] = ei[y, x]

    pl.semaphore_wait(barrier, len(peers))

    def half_rows(ref, *at):
        return [ref.at[(*at, slice(0, H))], ref.at[(*at, slice(H, R))]]

    own = half_rows(ei, y, x)
    for k, i in ((2, 0), (2, 1), (1, 0), (3, 0), (1, 1), (3, 1)):
        send(("x", k, i), own[i], own[i], dev(dx=k))
    for k, i in ((1, 1), (3, 1), (2, 1), (1, 0), (3, 0), (2, 0)):
        send(("y", k, i), own[i], own[i], dev(dy=k))

    def along_z(half, f, i):
        piece = half_rows(ej, f, z)[i]
        for k in (2, 6, 1, 7):
            copy(("z", half, k, i), piece, piece, dev(dz=k)).start()

    def hand(half, f, k):
        piece = ej.at[f, step(z, -k, 8)]
        copy(("c", half, k), piece, piece, dev(dc=1)).start()

    @pl.when(fetches)
    def _():
        along_z(0, xh, 0)
        along_z(0, xh, 1)
        hand(0, xh, 0)

    first = z < 4
    lanes = lax.broadcasted_iota(jnp.int32, (1, R), 1)
    b_row = []
    for k in ORDER:
        zz = step(z, -k, 8)
        jglob = (((zz * 4 + y) * 2 + xl) * 2 + xh) * R + lanes
        pair = perm_ref[pl.ds(lax.rem(zz, 4) * 16 + y * 4 + xl * 2 + xh, 1), :] + ROWS // 2
        b_row.append(jnp.where(first, jglob, jnp.where(zz < 4, pair, -1)).astype(F32))
    b_row = jnp.concatenate(b_row, axis=1)
    for p in range(8):
        mine = (z * 16 + p * 2 + c) * R + lanes
        pair = perm_ref[pl.ds(lax.rem(z, 4) * 16 + p * 2 + c, 1), :] + ROWS // 2
        a_col = to_columns(jnp.where(first, pair, mine).astype(F32))
        mark[p * R:(p + 1) * R, :] = jnp.where(jnp.concatenate([a_col] * 8, axis=1) == b_row, -2.0, 0.0)

    def on_from_x(k):
        part = half_rows(ei, y, step(x, -k, 4))[0]
        arrived(("x", k, 0), part)
        for ky in (2, 1, 3):
            send(("xy", k, ky), part, part, dev(dy=ky))

    def on_from_y(k):
        part = half_rows(ei, step(y, -k, 4), x)[1]
        arrived(("y", k, 1), part)
        for kx in (2, 1, 3):
            send(("yx", k, kx), part, part, dev(dx=kx))

    across = step(x, 2, 4)
    on_from_x(2)

    @pl.when(fetches)
    def _():
        ej[1 - xh, z, 0:H] = ei[y, across, 0:H]
        along_z(1, 1 - xh, 0)

    arrived(("x", 2, 1), half_rows(ei, y, across)[1])

    @pl.when(fetches)
    def _():
        ej[1 - xh, z, H:R] = ei[y, across, H:R]
        along_z(1, 1 - xh, 1)
        hand(1, 1 - xh, 0)

    on_from_x(1)
    on_from_x(3)
    on_from_y(1)
    on_from_y(3)
    on_from_y(2)

    def from_z(half, f, k, i):
        part = half_rows(ej, f, step(z, -k, 8))[i]
        arrived(("z", half, k, i), part)
        if k == 2:
            if i == 0:
                copy(("z", half, 4, 0), part, part, dev(dz=2)).start()
            copy(("z", half, 3, i), part, part, dev(dz=1)).start()
        if k == 6:
            if i == 1:
                copy(("z", half, 4, 1), part, part, dev(dz=-2)).start()
            copy(("z", half, 5, i), part, part, dev(dz=-1)).start()

    @pl.when(fetches)
    def _():
        for half, f in ((0, xh), (1, 1 - xh)):
            for k, i in ((2, 0), (6, 1), (2, 1), (6, 0)):
                from_z(half, f, k, i)
            hand(half, f, 2)
            hand(half, f, 6)
            for k in (1, 7):
                from_z(half, f, k, 0)
                from_z(half, f, k, 1)
                hand(half, f, k)

    def unit(dst, rows, e0, e1):
        e0 = e0.astype(F32)
        e1 = e1.astype(F32)
        inv = inverse_norm(e0, e1)
        dst[0, rows, :] = (e0 * inv).astype(BF16)
        dst[1, rows, :] = (e1 * inv).astype(BF16)

    def unit_columns(slots_):
        for slot in slots_:
            zz = step(z, -ORDER[slot], 8)
            unit(uj, slice(slot * R, (slot + 1) * R), ej[0, zz], ej[1, zz])

    def handed(slots_):
        for slot in slots_:
            for half, f in ((0, xh), (1, 1 - xh)):
                arrived(("c", half, ORDER[slot]), ej.at[f, step(z, -ORDER[slot], 8)])

    own_row = y * 4 + x
    own_col = z * 2 + c
    rowmsg[own_row] = jnp.zeros((16, R), F32)

    def scores(first_slot, last_slot, ky, so_far):
        y_from = step(y, -ky, 4)
        rows = pl.ds(pl.multiple_of(y_from * 256, 256), 256)
        cols = slice(first_slot * R, last_slot * R)
        s = nt(ui[0, rows, :], uj[0, cols, :]) + nt(ui[1, rows, :], uj[1, cols, :])
        hit = jnp.sum(s * mark[rows, cols], axis=0, keepdims=True)
        e = jnp.exp2(EXP2_SCALE * s - EXP2_SCALE)
        if first_slot == 0 and ky == 0:
            at = lax.broadcasted_iota(jnp.int32, (256, R), 0) - lax.broadcasted_iota(jnp.int32, (256, R), 1)
            diagonal = at == jnp.where(fetches, xl * R, -ROWS)
            e = jnp.concatenate([jnp.where(diagonal, 0.0, e[:, 0:R]), e[:, R:]], axis=1)
        sim[rows, cols] = e
        part = e[:, 0:R]
        for t in range(1, last_slot - first_slot):
            part = part + e[:, t * R:(t + 1) * R]
        rowacc[rows, :] = part if first_slot == 0 else rowacc[rows, :] + part
        total = jnp.sum(e, axis=0, keepdims=True)
        return (total, hit) if so_far is None else (so_far[0] + total, so_far[1] + hit)

    def hand_in(first_slot, last_slot, so_far):
        sums, hits = so_far
        line = hits[:, 0:R]
        for slot in range(first_slot, last_slot):
            t = slot - first_slot
            colmsg[own_col, pl.ds(step(z, -ORDER[slot], 8), 1), :] = sums[:, t * R:(t + 1) * R]
            if t:
                line = line + hits[:, t * R:(t + 1) * R]
        rowmsg[own_row, 8:9, :] = rowmsg[own_row, 8:9, :] - 0.5 * line

    @pl.when(jnp.logical_not(fetches))
    def _():
        handed(range(5))

    unit_columns(range(5))
    so_far = None
    for ky in (0, 1, 3, 2):
        y_from = step(y, -ky, 4)
        if ky == 0:
            for k in (1, 3):
                arrived(("x", k, 1), half_rows(ei, y, step(x, -k, 4))[1])
        else:
            arrived(("y", ky, 0), half_rows(ei, y_from, x)[0])
            for k in (1, 3, 2):
                arrived(("xy", k, ky), half_rows(ei, y_from, step(x, -k, 4))[0])
                arrived(("yx", ky, k), half_rows(ei, y_from, step(x, -k, 4))[1])
        for half in range(2):
            rows = pl.ds(pl.multiple_of(y_from * 256 + half * R, R), R)
            unit(ui, rows, ei[y_from, half], ei[y_from, 2 + half])
        so_far = scores(0, 5, ky, so_far)
    hand_in(0, 5, so_far)

    def hidden_rows(kc, x_):
        return pl.ds(pl.multiple_of((kc * 2 + x_) * R, R), R)

    def half_of(core):
        return pl.ds(pl.multiple_of(core * 1024, 1024), 1024)

    def send_hidden(kc):
        for n, dx in ((0, 1), (1, 3)):
            cols = pl.ds(pl.multiple_of(step(c, kc, 2) * 1024 + n * 512, 512), 512)
            there = hq.at[hidden_rows(kc, xl), n * 512:(n + 1) * 512]
            send(("hx", n, kc), h_ref.at[:, cols], there, dev(dx=dx, dc=kc))

    hq[hidden_rows(0, xl), :] = h_ref[:, half_of(c)]
    send(("h",), h_ref.at[:, half_of(1 - c)], hq.at[hidden_rows(1, xl), :], dev(dc=1))
    send_hidden(0)

    @pl.when(fetches)
    def _():
        for half, f in ((0, xh), (1, 1 - xh)):
            for k in (3, 5, 4):
                from_z(half, f, k, 0)
                from_z(half, f, k, 1)
                hand(half, f, k)

    @pl.when(jnp.logical_not(fetches))
    def _():
        handed(range(5, 8))

    unit_columns(range(5, 8))
    so_far = None
    for ky in (0, 1, 3, 2):
        so_far = scores(5, 8, ky, so_far)
    hand_in(5, 8, so_far)
    for p in range(8):
        rowmsg[own_row, p:p + 1, :] = to_rows(rowacc[p * R:(p + 1) * R, :])

    for kz, kc in COLUMN:
        send(("col", kz, kc), colmsg.at[own_col], colmsg.at[own_col], dev(dz=kz, dc=kc))
    for ky, kx in PLANE:
        send(("row", ky, kx), rowmsg.at[own_row], rowmsg.at[own_row], dev(dy=ky, dx=kx))
    send_hidden(1)
    for ky, kx in PLANE:
        arrived(("row", ky, kx), rowmsg.at[step(y, -ky, 4) * 4 + step(x, -kx, 4)])
    for kz, kc in COLUMN:
        arrived(("col", kz, kc), colmsg.at[step(z, -kz, 8) * 2 + step(c, kc, 2)])

    all_rows = rowmsg[0]
    all_cols = colmsg[0]
    for n in range(1, 16):
        all_rows = all_rows + rowmsg[n]
        all_cols = all_cols + colmsg[n]
    row_total = all_rows[0:8]
    hit_total = all_rows[8:9]
    cost = jnp.sum(jnp.log(row_total), axis=0, keepdims=True) - SHARPNESS * (hit_total - 8.0)
    losses[own_col] = jnp.broadcast_to(cost, (8, R))

    inv_rows = 1.0 / row_total
    inv_cols = 1.0 / all_cols
    isum_cols[...] = inv_cols
    tsum[...] = jnp.concatenate([isum_cols[pl.ds(step(z, -k, 8), 1), :] for k in ORDER], axis=1)
    for p in range(8):
        factor[p] = to_columns(inv_rows[p:p + 1])
    def send_b(ky, kx):
        y_to, x_to = step(y, ky, 4), step(x, kx, 4)
        send(("rb", ky, kx), sb.at[y_to, x_to], rb.at[ky, x_to], dev(dy=ky))

    older = len(sent)

    for ky in (2, 1, 3, 0):
        y_to = step(y, ky, 4)
        rows = pl.ds(pl.multiple_of(y_to * 256, 256), 256)
        wide = jnp.concatenate([factor[pl.ds(y_to * 2, 2)].reshape(256, R)] * 8, axis=1)
        weights = (sim[rows, :] * (wide + tsum[...]) + mark[rows, :]).astype(BF16)
        acc = None
        for f in range(2):
            g = jnp.dot(weights, uj[f], preferred_element_type=F32)
            for q in range(2):
                sa[2 * f + q, y_to] = g[0:R, q * R:(q + 1) * R].astype(BF16)
                sb[y_to, 2 * f + q] = g[R:2 * R, q * R:(q + 1) * R].astype(BF16)
            t = g * ui[f, rows, :].astype(F32)
            t = t[:, 0:R] + t[:, R:]
            acc = t if acc is None else acc + t
        for kx in (2, 1, 3):
            send(("ra", kx, ky), sa.at[step(x, kx, 4), y_to], ra.at[kx, y_to], dev(dx=kx))
        if ky:
            send_b(ky, 2)
        for half in range(2):
            v = to_rows(acc[half * R:(half + 1) * R])
            inner_out[y_to, half:half + 1, :] = v
        for kx in (2, 1, 3, 0):
            if ky or kx:
                send(
                    ("in", ky, kx), inner_out.at[y_to], inner_in.at[ky * 4 + kx],
                    dev(dy=ky, dx=kx),
                )
    for kx in (1, 3, 0):
        for ky in (2, 1, 3):
            send_b(ky, kx)
    for kz, kc in COLUMN:
        send(("loss", kz, kc), losses.at[own_col], losses.at[own_col], dev(dz=kz, dc=kc))

    flush(0, older)

    @pl.when(fetches)
    def _():
        whole = ej.at[0, 0]
        part = ej.at[0, 0, 0:H]
        for half in range(2):
            for k in range(1, 8):
                for i in range(2):
                    copy(("z", half, k, i), part, part, dev(dc=1)).wait_send()
            for k in range(8):
                copy(("c", half, k), whole, whole, dev(dc=1)).wait_send()
    def total_a(ky):
        y_to = step(y, ky, 4)
        g = sa[x, y_to].astype(F32)
        for kx in (1, 2, 3):
            arrived(("ra", kx, ky), ra.at[kx, y_to])
            g = g + ra[kx, y_to].astype(F32)
        return g

    def total_b(kx):
        x_to = step(x, kx, 4)
        g = sb[y, x_to].astype(F32)
        for ky in (1, 2, 3):
            arrived(("rb", ky, kx), rb.at[ky, x_to])
            g = g + rb[ky, x_to].astype(F32)
        return g

    for k in (2, 1, 3):
        sa2[k] = total_a(k).astype(BF16)
        send(("ra2", k), sa2.at[k], ra2.at[k], dev(dy=k))
        sb2[k] = total_b(k).astype(BF16)
        send(("rb2", k), sb2.at[k], rb2.at[k], dev(dx=k))
    g_a = total_a(0)
    g_b = total_b(0)
    inner = inner_out[y]
    for ky, kx in PLANE:
        arrived(("in", ky, kx), inner_in.at[ky * 4 + kx])
        inner = inner + inner_in[ky * 4 + kx]
    for k in (2, 1, 3):
        arrived(("ra2", k), ra2.at[k])
        arrived(("rb2", k), rb2.at[k])
        g_a = g_a + ra2[k].astype(F32)
        g_b = g_b + rb2[k].astype(F32)
    quarter = pl.ds(pl.multiple_of(xl * R, R), R)
    for half, g in ((0, g_a), (1, g_b)):
        inv = inverse_norm(ei[y, half].astype(F32), ei[y, 2 + half].astype(F32))
        some_unit = ei[y, 2 * xh + half, :, quarter].astype(F32) * inv
        grad = (SHARPNESS * inv) * (g - some_unit * to_columns(inner[half:half + 1]))
        g4[half * R:(half + 1) * R, :] = grad.astype(BF16)
        gout[half] = grad

    def tn(a, b):
        return lax.dot_general(a, b, (((0,), (0,)), ((), ())), preferred_element_type=F32)

    send(("g",), g4.at[0:2 * R, :], g4.at[2 * R:4 * R, :], dev(dc=1))
    send(("ge",), gout.at[1 - xl], gemb_ref.at[:, quarter], neighbour)
    gemb_ref[:, quarter] = gout[xl]
    arrived(("h",), hq.at[hidden_rows(1, xl), :])
    for kc in range(2):
        for n in range(2):
            arrived(("hx", n, kc), hq.at[hidden_rows(kc, 1 - xl), n * 512:(n + 1) * 512])
    near = tn(hq[0:2 * R, :], g4[0:2 * R, :])
    arrived(("g",), g4.at[2 * R:4 * R, :])
    full = near + tn(hq[2 * R:, :], g4[2 * R:, :])
    gp[...] = full
    gpb[...] = full.astype(BF16)
    def piece_at(kz, ky):
        return pl.ds(pl.multiple_of(step(y, ky, 4) * 256 + step(z, kz, 8) * 32, 32), 32)

    for kz in (4, 3, 5, 2, 6, 1, 7, 0):
        for ky in (2, 1, 3):
            send(("gy", ky, kz), gpb.at[piece_at(kz, ky), :], ry.at[ky, kz], dev(dy=ky))
    older = len(sent)
    for kz in (4, 3, 5, 2, 6, 1, 7, 0):
        piece = gp[piece_at(kz, 0), :]
        for ky in (1, 3, 2):
            arrived(("gy", ky, kz), ry.at[ky, kz])
            piece = piece + ry[ky, kz].astype(F32)
        if kz:
            rzb[kz] = piece.astype(BF16)
            send(("gz", kz), rzb.at[kz], rz.at[kz], dev(dz=kz))
    for kz, kc in COLUMN:
        arrived(("loss", kz, kc), losses.at[step(z, -kz, 8) * 2 + step(c, kc, 2)])
    cost = losses[0]
    for n in range(1, 16):
        cost = cost + losses[n]
    loss_ref[...] = jnp.broadcast_to(jnp.sum(cost, axis=1, keepdims=True) * (1.0 / ROWS), (8, R))

    flush(0, older)
    for kz in (1, 7, 2, 6, 3, 5, 4):
        arrived(("gz", kz), rz.at[kz])
        piece = piece + rz[kz].astype(F32)

    def place(x_, c_, y_, z_=None):
        rows = slice(None) if z_ is None else pl.ds(pl.multiple_of(z_ * 32, 32), 32)
        return gproj_ref.at[c_, y_, rows, pl.ds(pl.multiple_of(x_ * R, R), R)]

    gproj_ref[c, y, pl.ds(pl.multiple_of(z * 32, 32), 32), quarter] = piece.astype(BF16)
    def both(c_, y_, z_=None):
        rows = slice(None) if z_ is None else pl.ds(pl.multiple_of(z_ * 32, 32), 32)
        return gproj_ref.at[c_, y_, rows, :]

    near_z, far_z = (0, 1, 7, 2, 6), (3, 5, 4)
    mine = place(xl, c, y, z)
    for kz in (4, 3, 5):
        send(("az", 1, kz), mine, mine, pair_dev(kz))
        send(("az", 0, kz), mine, mine, dev(dz=kz))
    for kz in (2, 6, 1, 7):
        send(("az", 0, kz), mine, mine, dev(dz=kz))
    for kz in near_z:
        there = place(xl, c, y, step(z, -kz, 8))
        if kz:
            arrived(("az", 0, kz), there)
        for ky in (2, 1, 3):
            send(("ay", ky, kz), there, there, dev(dy=ky))
        send(("ax", 0, kz), there, there, neighbour)
    for kz in far_z:
        z_from = step(z, -kz, 8)
        arrived(("az", 0, kz), place(xl, c, y, z_from))
        arrived(("az", 1, kz), place(1 - xl, c, y, z_from))
        there = both(c, y, z_from)
        for ky in (2, 1, 3):
            send(("ay", ky, kz), there, there, dev(dy=ky))
    for ky in (1, 3, 2):
        for kz in near_z:
            there = place(xl, c, step(y, -ky, 4), step(z, -kz, 8))
            arrived(("ay", ky, kz), there)
            send(("ax", ky, kz), there, there, neighbour)
    for ky in (0, 1, 3, 2):
        y_from = step(y, -ky, 4)
        if ky:
            for kz in far_z:
                arrived(("ay", ky, kz), both(c, y_from, step(z, -kz, 8)))
        for kz in near_z:
            arrived(("ax", ky, kz), place(1 - xl, c, y_from, step(z, -kz, 8)))
        send(("ac", ky), both(c, y_from), both(c, y_from), dev(dc=1))
    for ky in (0, 1, 3, 2):
        there = both(1 - c, step(y, -ky, 4))
        arrived(("ac", ky), there)
    arrived(("ge",), gemb_ref.at[:, pl.ds(pl.multiple_of((1 - xl) * R, R), R)])
    flush(0, len(sent))


def finish(loss_in, gemb_in, gproj_in, loss_out, gemb_out, gproj_out, wide, one_value, sems):
    one_value[...] = loss_in[0:1, 0:1]
    copies = [
        pltpu.make_async_copy(gemb_in, gemb_out, sems.at[8]),
        pltpu.make_async_copy(one_value, loss_out, sems.at[9]),
    ]
    for one in copies:
        one.start()
    for n in range(8):
        rows = slice(n * 256, (n + 1) * 256)
        wide[rows, :] = gproj_in[rows, :].astype(F32)
        copies.append(pltpu.make_async_copy(wide.at[rows, :], gproj_out.at[rows, :], sems.at[n]))
        copies[-1].start()
    for one in copies:
        one.wait()


def per_device(head_hidden, proj_weight, pair_perm):
    vmem = pltpu.VMEM
    hbm = pl.BlockSpec(memory_space=pltpu.HBM)
    space = pl.BlockSpec(memory_space=pltpu.VMEM)
    loss, grad_emb, grad_proj = pl.pallas_call(
        kernel,
        out_shape=(
            jax.ShapeDtypeStruct((8, R), F32),
            jax.ShapeDtypeStruct((R, 256), F32),
            jax.ShapeDtypeStruct((2, 4, 256, 256), BF16),
        ),
        in_specs=[hbm] * 3,
        out_specs=[space] * 3,
        scratch_shapes=[
            vmem((R, 2048), BF16),
            vmem((2048, 256), BF16),
            vmem((64, R), jnp.int32),
            vmem((4, 4, R, 256), BF16),
            vmem((2, 8, R, 256), BF16),
            vmem((2, 1024, 256), BF16),
            vmem((2, 1024, 256), BF16),
            vmem((1024, 1024), F32),
            vmem((1024, 1024), F32),
            vmem((16, 16, R), F32),
            vmem((16, 8, R), F32),
            vmem((16, 8, R), F32),
            vmem((1, 1024), F32),
            vmem((8, R), F32),
            vmem((1024, R), F32),
            vmem((8, R, R), F32),
            vmem((4, 4, R, R), BF16),
            vmem((4, 4, R, R), BF16),
            vmem((4, 4, R, R), BF16),
            vmem((4, 4, R, R), BF16),
            vmem((4, R, R), BF16),
            vmem((4, R, R), BF16),
            vmem((4, R, R), BF16),
            vmem((4, R, R), BF16),
            vmem((4, 8, R), F32),
            vmem((16, 8, R), F32),
            vmem((2, R, R), F32),
            vmem((512, R), BF16),
            vmem((512, 1024), BF16),
            vmem((1024, R), F32),
            vmem((1024, R), BF16),
            vmem((4, 8, 32, R), BF16),
            vmem((8, 32, R), BF16),
            vmem((8, 32, R), BF16),
            pltpu.SemaphoreType.DMA((9,)),
            pltpu.SemaphoreType.DMA((COPIES,)),
            pltpu.SemaphoreType.DMA((COPIES,)),
        ],
        compiler_params=pltpu.CompilerParams(
            collective_id=0, has_side_effects=True, vmem_limit_bytes=40 * 1024 * 1024
        ),
    )(*[pltpu.with_memory_space_constraint(v, pltpu.HBM) for v in (head_hidden, proj_weight, pair_perm.reshape(64, R))])
    hbm = pl.BlockSpec(memory_space=pl.ANY)
    loss, grad_emb, grad_proj = pl.pallas_call(
        finish,
        out_shape=(
            jax.ShapeDtypeStruct((1, 1), F32),
            jax.ShapeDtypeStruct((R, 256), F32),
            jax.ShapeDtypeStruct((2048, 256), F32),
        ),
        in_specs=[space] * 3,
        out_specs=[hbm, hbm, hbm],
        scratch_shapes=[vmem((2048, 256), F32), vmem((1, 1), F32), pltpu.SemaphoreType.DMA((10,))],
        compiler_params=pltpu.CompilerParams(vmem_limit_bytes=16 * 1024 * 1024),
    )(loss, grad_emb, grad_proj.reshape(2048, 256))
    return loss[0, 0], grad_emb, grad_proj


def solution(mesh):
    placed = (P("dp", None), P(None, "mp"), P())
    return jax.shard_map(
        per_device,
        mesh=mesh,
        in_specs=placed,
        out_specs=(P(), P("dp", "mp"), P(None, "mp")),
        check_vma=False,
    )
```

```python
import jax
import jax.numpy as jnp
from jax import lax
from jax.experimental import pallas as pl
from jax.experimental.pallas import tpu as pltpu
from jax.sharding import PartitionSpec as P

MESH = pl.DeviceIdType.MESH
F32 = jnp.float32
BF16 = jnp.bfloat16
SHARPNESS = 10.0
EXP2_SCALE = SHARPNESS * 1.4426950408889634
ORDER = (0, 1, 7, 2, 6, 3, 5, 4)
R = 128
H = 64
ROWS = 16384
COPIES = 320


def far(k, n):
    return min(k, n - k)


PLANE = sorted([(ky, kx) for ky in range(4) for kx in range(4)][1:], key=lambda k: -far(k[0], 4) - far(k[1], 4))
COLUMN = sorted([(kz, kc) for kz in range(8) for kc in range(2)][1:], key=lambda k: -far(k[0], 8))


def nt(a, b):
    return lax.dot_general(a, b, (((1,), (1,)), ((), ())), preferred_element_type=F32)


def to_rows(x):
    return jnp.sum(x.T, axis=0, keepdims=True)


def to_columns(row):
    return jnp.broadcast_to(row, (R, R)).T


def inverse_norm(e0, e1):
    return lax.rsqrt(jnp.sum(e0 * e0 + e1 * e1, axis=1, keepdims=True) + 1e-06)


def kernel(
    h_hbm, w_hbm, perm_hbm,
    loss_ref, gemb_ref, gproj_ref,
    h_ref, w_ref, perm_ref, ei, ej, ui, uj, sim, raw, mark, rowmsg, colmsg, losses, tsum, isum_cols, rowacc, factor,
    sa, sb, ra, rb, sa2, sb2, ra2, rb2, inner_out, inner_in,
    gout, g4, hq, gp, gpb, ry, rz, rzb, s_in, s_out, s_back,
):
    dp = lax.axis_index("dp")
    xh = lax.axis_index("mp")
    c = lax.rem(dp, 2)
    xl = lax.rem(dp // 2, 2)
    y = lax.rem(dp // 4, 4)
    z = dp // 16
    x = xh * 2 + xl
    p_me = y * 2 + xl
    fetches = c == xh

    def dev(dz=0, dy=0, dx=0, dc=0):
        x_ = step(x, dx, 4)
        return (((step(z, dz, 8) * 4 + step(y, dy, 4)) * 2 + lax.rem(x_, 2)) * 2 + step(c, dc, 2), x_ // 2)

    def step(v, k, n):
        k = k % n
        return v if k == 0 else lax.rem(v + k, n)

    def pair_dev(kz):
        return (((step(z, kz, 8) * 4 + y) * 2 + (1 - xl)) * 2 + c, xh)

    neighbour = pair_dev(0)

    slots = {}

    def copy(key, src, dst, to):
        n = slots.setdefault(key, len(slots))
        return pltpu.make_async_remote_copy(
            src_ref=src, dst_ref=dst, send_sem=s_out.at[n], recv_sem=s_back.at[n],
            device_id=to, device_id_type=MESH,
        )

    sent = []

    def send(key, src, dst, to):
        one = copy(key, src, dst, to)
        one.start()
        sent.append(one)

    def flush(start, stop):
        for one in sent[start:stop]:
            one.wait_send()
        del sent[start:stop]

    def arrived(key, dst):
        copy(key, dst, dst, dev(dc=1)).wait_recv()

    depth = 512
    parts = [slice(k * depth, (k + 1) * depth) for k in range(2048 // depth)]
    loads = []
    for n, part in enumerate(parts):
        loads.append(pltpu.make_async_copy(h_hbm.at[:, part], h_ref.at[:, part], s_in.at[2 * n]))
        loads.append(pltpu.make_async_copy(w_hbm.at[part, :], w_ref.at[part, :], s_in.at[2 * n + 1]))
    loads.append(pltpu.make_async_copy(perm_hbm, perm_ref, s_in.at[2 * len(parts)]))
    for load in loads:
        load.start()

    barrier = pltpu.get_barrier_semaphore()
    peers = [dev(dx=k) for k in (2, 1, 3)] + [dev(dy=k) for k in (2, 1, 3)] + [dev(dz=k) for k in (2, 6, 1, 7)] + [dev(dc=1)]
    for peer in peers:
        pl.semaphore_signal(barrier, inc=1, device_id=peer, device_id_type=MESH)

    total = None
    for n, part in enumerate(parts):
        loads[2 * n].wait()
        loads[2 * n + 1].wait()
        product = jnp.dot(h_ref[:, part], w_ref[part, :], preferred_element_type=F32)
        total = product if total is None else total + product
    ei[y, x] = total.astype(BF16)
    loads[-1].wait()

    @pl.when(fetches)
    def _():
        ej[xh, z] = ei[y, x]

    pl.semaphore_wait(barrier, len(peers))

    def half_rows(ref, *at):
        return [ref.at[(*at, slice(0, H))], ref.at[(*at, slice(H, R))]]

    own = half_rows(ei, y, x)
    for k, i in ((2, 0), (2, 1), (1, 0), (3, 0), (1, 1), (3, 1)):
        send(("x", k, i), own[i], own[i], dev(dx=k))
    for k, i in ((1, 1), (3, 1), (2, 1), (1, 0), (3, 0), (2, 0)):
        send(("y", k, i), own[i], own[i], dev(dy=k))

    def along_z(half, f, i):
        piece = half_rows(ej, f, z)[i]
        for k in (2, 6, 1, 7):
            copy(("z", half, k, i), piece, piece, dev(dz=k)).start()

    def hand(half, f, k):
        piece = ej.at[f, step(z, -k, 8)]
        copy(("c", half, k), piece, piece, dev(dc=1)).start()

    @pl.when(fetches)
    def _():
        along_z(0, xh, 0)
        along_z(0, xh, 1)
        hand(0, xh, 0)

    first = z < 4
    lanes = lax.broadcasted_iota(jnp.int32, (1, R), 1)
    b_row = []
    for k in ORDER:
        zz = step(z, -k, 8)
        jglob = (((zz * 4 + y) * 2 + xl) * 2 + xh) * R + lanes
        pair = perm_ref[pl.ds(lax.rem(zz, 4) * 16 + y * 4 + xl * 2 + xh, 1), :] + ROWS // 2
        b_row.append(jnp.where(first, jglob, jnp.where(zz < 4, pair, -1)).astype(F32))
    b_row = jnp.concatenate(b_row, axis=1)
    for p in range(8):
        mine = (z * 16 + p * 2 + c) * R + lanes
        pair = perm_ref[pl.ds(lax.rem(z, 4) * 16 + p * 2 + c, 1), :] + ROWS // 2
        a_col = to_columns(jnp.where(first, pair, mine).astype(F32))
        mark[p * R:(p + 1) * R, :] = jnp.where(jnp.concatenate([a_col] * 8, axis=1) == b_row, -2.0, 0.0)

    def on_from_x(k):
        part = half_rows(ei, y, step(x, -k, 4))[0]
        arrived(("x", k, 0), part)
        for ky in (2, 1, 3):
            send(("xy", k, ky), part, part, dev(dy=ky))

    def on_from_y(k):
        part = half_rows(ei, step(y, -k, 4), x)[1]
        arrived(("y", k, 1), part)
        for kx in (2, 1, 3):
            send(("yx", k, kx), part, part, dev(dx=kx))

    across = step(x, 2, 4)
    on_from_x(2)

    @pl.when(fetches)
    def _():
        ej[1 - xh, z, 0:H] = ei[y, across, 0:H]
        along_z(1, 1 - xh, 0)

    arrived(("x", 2, 1), half_rows(ei, y, across)[1])

    @pl.when(fetches)
    def _():
        ej[1 - xh, z, H:R] = ei[y, across, H:R]
        along_z(1, 1 - xh, 1)
        hand(1, 1 - xh, 0)

    on_from_x(1)
    on_from_x(3)
    on_from_y(1)
    on_from_y(3)
    on_from_y(2)

    def from_z(half, f, k, i):
        part = half_rows(ej, f, step(z, -k, 8))[i]
        arrived(("z", half, k, i), part)
        if k == 2:
            if i == 0:
                copy(("z", half, 4, 0), part, part, dev(dz=2)).start()
            copy(("z", half, 3, i), part, part, dev(dz=1)).start()
        if k == 6:
            if i == 1:
                copy(("z", half, 4, 1), part, part, dev(dz=-2)).start()
            copy(("z", half, 5, i), part, part, dev(dz=-1)).start()

    @pl.when(fetches)
    def _():
        for half, f in ((0, xh), (1, 1 - xh)):
            for k, i in ((2, 0), (6, 1), (2, 1), (6, 0)):
                from_z(half, f, k, i)
            hand(half, f, 2)
            hand(half, f, 6)
            for k in (1, 7):
                from_z(half, f, k, 0)
                from_z(half, f, k, 1)
                hand(half, f, k)

    def unit(dst, rows, e0, e1):
        e0 = e0.astype(F32)
        e1 = e1.astype(F32)
        inv = inverse_norm(e0, e1)
        dst[0, rows, :] = (e0 * inv).astype(BF16)
        dst[1, rows, :] = (e1 * inv).astype(BF16)

    def unit_columns(slots_):
        for slot in slots_:
            zz = step(z, -ORDER[slot], 8)
            unit(uj, slice(slot * R, (slot + 1) * R), ej[0, zz], ej[1, zz])

    def handed(slots_):
        for slot in slots_:
            for half, f in ((0, xh), (1, 1 - xh)):
                arrived(("c", half, ORDER[slot]), ej.at[f, step(z, -ORDER[slot], 8)])

    own_row = y * 4 + x
    own_col = z * 2 + c

    def scores(first_slot, last_slot, b, so_far):
        rows = slice(b * 256, (b + 1) * 256)
        cols = slice(first_slot * R, last_slot * R)
        s = nt(ui[0, rows, :], uj[0, cols, :]) + nt(ui[1, rows, :], uj[1, cols, :])
        raw[rows, cols] = s
        e = jnp.exp2(EXP2_SCALE * s - EXP2_SCALE)
        if first_slot == 0:
            at = lax.broadcasted_iota(jnp.int32, (256, R), 0) - lax.broadcasted_iota(jnp.int32, (256, R), 1)
            diagonal = at == jnp.where(fetches, p_me * R - b * 256, -ROWS)
            e = jnp.concatenate([jnp.where(diagonal, 0.0, e[:, 0:R]), e[:, R:]], axis=1)
        sim[rows, cols] = e
        part = e[:, 0:R]
        for t in range(1, last_slot - first_slot):
            part = part + e[:, t * R:(t + 1) * R]
        rowacc[rows, :] = part if first_slot == 0 else rowacc[rows, :] + part
        total = jnp.sum(e, axis=0, keepdims=True)
        return total if so_far is None else so_far + total

    def hand_in(first_slot, last_slot, so_far):
        for slot in range(first_slot, last_slot):
            t = slot - first_slot
            colmsg[own_col, pl.ds(step(z, -ORDER[slot], 8), 1), :] = so_far[:, t * R:(t + 1) * R]

    @pl.when(jnp.logical_not(fetches))
    def _():
        handed(range(5))

    for ky in (0, 1, 3, 2):
        y_from = step(y, -ky, 4)
        if ky == 0:
            for k in (1, 3):
                arrived(("x", k, 1), half_rows(ei, y, step(x, -k, 4))[1])
        else:
            arrived(("y", ky, 0), half_rows(ei, y_from, x)[0])
            for k in (1, 3, 2):
                arrived(("xy", k, ky), half_rows(ei, y_from, step(x, -k, 4))[0])
                arrived(("yx", ky, k), half_rows(ei, y_from, step(x, -k, 4))[1])
    for p in range(8):
        unit(ui, slice(p * R, (p + 1) * R), ei[p // 2, p % 2], ei[p // 2, 2 + p % 2])
    unit_columns(range(5))
    so_far = None
    for b in range(4):
        so_far = scores(0, 5, b, so_far)
    hand_in(0, 5, so_far)

    def hidden_rows(kc, x_):
        return pl.ds(pl.multiple_of((kc * 2 + x_) * R, R), R)

    def half_of(core):
        return pl.ds(pl.multiple_of(core * 1024, 1024), 1024)

    def send_hidden(kc):
        for n, dx in ((0, 1), (1, 3)):
            cols = pl.ds(pl.multiple_of(step(c, kc, 2) * 1024 + n * 512, 512), 512)
            there = hq.at[hidden_rows(kc, xl), n * 512:(n + 1) * 512]
            send(("hx", n, kc), h_ref.at[:, cols], there, dev(dx=dx, dc=kc))

    hq[hidden_rows(0, xl), :] = h_ref[:, half_of(c)]
    send(("h",), h_ref.at[:, half_of(1 - c)], hq.at[hidden_rows(1, xl), :], dev(dc=1))
    send_hidden(0)

    @pl.when(fetches)
    def _():
        for half, f in ((0, xh), (1, 1 - xh)):
            for k in (3, 5, 4):
                from_z(half, f, k, 0)
                from_z(half, f, k, 1)
                hand(half, f, k)

    @pl.when(jnp.logical_not(fetches))
    def _():
        handed(range(5, 8))

    unit_columns(range(5, 8))
    so_far = None
    for b in range(4):
        so_far = scores(5, 8, b, so_far)
    hand_in(5, 8, so_far)
    for p in range(8):
        rowmsg[own_row, p:p + 1, :] = to_rows(rowacc[p * R:(p + 1) * R, :])

    for kz, kc in COLUMN:
        send(("col", kz, kc), colmsg.at[own_col], colmsg.at[own_col], dev(dz=kz, dc=kc))
    for ky, kx in PLANE:
        send(("row", ky, kx), rowmsg.at[own_row], rowmsg.at[own_row], dev(dy=ky, dx=kx))
    send_hidden(1)
    hits = jnp.zeros((1, R), F32)
    for p in range(8):
        rows = slice(p * R, (p + 1) * R)
        hit = jnp.sum(raw[rows, :] * mark[rows, :], axis=0, keepdims=True)
        for t in range(8):
            hits = hits - 0.5 * hit[:, t * R:(t + 1) * R]
    for ky, kx in PLANE:
        arrived(("row", ky, kx), rowmsg.at[step(y, -ky, 4) * 4 + step(x, -kx, 4)])
    for kz, kc in COLUMN:
        arrived(("col", kz, kc), colmsg.at[step(z, -kz, 8) * 2 + step(c, kc, 2)])

    all_rows = rowmsg[0]
    all_cols = colmsg[0]
    for n in range(1, 16):
        all_rows = all_rows + rowmsg[n]
        all_cols = all_cols + colmsg[n]
    row_total = all_rows
    log_sums = jnp.sum(jnp.log(row_total), axis=0, keepdims=True)

    inv_rows = 1.0 / row_total
    inv_cols = 1.0 / all_cols
    isum_cols[...] = inv_cols
    tsum[...] = jnp.concatenate([isum_cols[pl.ds(step(z, -k, 8), 1), :] for k in ORDER], axis=1)
    for p in range(8):
        factor[p] = to_columns(inv_rows[p:p + 1])
    def send_b(ky, kx):
        y_to, x_to = step(y, ky, 4), step(x, kx, 4)
        send(("rb", ky, kx), sb.at[y_to, x_to], rb.at[ky, x_to], dev(dy=ky))

    older = len(sent)

    for ky in (2, 1, 3, 0):
        y_to = step(y, ky, 4)
        rows = pl.ds(pl.multiple_of(y_to * 256, 256), 256)
        wide = jnp.concatenate([factor[pl.ds(y_to * 2, 2)].reshape(256, R)] * 8, axis=1)
        weights = (sim[rows, :] * (wide + tsum[...]) + mark[rows, :]).astype(BF16)
        acc = None
        for f in range(2):
            g = jnp.dot(weights, uj[f], preferred_element_type=F32)
            for q in range(2):
                sa[2 * f + q, y_to] = g[0:R, q * R:(q + 1) * R].astype(BF16)
                sb[y_to, 2 * f + q] = g[R:2 * R, q * R:(q + 1) * R].astype(BF16)
            t = g * ui[f, rows, :].astype(F32)
            t = t[:, 0:R] + t[:, R:]
            acc = t if acc is None else acc + t
        for kx in (2, 1, 3):
            send(("ra", kx, ky), sa.at[step(x, kx, 4), y_to], ra.at[kx, y_to], dev(dx=kx))
        if ky:
            send_b(ky, 2)
        for half in range(2):
            v = to_rows(acc[half * R:(half + 1) * R])
            inner_out[y_to, half:half + 1, :] = v
        inner_out[y_to, 2:3, :] = hits
        if ky == 0:
            inner_in[own_row] = inner_out[y]
        for kx in (2, 1, 3, 0):
            if ky or kx:
                send(
                    ("in", ky, kx), inner_out.at[y_to], inner_in.at[own_row],
                    dev(dy=ky, dx=kx),
                )
    for kx in (1, 3, 0):
        for ky in (2, 1, 3):
            send_b(ky, kx)
    flush(0, older)

    @pl.when(fetches)
    def _():
        whole = ej.at[0, 0]
        part = ej.at[0, 0, 0:H]
        for half in range(2):
            for k in range(1, 8):
                for i in range(2):
                    copy(("z", half, k, i), part, part, dev(dc=1)).wait_send()
            for k in range(8):
                copy(("c", half, k), whole, whole, dev(dc=1)).wait_send()
    def total_a(ky):
        y_to = step(y, ky, 4)
        g = sa[x, y_to].astype(F32)
        for kx in (1, 2, 3):
            arrived(("ra", kx, ky), ra.at[kx, y_to])
            g = g + ra[kx, y_to].astype(F32)
        return g

    def total_b(kx):
        x_to = step(x, kx, 4)
        g = sb[y, x_to].astype(F32)
        for ky in (1, 2, 3):
            arrived(("rb", ky, kx), rb.at[ky, x_to])
            g = g + rb[ky, x_to].astype(F32)
        return g

    for k in (2, 1, 3):
        sa2[k] = total_a(k).astype(BF16)
        send(("ra2", k), sa2.at[k], ra2.at[k], dev(dy=k))
        sb2[k] = total_b(k).astype(BF16)
        send(("rb2", k), sb2.at[k], rb2.at[k], dev(dx=k))
    g_a = total_a(0)
    g_b = total_b(0)
    for ky, kx in PLANE:
        arrived(("in", ky, kx), inner_in.at[step(y, -ky, 4) * 4 + step(x, -kx, 4)])
    inner = inner_in[0]
    for n in range(1, 16):
        inner = inner + inner_in[n]
    for k in (2, 1, 3):
        arrived(("ra2", k), ra2.at[k])
        arrived(("rb2", k), rb2.at[k])
        g_a = g_a + ra2[k].astype(F32)
        g_b = g_b + rb2[k].astype(F32)
    quarter = pl.ds(pl.multiple_of(xl * R, R), R)
    for half, g in ((0, g_a), (1, g_b)):
        inv = inverse_norm(ei[y, half].astype(F32), ei[y, 2 + half].astype(F32))
        some_unit = ei[y, 2 * xh + half, :, quarter].astype(F32) * inv
        grad = (SHARPNESS * inv) * (g - some_unit * to_columns(inner[half:half + 1]))
        g4[half * R:(half + 1) * R, :] = grad.astype(BF16)
        gout[half] = grad

    def tn(a, b):
        return lax.dot_general(a, b, (((0,), (0,)), ((), ())), preferred_element_type=F32)

    send(("g",), g4.at[0:2 * R, :], g4.at[2 * R:4 * R, :], dev(dc=1))
    send(("ge",), gout.at[1 - xl], gemb_ref.at[:, quarter], neighbour)
    gemb_ref[:, quarter] = gout[xl]
    arrived(("h",), hq.at[hidden_rows(1, xl), :])
    for kc in range(2):
        for n in range(2):
            arrived(("hx", n, kc), hq.at[hidden_rows(kc, 1 - xl), n * 512:(n + 1) * 512])
    near = tn(hq[0:2 * R, :], g4[0:2 * R, :])
    arrived(("g",), g4.at[2 * R:4 * R, :])
    cost = log_sums - SHARPNESS * (inner[2:3] - 8.0)
    losses[own_col] = jnp.broadcast_to(cost, (8, R))
    full = near + tn(hq[2 * R:, :], g4[2 * R:, :])
    gp[...] = full
    gpb[...] = full.astype(BF16)
    def piece_at(kz, ky):
        return pl.ds(pl.multiple_of(step(y, ky, 4) * 256 + step(z, kz, 8) * 32, 32), 32)

    for kz in (4, 3, 5, 2, 6, 1, 7, 0):
        for ky in (2, 1, 3):
            send(("gy", ky, kz), gpb.at[piece_at(kz, ky), :], ry.at[ky, kz], dev(dy=ky))
    older = len(sent)
    for kz, kc in COLUMN:
        send(("loss", kz, kc), losses.at[own_col], losses.at[own_col], dev(dz=kz, dc=kc))
    for kz in (4, 3, 5, 2, 6, 1, 7, 0):
        piece = gp[piece_at(kz, 0), :]
        for ky in (1, 3, 2):
            arrived(("gy", ky, kz), ry.at[ky, kz])
            piece = piece + ry[ky, kz].astype(F32)
        if kz:
            rzb[kz] = piece.astype(BF16)
            send(("gz", kz), rzb.at[kz], rz.at[kz], dev(dz=kz))
    flush(0, older)
    for kz in (1, 7, 2, 6, 3, 5, 4):
        arrived(("gz", kz), rz.at[kz])
        piece = piece + rz[kz].astype(F32)

    def place(x_, c_, y_, z_=None):
        rows = slice(None) if z_ is None else pl.ds(pl.multiple_of(z_ * 32, 32), 32)
        return gproj_ref.at[c_, y_, rows, pl.ds(pl.multiple_of(x_ * R, R), R)]

    gproj_ref[c, y, pl.ds(pl.multiple_of(z * 32, 32), 32), quarter] = piece.astype(BF16)
    def both(c_, y_, z_=None):
        rows = slice(None) if z_ is None else pl.ds(pl.multiple_of(z_ * 32, 32), 32)
        return gproj_ref.at[c_, y_, rows, :]

    near_z, far_z = (0, 1, 7, 2, 6), (3, 5, 4)
    mine = place(xl, c, y, z)
    for kz in (4, 3, 5):
        send(("az", 1, kz), mine, mine, pair_dev(kz))
        send(("az", 0, kz), mine, mine, dev(dz=kz))
    for kz in (2, 6, 1, 7):
        send(("az", 0, kz), mine, mine, dev(dz=kz))
    for kz in near_z:
        there = place(xl, c, y, step(z, -kz, 8))
        if kz:
            arrived(("az", 0, kz), there)
        for ky in (2, 1, 3):
            send(("ay", ky, kz), there, there, dev(dy=ky))
        send(("ax", 0, kz), there, there, neighbour)
    for kz in far_z:
        z_from = step(z, -kz, 8)
        arrived(("az", 0, kz), place(xl, c, y, z_from))
        arrived(("az", 1, kz), place(1 - xl, c, y, z_from))
        there = both(c, y, z_from)
        for ky in (2, 1, 3):
            send(("ay", ky, kz), there, there, dev(dy=ky))
    for ky in (1, 3, 2):
        for kz in near_z:
            there = place(xl, c, step(y, -ky, 4), step(z, -kz, 8))
            arrived(("ay", ky, kz), there)
            send(("ax", ky, kz), there, there, neighbour)
    for ky in (0, 1, 3, 2):
        y_from = step(y, -ky, 4)
        if ky:
            for kz in far_z:
                arrived(("ay", ky, kz), both(c, y_from, step(z, -kz, 8)))
        for kz in near_z:
            arrived(("ax", ky, kz), place(1 - xl, c, y_from, step(z, -kz, 8)))
        send(("ac", ky), both(c, y_from), both(c, y_from), dev(dc=1))
    for kz, kc in COLUMN:
        arrived(("loss", kz, kc), losses.at[step(z, -kz, 8) * 2 + step(c, kc, 2)])
    cost = losses[0]
    for n in range(1, 16):
        cost = cost + losses[n]
    loss_ref[...] = jnp.broadcast_to(jnp.sum(cost, axis=1, keepdims=True) * (1.0 / ROWS), (8, R))

    for ky in (0, 1, 3, 2):
        there = both(1 - c, step(y, -ky, 4))
        arrived(("ac", ky), there)
    arrived(("ge",), gemb_ref.at[:, pl.ds(pl.multiple_of((1 - xl) * R, R), R)])
    flush(0, len(sent))


def finish(loss_in, gemb_in, gproj_in, loss_out, gemb_out, gproj_out, wide, one_value, sems):
    one_value[...] = loss_in[0:1, 0:1]
    copies = [
        pltpu.make_async_copy(gemb_in, gemb_out, sems.at[8]),
        pltpu.make_async_copy(one_value, loss_out, sems.at[9]),
    ]
    for one in copies:
        one.start()
    for n in range(8):
        rows = slice(n * 256, (n + 1) * 256)
        wide[rows, :] = gproj_in[rows, :].astype(F32)
        copies.append(pltpu.make_async_copy(wide.at[rows, :], gproj_out.at[rows, :], sems.at[n]))
        copies[-1].start()
    for one in copies:
        one.wait()


def per_device(head_hidden, proj_weight, pair_perm):
    vmem = pltpu.VMEM
    hbm = pl.BlockSpec(memory_space=pltpu.HBM)
    space = pl.BlockSpec(memory_space=pltpu.VMEM)
    loss, grad_emb, grad_proj = pl.pallas_call(
        kernel,
        out_shape=(
            jax.ShapeDtypeStruct((8, R), F32),
            jax.ShapeDtypeStruct((R, 256), F32),
            jax.ShapeDtypeStruct((2, 4, 256, 256), BF16),
        ),
        in_specs=[hbm] * 3,
        out_specs=[space] * 3,
        scratch_shapes=[
            vmem((R, 2048), BF16),
            vmem((2048, 256), BF16),
            vmem((64, R), jnp.int32),
            vmem((4, 4, R, 256), BF16),
            vmem((2, 8, R, 256), BF16),
            vmem((2, 1024, 256), BF16),
            vmem((2, 1024, 256), BF16),
            vmem((1024, 1024), F32),
            vmem((1024, 1024), F32),
            vmem((1024, 1024), F32),
            vmem((16, 8, R), F32),
            vmem((16, 8, R), F32),
            vmem((16, 8, R), F32),
            vmem((1, 1024), F32),
            vmem((8, R), F32),
            vmem((1024, R), F32),
            vmem((8, R, R), F32),
            vmem((4, 4, R, R), BF16),
            vmem((4, 4, R, R), BF16),
            vmem((4, 4, R, R), BF16),
            vmem((4, 4, R, R), BF16),
            vmem((4, R, R), BF16),
            vmem((4, R, R), BF16),
            vmem((4, R, R), BF16),
            vmem((4, R, R), BF16),
            vmem((4, 8, R), F32),
            vmem((16, 8, R), F32),
            vmem((2, R, R), F32),
            vmem((512, R), BF16),
            vmem((512, 1024), BF16),
            vmem((1024, R), F32),
            vmem((1024, R), BF16),
            vmem((4, 8, 32, R), BF16),
            vmem((8, 32, R), BF16),
            vmem((8, 32, R), BF16),
            pltpu.SemaphoreType.DMA((9,)),
            pltpu.SemaphoreType.DMA((COPIES,)),
            pltpu.SemaphoreType.DMA((COPIES,)),
        ],
        compiler_params=pltpu.CompilerParams(
            collective_id=0, has_side_effects=True, vmem_limit_bytes=40 * 1024 * 1024
        ),
    )(*[pltpu.with_memory_space_constraint(v, pltpu.HBM) for v in (head_hidden, proj_weight, pair_perm.reshape(64, R))])
    hbm = pl.BlockSpec(memory_space=pl.ANY)
    loss, grad_emb, grad_proj = pl.pallas_call(
        finish,
        out_shape=(
            jax.ShapeDtypeStruct((1, 1), F32),
            jax.ShapeDtypeStruct((R, 256), F32),
            jax.ShapeDtypeStruct((2048, 256), F32),
        ),
        in_specs=[space] * 3,
        out_specs=[hbm, hbm, hbm],
        scratch_shapes=[vmem((2048, 256), F32), vmem((1, 1), F32), pltpu.SemaphoreType.DMA((10,))],
        compiler_params=pltpu.CompilerParams(vmem_limit_bytes=16 * 1024 * 1024),
    )(loss, grad_emb, grad_proj.reshape(2048, 256))
    return loss[0, 0], grad_emb, grad_proj


def solution(mesh):
    placed = (P("dp", None), P(None, "mp"), P())
    return jax.shard_map(
        per_device,
        mesh=mesh,
        in_specs=placed,
        out_specs=(P(), P("dp", "mp"), P(None, "mp")),
        check_vma=False,
    )
```

```python
import jax
import jax.numpy as jnp
from jax import lax
from jax.experimental import pallas as pl
from jax.experimental.pallas import tpu as pltpu
from jax.sharding import PartitionSpec as P

MESH = pl.DeviceIdType.MESH
F32 = jnp.float32
BF16 = jnp.bfloat16
SHARPNESS = 10.0
EXP2_SCALE = SHARPNESS * 1.4426950408889634
ORDER = (0, 1, 7, 2, 6, 3, 5, 4)
R = 128
H = 64
ROWS = 16384
COPIES = 320


def far(k, n):
    return min(k, n - k)


PLANE = sorted([(ky, kx) for ky in range(4) for kx in range(4)][1:], key=lambda k: -far(k[0], 4) - far(k[1], 4))
COLUMN = sorted([(kz, kc) for kz in range(8) for kc in range(2)][1:], key=lambda k: -far(k[0], 8))


def nt(a, b):
    return lax.dot_general(a, b, (((1,), (1,)), ((), ())), preferred_element_type=F32)


def to_rows(x):
    return jnp.sum(x.T, axis=0, keepdims=True)


def to_columns(row):
    return jnp.broadcast_to(row, (R, R)).T


def inverse_norm(e0, e1):
    return lax.rsqrt(jnp.sum(e0 * e0 + e1 * e1, axis=1, keepdims=True) + 1e-06)


def kernel(
    h_hbm, w_hbm, perm_hbm,
    loss_ref, gemb_ref, gproj_ref,
    h_ref, w_ref, perm_ref, ei, ej, ui, uj, sim, raw, mark, rowmsg, colmsg, losses, tsum, isum_cols, rowacc, factor,
    sa, sb, ra, rb, sa2, sb2, ra2, rb2, inner_out, inner_in,
    gout, g4, hq, gp, gpb, ry, rz, rzb, s_in, s_out, s_back,
):
    dp = lax.axis_index("dp")
    xh = lax.axis_index("mp")
    c = lax.rem(dp, 2)
    xl = lax.rem(dp // 2, 2)
    y = lax.rem(dp // 4, 4)
    z = dp // 16
    x = xh * 2 + xl
    p_me = y * 2 + xl
    fetches = c == xh

    def dev(dz=0, dy=0, dx=0, dc=0):
        x_ = step(x, dx, 4)
        return (((step(z, dz, 8) * 4 + step(y, dy, 4)) * 2 + lax.rem(x_, 2)) * 2 + step(c, dc, 2), x_ // 2)

    def step(v, k, n):
        k = k % n
        return v if k == 0 else lax.rem(v + k, n)

    def pair_dev(kz):
        return (((step(z, kz, 8) * 4 + y) * 2 + (1 - xl)) * 2 + c, xh)

    neighbour = pair_dev(0)

    slots = {}

    def copy(key, src, dst, to):
        n = slots.setdefault(key, len(slots))
        return pltpu.make_async_remote_copy(
            src_ref=src, dst_ref=dst, send_sem=s_out.at[n], recv_sem=s_back.at[n],
            device_id=to, device_id_type=MESH,
        )

    sent = []

    def send(key, src, dst, to):
        one = copy(key, src, dst, to)
        one.start()
        sent.append(one)

    def flush(start, stop):
        for one in sent[start:stop]:
            one.wait_send()
        del sent[start:stop]

    def arrived(key, dst):
        copy(key, dst, dst, dev(dc=1)).wait_recv()

    barrier = pltpu.get_barrier_semaphore()
    peers = [dev(dx=k) for k in (2, 1, 3)] + [dev(dy=k) for k in (2, 1, 3)] + [dev(dz=k) for k in (2, 6, 1, 7)] + [dev(dc=1)]
    for peer in peers:
        pl.semaphore_signal(barrier, inc=1, device_id=peer, device_id_type=MESH)

    depth = 512
    parts = [slice(k * depth, (k + 1) * depth) for k in range(2048 // depth)]
    loads = []
    for n, part in enumerate(parts):
        loads.append(pltpu.make_async_copy(h_hbm.at[:, part], h_ref.at[:, part], s_in.at[2 * n]))
        loads.append(pltpu.make_async_copy(w_hbm.at[part, :], w_ref.at[part, :], s_in.at[2 * n + 1]))
    loads.append(pltpu.make_async_copy(perm_hbm, perm_ref, s_in.at[2 * len(parts)]))
    for load in loads:
        load.start()

    total = None
    for n, part in enumerate(parts):
        loads[2 * n].wait()
        loads[2 * n + 1].wait()
        product = jnp.dot(h_ref[:, part], w_ref[part, :], preferred_element_type=F32)
        total = product if total is None else total + product
    ei[y, x] = total.astype(BF16)
    loads[-1].wait()

    @pl.when(fetches)
    def _():
        ej[xh, z] = ei[y, x]

    pl.semaphore_wait(barrier, len(peers))

    def half_rows(ref, *at):
        return [ref.at[(*at, slice(0, H))], ref.at[(*at, slice(H, R))]]

    own = half_rows(ei, y, x)
    for k, i in ((2, 0), (2, 1), (1, 0), (3, 0), (1, 1), (3, 1)):
        send(("x", k, i), own[i], own[i], dev(dx=k))
    for k, i in ((1, 1), (3, 1), (2, 1), (1, 0), (3, 0), (2, 0)):
        send(("y", k, i), own[i], own[i], dev(dy=k))

    def along_z(half, f, i):
        piece = half_rows(ej, f, z)[i]
        for k in (2, 6, 1, 7):
            copy(("z", half, k, i), piece, piece, dev(dz=k)).start()

    def hand(half, f, k):
        piece = ej.at[f, step(z, -k, 8)]
        copy(("c", half, k), piece, piece, dev(dc=1)).start()

    @pl.when(fetches)
    def _():
        along_z(0, xh, 0)
        along_z(0, xh, 1)
        hand(0, xh, 0)

    first = z < 4
    lanes = lax.broadcasted_iota(jnp.int32, (1, R), 1)
    b_row = []
    for k in ORDER:
        zz = step(z, -k, 8)
        jglob = (((zz * 4 + y) * 2 + xl) * 2 + xh) * R + lanes
        pair = perm_ref[pl.ds(lax.rem(zz, 4) * 16 + y * 4 + xl * 2 + xh, 1), :] + ROWS // 2
        b_row.append(jnp.where(first, jglob, jnp.where(zz < 4, pair, -1)).astype(F32))
    b_row = jnp.concatenate(b_row, axis=1)
    for p in range(8):
        mine = (z * 16 + p * 2 + c) * R + lanes
        pair = perm_ref[pl.ds(lax.rem(z, 4) * 16 + p * 2 + c, 1), :] + ROWS // 2
        a_col = to_columns(jnp.where(first, pair, mine).astype(F32))
        mark[p * R:(p + 1) * R, :] = jnp.where(jnp.concatenate([a_col] * 8, axis=1) == b_row, -2.0, 0.0)

    def on_from_x(k):
        part = half_rows(ei, y, step(x, -k, 4))[0]
        arrived(("x", k, 0), part)
        for ky in (2, 1, 3):
            send(("xy", k, ky), part, part, dev(dy=ky))

    def on_from_y(k):
        part = half_rows(ei, step(y, -k, 4), x)[1]
        arrived(("y", k, 1), part)
        for kx in (2, 1, 3):
            send(("yx", k, kx), part, part, dev(dx=kx))

    across = step(x, 2, 4)
    on_from_x(2)

    @pl.when(fetches)
    def _():
        ej[1 - xh, z, 0:H] = ei[y, across, 0:H]
        along_z(1, 1 - xh, 0)

    arrived(("x", 2, 1), half_rows(ei, y, across)[1])

    @pl.when(fetches)
    def _():
        ej[1 - xh, z, H:R] = ei[y, across, H:R]
        along_z(1, 1 - xh, 1)
        hand(1, 1 - xh, 0)

    on_from_x(1)
    on_from_x(3)
    on_from_y(1)
    on_from_y(3)
    on_from_y(2)

    def from_z(half, f, k, i):
        part = half_rows(ej, f, step(z, -k, 8))[i]
        arrived(("z", half, k, i), part)
        if k == 2:
            if i == 0:
                copy(("z", half, 4, 0), part, part, dev(dz=2)).start()
            copy(("z", half, 3, i), part, part, dev(dz=1)).start()
        if k == 6:
            if i == 1:
                copy(("z", half, 4, 1), part, part, dev(dz=-2)).start()
            copy(("z", half, 5, i), part, part, dev(dz=-1)).start()

    @pl.when(fetches)
    def _():
        for half, f in ((0, xh), (1, 1 - xh)):
            for k, i in ((2, 0), (6, 1), (2, 1), (6, 0)):
                from_z(half, f, k, i)
            hand(half, f, 2)
            hand(half, f, 6)
            for k in (1, 7):
                from_z(half, f, k, 0)
                from_z(half, f, k, 1)
                hand(half, f, k)

    def unit(dst, rows, e0, e1):
        e0 = e0.astype(F32)
        e1 = e1.astype(F32)
        inv = inverse_norm(e0, e1)
        dst[0, rows, :] = (e0 * inv).astype(BF16)
        dst[1, rows, :] = (e1 * inv).astype(BF16)

    def unit_columns(slots_):
        for slot in slots_:
            zz = step(z, -ORDER[slot], 8)
            unit(uj, slice(slot * R, (slot + 1) * R), ej[0, zz], ej[1, zz])

    def handed(slots_):
        for slot in slots_:
            for half, f in ((0, xh), (1, 1 - xh)):
                arrived(("c", half, ORDER[slot]), ej.at[f, step(z, -ORDER[slot], 8)])

    own_row = y * 4 + x
    own_col = z * 2 + c

    def scores(first_slot, last_slot, b, so_far):
        rows = slice(b * 256, (b + 1) * 256)
        cols = slice(first_slot * R, last_slot * R)
        s = nt(ui[0, rows, :], uj[0, cols, :]) + nt(ui[1, rows, :], uj[1, cols, :])
        raw[rows, cols] = s
        e = jnp.exp2(EXP2_SCALE * s - EXP2_SCALE)
        if first_slot == 0:
            at = lax.broadcasted_iota(jnp.int32, (256, R), 0) - lax.broadcasted_iota(jnp.int32, (256, R), 1)
            diagonal = at == jnp.where(fetches, p_me * R - b * 256, -ROWS)
            e = jnp.concatenate([jnp.where(diagonal, 0.0, e[:, 0:R]), e[:, R:]], axis=1)
        sim[rows, cols] = e
        part = e[:, 0:R]
        for t in range(1, last_slot - first_slot):
            part = part + e[:, t * R:(t + 1) * R]
        rowacc[rows, :] = part if first_slot == 0 else rowacc[rows, :] + part
        total = jnp.sum(e, axis=0, keepdims=True)
        return total if so_far is None else so_far + total

    def hand_in(first_slot, last_slot, so_far):
        for slot in range(first_slot, last_slot):
            t = slot - first_slot
            colmsg[own_col, pl.ds(step(z, -ORDER[slot], 8), 1), :] = so_far[:, t * R:(t + 1) * R]

    @pl.when(jnp.logical_not(fetches))
    def _():
        handed(range(5))

    for ky in (0, 1, 3, 2):
        y_from = step(y, -ky, 4)
        if ky == 0:
            for k in (1, 3):
                arrived(("x", k, 1), half_rows(ei, y, step(x, -k, 4))[1])
        else:
            arrived(("y", ky, 0), half_rows(ei, y_from, x)[0])
            for k in (1, 3, 2):
                arrived(("xy", k, ky), half_rows(ei, y_from, step(x, -k, 4))[0])
                arrived(("yx", ky, k), half_rows(ei, y_from, step(x, -k, 4))[1])
    for p in range(8):
        unit(ui, slice(p * R, (p + 1) * R), ei[p // 2, p % 2], ei[p // 2, 2 + p % 2])
    unit_columns(range(5))
    so_far = None
    for b in range(4):
        so_far = scores(0, 5, b, so_far)
    hand_in(0, 5, so_far)

    def hidden_rows(kc, x_):
        return pl.ds(pl.multiple_of((kc * 2 + x_) * R, R), R)

    def half_of(core):
        return pl.ds(pl.multiple_of(core * 1024, 1024), 1024)

    def send_hidden(kc):
        for n, dx in ((0, 1), (1, 3)):
            cols = pl.ds(pl.multiple_of(step(c, kc, 2) * 1024 + n * 512, 512), 512)
            there = hq.at[hidden_rows(kc, xl), n * 512:(n + 1) * 512]
            send(("hx", n, kc), h_ref.at[:, cols], there, dev(dx=dx, dc=kc))

    hq[hidden_rows(0, xl), :] = h_ref[:, half_of(c)]
    send(("h",), h_ref.at[:, half_of(1 - c)], hq.at[hidden_rows(1, xl), :], dev(dc=1))
    send_hidden(0)

    @pl.when(fetches)
    def _():
        for half, f in ((0, xh), (1, 1 - xh)):
            for k in (3, 5, 4):
                from_z(half, f, k, 0)
                from_z(half, f, k, 1)
                hand(half, f, k)

    @pl.when(jnp.logical_not(fetches))
    def _():
        handed(range(5, 8))

    unit_columns(range(5, 8))
    so_far = None
    for b in range(4):
        so_far = scores(5, 8, b, so_far)
    hand_in(5, 8, so_far)
    for p in range(8):
        rowmsg[own_row, p:p + 1, :] = to_rows(rowacc[p * R:(p + 1) * R, :])

    for kz, kc in COLUMN:
        send(("col", kz, kc), colmsg.at[own_col], colmsg.at[own_col], dev(dz=kz, dc=kc))
    for ky, kx in PLANE:
        send(("row", ky, kx), rowmsg.at[own_row], rowmsg.at[own_row], dev(dy=ky, dx=kx))
    send_hidden(1)
    hits = jnp.zeros((1, R), F32)
    for p in range(8):
        rows = slice(p * R, (p + 1) * R)
        hit = jnp.sum(raw[rows, :] * mark[rows, :], axis=0, keepdims=True)
        for t in range(8):
            hits = hits - 0.5 * hit[:, t * R:(t + 1) * R]
    for ky, kx in PLANE:
        arrived(("row", ky, kx), rowmsg.at[step(y, -ky, 4) * 4 + step(x, -kx, 4)])
    for kz, kc in COLUMN:
        arrived(("col", kz, kc), colmsg.at[step(z, -kz, 8) * 2 + step(c, kc, 2)])

    all_rows = rowmsg[0]
    all_cols = colmsg[0]
    for n in range(1, 16):
        all_rows = all_rows + rowmsg[n]
        all_cols = all_cols + colmsg[n]
    row_total = all_rows
    log_sums = jnp.sum(jnp.log(row_total), axis=0, keepdims=True)

    inv_rows = 1.0 / row_total
    inv_cols = 1.0 / all_cols
    isum_cols[...] = inv_cols
    tsum[...] = jnp.concatenate([isum_cols[pl.ds(step(z, -k, 8), 1), :] for k in ORDER], axis=1)
    for p in range(8):
        factor[p] = to_columns(inv_rows[p:p + 1])
    def send_b(ky, kx):
        y_to, x_to = step(y, ky, 4), step(x, kx, 4)
        send(("rb", ky, kx), sb.at[y_to, x_to], rb.at[ky, x_to], dev(dy=ky))

    older = len(sent)

    for ky in (2, 1, 3, 0):
        y_to = step(y, ky, 4)
        rows = pl.ds(pl.multiple_of(y_to * 256, 256), 256)
        wide = jnp.concatenate([factor[pl.ds(y_to * 2, 2)].reshape(256, R)] * 8, axis=1)
        weights = (sim[rows, :] * (wide + tsum[...]) + mark[rows, :]).astype(BF16)
        acc = None
        for f in range(2):
            g = jnp.dot(weights, uj[f], preferred_element_type=F32)
            for q in range(2):
                sa[2 * f + q, y_to] = g[0:R, q * R:(q + 1) * R].astype(BF16)
                sb[y_to, 2 * f + q] = g[R:2 * R, q * R:(q + 1) * R].astype(BF16)
            t = g * ui[f, rows, :].astype(F32)
            t = t[:, 0:R] + t[:, R:]
            acc = t if acc is None else acc + t
        for kx in (2, 1, 3):
            send(("ra", kx, ky), sa.at[step(x, kx, 4), y_to], ra.at[kx, y_to], dev(dx=kx))
        if ky:
            send_b(ky, 2)
        for half in range(2):
            v = to_rows(acc[half * R:(half + 1) * R])
            inner_out[y_to, half:half + 1, :] = v
        inner_out[y_to, 2:3, :] = hits
        if ky == 0:
            inner_in[own_row] = inner_out[y]
        for kx in (2, 1, 3, 0):
            if ky or kx:
                send(
                    ("in", ky, kx), inner_out.at[y_to], inner_in.at[own_row],
                    dev(dy=ky, dx=kx),
                )
    for kx in (1, 3, 0):
        for ky in (2, 1, 3):
            send_b(ky, kx)
    flush(0, older)

    @pl.when(fetches)
    def _():
        whole = ej.at[0, 0]
        part = ej.at[0, 0, 0:H]
        for half in range(2):
            for k in range(1, 8):
                for i in range(2):
                    copy(("z", half, k, i), part, part, dev(dc=1)).wait_send()
            for k in range(8):
                copy(("c", half, k), whole, whole, dev(dc=1)).wait_send()
    def total_a(ky):
        y_to = step(y, ky, 4)
        g = sa[x, y_to].astype(F32)
        for kx in (1, 2, 3):
            arrived(("ra", kx, ky), ra.at[kx, y_to])
            g = g + ra[kx, y_to].astype(F32)
        return g

    def total_b(kx):
        x_to = step(x, kx, 4)
        g = sb[y, x_to].astype(F32)
        for ky in (1, 2, 3):
            arrived(("rb", ky, kx), rb.at[ky, x_to])
            g = g + rb[ky, x_to].astype(F32)
        return g

    for k in (2, 1, 3):
        sa2[k] = total_a(k).astype(BF16)
        send(("ra2", k), sa2.at[k], ra2.at[k], dev(dy=k))
        sb2[k] = total_b(k).astype(BF16)
        send(("rb2", k), sb2.at[k], rb2.at[k], dev(dx=k))
    g_a = total_a(0)
    g_b = total_b(0)
    for ky, kx in PLANE:
        arrived(("in", ky, kx), inner_in.at[step(y, -ky, 4) * 4 + step(x, -kx, 4)])
    inner = inner_in[0]
    for n in range(1, 16):
        inner = inner + inner_in[n]
    for k in (2, 1, 3):
        arrived(("ra2", k), ra2.at[k])
        arrived(("rb2", k), rb2.at[k])
        g_a = g_a + ra2[k].astype(F32)
        g_b = g_b + rb2[k].astype(F32)
    quarter = pl.ds(pl.multiple_of(xl * R, R), R)
    for half, g in ((0, g_a), (1, g_b)):
        inv = inverse_norm(ei[y, half].astype(F32), ei[y, 2 + half].astype(F32))
        some_unit = ei[y, 2 * xh + half, :, quarter].astype(F32) * inv
        grad = (SHARPNESS * inv) * (g - some_unit * to_columns(inner[half:half + 1]))
        g4[half * R:(half + 1) * R, :] = grad.astype(BF16)
        gout[half] = grad

    def tn(a, b):
        return lax.dot_general(a, b, (((0,), (0,)), ((), ())), preferred_element_type=F32)

    send(("g",), g4.at[0:2 * R, :], g4.at[2 * R:4 * R, :], dev(dc=1))
    send(("ge",), gout.at[1 - xl], gemb_ref.at[:, quarter], neighbour)
    gemb_ref[:, quarter] = gout[xl]
    arrived(("h",), hq.at[hidden_rows(1, xl), :])
    for kc in range(2):
        for n in range(2):
            arrived(("hx", n, kc), hq.at[hidden_rows(kc, 1 - xl), n * 512:(n + 1) * 512])
    near = tn(hq[0:2 * R, :], g4[0:2 * R, :])
    arrived(("g",), g4.at[2 * R:4 * R, :])
    cost = log_sums - SHARPNESS * (inner[2:3] - 8.0)
    losses[own_col] = jnp.broadcast_to(cost, (8, R))
    full = near + tn(hq[2 * R:, :], g4[2 * R:, :])
    gp[...] = full
    gpb[...] = full.astype(BF16)
    def piece_at(kz, ky):
        return pl.ds(pl.multiple_of(step(y, ky, 4) * 256 + step(z, kz, 8) * 32, 32), 32)

    for kz in (4, 3, 5, 2, 6, 1, 7, 0):
        for ky in (2, 1, 3):
            send(("gy", ky, kz), gpb.at[piece_at(kz, ky), :], ry.at[ky, kz], dev(dy=ky))
    older = len(sent)
    for kz, kc in COLUMN:
        send(("loss", kz, kc), losses.at[own_col], losses.at[own_col], dev(dz=kz, dc=kc))
    for kz in (4, 3, 5, 2, 6, 1, 7, 0):
        piece = gp[piece_at(kz, 0), :]
        for ky in (1, 3, 2):
            arrived(("gy", ky, kz), ry.at[ky, kz])
            piece = piece + ry[ky, kz].astype(F32)
        if kz:
            rzb[kz] = piece.astype(BF16)
            send(("gz", kz), rzb.at[kz], rz.at[kz], dev(dz=kz))
    flush(0, older)
    for kz in (1, 7, 2, 6, 3, 5, 4):
        arrived(("gz", kz), rz.at[kz])
        piece = piece + rz[kz].astype(F32)

    def place(x_, c_, y_, z_=None):
        rows = slice(None) if z_ is None else pl.ds(pl.multiple_of(z_ * 32, 32), 32)
        return gproj_ref.at[c_, y_, rows, pl.ds(pl.multiple_of(x_ * R, R), R)]

    gproj_ref[c, y, pl.ds(pl.multiple_of(z * 32, 32), 32), quarter] = piece.astype(BF16)
    def both(c_, y_, z_=None):
        rows = slice(None) if z_ is None else pl.ds(pl.multiple_of(z_ * 32, 32), 32)
        return gproj_ref.at[c_, y_, rows, :]

    near_z, far_z = (0, 1, 7, 2, 6), (3, 5, 4)
    mine = place(xl, c, y, z)
    for kz in (4, 3, 5):
        send(("az", 1, kz), mine, mine, pair_dev(kz))
        send(("az", 0, kz), mine, mine, dev(dz=kz))
    for kz in (2, 6, 1, 7):
        send(("az", 0, kz), mine, mine, dev(dz=kz))
    for kz in near_z:
        there = place(xl, c, y, step(z, -kz, 8))
        if kz:
            arrived(("az", 0, kz), there)
        for ky in (2, 1, 3):
            send(("ay", ky, kz), there, there, dev(dy=ky))
        send(("ax", 0, kz), there, there, neighbour)
    for kz in far_z:
        z_from = step(z, -kz, 8)
        arrived(("az", 0, kz), place(xl, c, y, z_from))
        arrived(("az", 1, kz), place(1 - xl, c, y, z_from))
        there = both(c, y, z_from)
        for ky in (2, 1, 3):
            send(("ay", ky, kz), there, there, dev(dy=ky))
    for ky in (1, 3, 2):
        for kz in near_z:
            there = place(xl, c, step(y, -ky, 4), step(z, -kz, 8))
            arrived(("ay", ky, kz), there)
            send(("ax", ky, kz), there, there, neighbour)
    for ky in (0, 1, 3, 2):
        y_from = step(y, -ky, 4)
        if ky:
            for kz in far_z:
                arrived(("ay", ky, kz), both(c, y_from, step(z, -kz, 8)))
        for kz in near_z:
            arrived(("ax", ky, kz), place(1 - xl, c, y_from, step(z, -kz, 8)))
        send(("ac", ky), both(c, y_from), both(c, y_from), dev(dc=1))
    for kz, kc in COLUMN:
        arrived(("loss", kz, kc), losses.at[step(z, -kz, 8) * 2 + step(c, kc, 2)])
    cost = losses[0]
    for n in range(1, 16):
        cost = cost + losses[n]
    loss_ref[...] = jnp.broadcast_to(jnp.sum(cost, axis=1, keepdims=True) * (1.0 / ROWS), (8, R))

    for ky in (0, 1, 3, 2):
        there = both(1 - c, step(y, -ky, 4))
        arrived(("ac", ky), there)
    arrived(("ge",), gemb_ref.at[:, pl.ds(pl.multiple_of((1 - xl) * R, R), R)])
    flush(0, len(sent))


def finish(loss_in, gemb_in, gproj_in, loss_out, gemb_out, gproj_out, wide, one_value, sems):
    one_value[...] = loss_in[0:1, 0:1]
    copies = [
        pltpu.make_async_copy(gemb_in, gemb_out, sems.at[8]),
        pltpu.make_async_copy(one_value, loss_out, sems.at[9]),
    ]
    for one in copies:
        one.start()
    for n in range(8):
        rows = slice(n * 256, (n + 1) * 256)
        wide[rows, :] = gproj_in[rows, :].astype(F32)
        copies.append(pltpu.make_async_copy(wide.at[rows, :], gproj_out.at[rows, :], sems.at[n]))
        copies[-1].start()
    for one in copies:
        one.wait()


def per_device(head_hidden, proj_weight, pair_perm):
    vmem = pltpu.VMEM
    hbm = pl.BlockSpec(memory_space=pltpu.HBM)
    space = pl.BlockSpec(memory_space=pltpu.VMEM)
    loss, grad_emb, grad_proj = pl.pallas_call(
        kernel,
        out_shape=(
            jax.ShapeDtypeStruct((8, R), F32),
            jax.ShapeDtypeStruct((R, 256), F32),
            jax.ShapeDtypeStruct((2, 4, 256, 256), BF16),
        ),
        in_specs=[hbm] * 3,
        out_specs=[space] * 3,
        scratch_shapes=[
            vmem((R, 2048), BF16),
            vmem((2048, 256), BF16),
            vmem((64, R), jnp.int32),
            vmem((4, 4, R, 256), BF16),
            vmem((2, 8, R, 256), BF16),
            vmem((2, 1024, 256), BF16),
            vmem((2, 1024, 256), BF16),
            vmem((1024, 1024), F32),
            vmem((1024, 1024), F32),
            vmem((1024, 1024), F32),
            vmem((16, 8, R), F32),
            vmem((16, 8, R), F32),
            vmem((16, 8, R), F32),
            vmem((1, 1024), F32),
            vmem((8, R), F32),
            vmem((1024, R), F32),
            vmem((8, R, R), F32),
            vmem((4, 4, R, R), BF16),
            vmem((4, 4, R, R), BF16),
            vmem((4, 4, R, R), BF16),
            vmem((4, 4, R, R), BF16),
            vmem((4, R, R), BF16),
            vmem((4, R, R), BF16),
            vmem((4, R, R), BF16),
            vmem((4, R, R), BF16),
            vmem((4, 8, R), F32),
            vmem((16, 8, R), F32),
            vmem((2, R, R), F32),
            vmem((512, R), BF16),
            vmem((512, 1024), BF16),
            vmem((1024, R), F32),
            vmem((1024, R), BF16),
            vmem((4, 8, 32, R), BF16),
            vmem((8, 32, R), BF16),
            vmem((8, 32, R), BF16),
            pltpu.SemaphoreType.DMA((9,)),
            pltpu.SemaphoreType.DMA((COPIES,)),
            pltpu.SemaphoreType.DMA((COPIES,)),
        ],
        compiler_params=pltpu.CompilerParams(
            collective_id=0, has_side_effects=True, vmem_limit_bytes=40 * 1024 * 1024
        ),
    )(*[pltpu.with_memory_space_constraint(v, pltpu.HBM) for v in (head_hidden, proj_weight, pair_perm.reshape(64, R))])
    hbm = pl.BlockSpec(memory_space=pl.ANY)
    loss, grad_emb, grad_proj = pl.pallas_call(
        finish,
        out_shape=(
            jax.ShapeDtypeStruct((1, 1), F32),
            jax.ShapeDtypeStruct((R, 256), F32),
            jax.ShapeDtypeStruct((2048, 256), F32),
        ),
        in_specs=[space] * 3,
        out_specs=[hbm, hbm, hbm],
        scratch_shapes=[vmem((2048, 256), F32), vmem((1, 1), F32), pltpu.SemaphoreType.DMA((10,))],
        compiler_params=pltpu.CompilerParams(vmem_limit_bytes=16 * 1024 * 1024),
    )(loss, grad_emb, grad_proj.reshape(2048, 256))
    return loss[0, 0], grad_emb, grad_proj


def solution(mesh):
    placed = (P("dp", None), P(None, "mp"), P())
    return jax.shard_map(
        per_device,
        mesh=mesh,
        in_specs=placed,
        out_specs=(P(), P("dp", "mp"), P(None, "mp")),
        check_vma=False,
    )
```
